32 devices in a mesh: groups: 2 (over y), elem: 4 (over z), energy: 2 (over x), rhs: 2 (over core).
Axes of the slice: x: 2, y: 2, z: 4, core: 2. Of those that a mesh axis runs over, the one named last changes fastest.
Arguments:
- ham_noise: float32 [8, 256, 256], P(('groups', 'elem')), parts along dimension 0, may hold values from -0.01171875 to 0.01171875
- channel_levels: float32 [8, 256], P(('groups', 'elem')), parts along dimension 0, may hold values from 0.2 to 1.2
- coupling_noise: float32 [8, 256, 256], P(('groups', 'elem')), parts along dimension 0, may hold values from -0.01171875 to 0.01171875
- corr_weight: float32 [8], P(('groups', 'elem')), parts along dimension 0, may hold values from 0.25 to 1
- corr_basis: float32 [512, 256], P('groups'), parts along dimension 0, may hold values from -0.1875 to 0.1875
- projector: float32 [8, 256, 256], P(('groups', 'elem')), parts along dimension 0, may hold values from -0.1875 to 0.1875
- energy_shift: float32 [4], P(('groups', 'energy')), parts along dimension 0, may hold values from 0.1 to 0.4
- sources: float32 [4, 4, 256, 256], P(('groups', 'energy'), 'elem', None, 'rhs'), parts along dimension 0, may hold values from -6 to 6
- target: float32 [4, 256, 256], P(('groups', 'energy'), None, 'rhs'), parts along dimension 0, may hold values from -6 to 6
- open_channels: int32 [4], P(('groups', 'energy')), parts along dimension 0, may hold values from 64 to 256
Outputs:
- wave_functions: float32 [4, 4, 256, 256], P(('groups', 'energy'), 'elem', None, 'rhs'), parts along dimension 0
- adjoints: float32 [4, 4, 256, 256], P(('groups', 'energy'), 'elem', None, 'rhs'), parts along dimension 0
- k_matrices: float32 [4, 256, 256], P(('groups', 'energy'), 'elem', 'rhs'), parts along dimension 0
- basis_grad: float32 [512, 256], P('groups'), parts along dimension 0
The draws below stay inside these ranges and needn't reach their ends.
There are 2 independent parts, one for each index of `groups`. The reference program is written for one: setup_inputs(seed, part) draws one part's arguments, and reference() takes and returns one part's arrays. A program takes and returns all parts, laid end to end along the dimension named above; each array names one. Nothing has to cross between parts.
All inputs are finite; a program needn't handle non-finite values.
Results may differ from the reference program's by a relative error of at most 0.0003.
Values sent between devices are 32-bit elements; how exact they have to be, the bound alone decides.
No kernel may reach another device: no remote copies, remote signals or barrier semaphores. Data moves between devices by JAX's collectives and lax.ppermute only.
A program may use at most 64 MiB of HBM per device.

```python
import math
import jax
import jax.numpy as jnp
from jax import lax

B = 256
R = 256
M = 256
NE = 4
ENERGIES = 2


def level_of(rng, extent, pieces, smallest, high):
    factor_of, own = 1.0, jax.random.fold_in(rng, 6)
    for dim, parts in pieces:
        steps = jnp.exp(jax.random.uniform(jax.random.fold_in(own, dim), (parts,), jnp.float32, smallest / len(pieces), high / len(pieces)))
        factor_of = factor_of * jnp.repeat(steps, extent[dim] // parts).reshape([-1 if axis == dim else 1 for axis in range(len(extent))])
    return factor_of


def gaussian(stream_key, shape, deviation, most, pieces=(), kind=jnp.bfloat16):
    level = level_of(stream_key, shape, pieces, -0.22, 0.18) if pieces else 1.0
    values = jax.random.normal(stream_key, shape, jnp.float32) * deviation * level
    return jnp.minimum(jnp.maximum(values, -most), most).astype(kind)


def setup_inputs(seed: int = 0, part: int = 0) -> dict:
    key_of = jax.random.split(jax.random.key(seed), 11)
    part_keys = jax.random.split(jax.random.fold_in(key_of[10], part), 11)
    ham_noise = gaussian(part_keys[0], (NE, B, B), (900 * B) ** -0.5, 0.01171875, ((0, 4),), jnp.float32)
    channel_levels = jnp.clip(0.2 + 1 * jax.random.uniform(part_keys[1], (NE, B), jnp.float32) ** level_of(part_keys[1], (NE, B), ((0, 4),), -0.2, 0.2), 0.2, 1.2)
    coupling_noise = gaussian(part_keys[2], (NE, B, B), (900 * B) ** -0.5, 0.01171875, ((0, 4),), jnp.float32)
    corr_weight = jnp.clip(jnp.exp(math.log(1.0) - 1.3862944 * jax.random.uniform(part_keys[3], (NE,), jnp.float32) ** level_of(part_keys[3], (NE,), ((0, 4),), -0.2, 0.2)), 0.25, 1.0)
    corr_basis = gaussian(part_keys[4], (B, M), (4 * M) ** -0.5, 0.1875, (), jnp.float32)
    projector = gaussian(part_keys[5], (NE, B, R), (B * NE) ** -0.5, 0.1875, ((0, 4),), jnp.float32)
    energy_shift = jnp.clip(0.1 + 0.3 * jax.random.uniform(part_keys[6], (ENERGIES,), jnp.float32) ** level_of(part_keys[6], (ENERGIES,), ((0, 2),), -0.2, 0.2), 0.1, 0.4)
    sources = gaussian(part_keys[7], (ENERGIES, NE, B, R), 1.0, 6.0, ((0, 2), (1, 4), (3, 2)), jnp.float32)
    target = gaussian(part_keys[8], (ENERGIES, R, R), 1.0, 6.0, ((0, 2), (2, 2)), jnp.float32)
    open_channels = jax.random.randint(part_keys[9], (ENERGIES,), R // 4, R + 1).astype(jnp.int32)
    return {"ham_noise": ham_noise, "channel_levels": channel_levels, "coupling_noise": coupling_noise, "corr_weight": corr_weight, "corr_basis": corr_basis, "projector": projector, "energy_shift": energy_shift, "sources": sources, "target": target, "open_channels": open_channels}


FULL_PRECISION = lax.Precision.HIGHEST
PENALTY = 0.5

def chol_apply(factor, values):
    halfway = lax.linalg.triangular_solve(factor, values, left_side=True, lower=True)
    return lax.linalg.triangular_solve(factor, halfway, left_side=True, lower=True, transpose_a=True)

def dense_dot(lhs_block, rhs_block):
    return jnp.dot(lhs_block.astype(jnp.float32), rhs_block.astype(jnp.float32), precision=FULL_PRECISION, preferred_element_type=jnp.float32)

def factorize(diagonal, lower_block):
    identity = jnp.eye(diagonal.shape[1], dtype=jnp.float32)

    def advance(factor_prev, scan_item):
        diag_block, coupling = scan_item
        coupled = chol_apply(factor_prev, coupling.T)
        reduced = diag_block - dense_dot(coupling, coupled)
        factor = jnp.linalg.cholesky(reduced)
        return (factor, factor)
    unused_carry, factors = lax.scan(advance, identity, (diagonal, lower_block))
    return factors

def block_solve(factors, lower_block, source):
    identity = jnp.eye(factors.shape[1], dtype=jnp.float32)

    def forward(carry, scan_item):
        factor_prev, reduced_prev = carry
        factor, coupling, column_block = scan_item
        reduced = column_block - dense_dot(coupling, chol_apply(factor_prev, reduced_prev))
        return ((factor, reduced), reduced)
    start_state = (identity, jnp.zeros_like(source[0]))
    unused_carry, reduced = lax.scan(forward, start_state, (factors, lower_block, source))
    last_value = chol_apply(factors[-1], reduced[-1])

    def backward(next_value, scan_item):
        factor, reduced_here, coupling_next = scan_item
        result = chol_apply(factor, reduced_here - dense_dot(coupling_next.T, next_value))
        return (result, result)
    unused_last, earlier = lax.scan(backward, last_value, (factors[:-1], reduced[:-1], lower_block[1:]), reverse=True)
    return jnp.concatenate([earlier, last_value[None]], axis=0)

def reference(ham_noise, channel_levels, coupling_noise, corr_weight, corr_basis, projector, energy_shift, sources, target, open_channels):
    identity = jnp.eye(ham_noise.shape[1], dtype=jnp.float32)
    potential = dense_dot(corr_basis, corr_basis.T)
    common = 0.5 * (ham_noise + jnp.swapaxes(ham_noise, 1, 2)) + (2.0 + channel_levels)[:, :, None] * identity + corr_weight[:, None, None] * potential
    not_first = (jnp.arange(NE) > 0).astype(jnp.float32)
    lower_block = -(identity + coupling_noise) * not_first[:, None, None]

    def per_energy(scan_item):
        shift_value, source_set, goal_block, open_count = scan_item
        diagonal = common + shift_value * identity
        factors = factorize(diagonal, lower_block)
        wave_set = block_solve(factors, lower_block, source_set)
        k_matrix = jnp.einsum('nbr,nbs->rs', projector, wave_set, precision=FULL_PRECISION)
        row_open = jnp.arange(R) < open_count
        open_mask = (row_open[:, None] & row_open[None, :]).astype(jnp.float32)
        residual = open_mask * (k_matrix - goal_block)
        drive = PENALTY * wave_set + jnp.einsum('nbr,rs->nbs', projector, residual, precision=FULL_PRECISION)
        adjoint_set = block_solve(factors, lower_block, drive)
        side_wave = jnp.einsum('nbs,bm->nsm', wave_set, corr_basis, precision=FULL_PRECISION)
        side_adjoint = jnp.einsum('nbs,bm->nsm', adjoint_set, corr_basis, precision=FULL_PRECISION)
        weighted_adjoint = corr_weight[:, None, None] * adjoint_set
        weighted_wave = corr_weight[:, None, None] * wave_set
        grad_term = jnp.einsum('nbs,nsm->bm', weighted_adjoint, side_wave, precision=FULL_PRECISION) + jnp.einsum('nbs,nsm->bm', weighted_wave, side_adjoint, precision=FULL_PRECISION)
        return (wave_set, adjoint_set, k_matrix, grad_term)
    wave_functions, adjoints, k_matrices, grad_terms = lax.map(per_energy, (energy_shift, sources, target, open_channels))
    basis_grad = -jnp.sum(grad_terms, axis=0) / (ENERGIES * NE)
    return (wave_functions, adjoints, k_matrices, basis_grad)
```

```python
import functools

import jax
import jax.numpy as jnp
from jax import lax
from jax.experimental import pallas as pl
from jax.experimental.pallas import tpu as pltpu
from jax.sharding import PartitionSpec as P

PENALTY = 0.5
STEPS = 3
START_SCALE = 1.75
RESIDUAL_BOUND = 0.01
F32 = jnp.float32
BF16 = jnp.bfloat16
NN = (((1,), (0,)), ((), ()))
NT = (((1,), (1,)), ((), ()))
VMEM_BYTES = 48 * 1024 * 1024


def split(value):
    high = value.astype(BF16)
    return high, (value - high.astype(F32)).astype(BF16)


def dot1(lhs, rhs, dims=NN):
    return lax.dot_general(lhs, rhs, dims, preferred_element_type=F32)


def dot3(lhs, rhs, dims=NN):
    return (
        dot1(lhs[0], rhs[0], dims) + dot1(lhs[0], rhs[1], dims) + dot1(lhs[1], rhs[0], dims)
    )


def eye_of(size):
    rows = lax.broadcasted_iota(jnp.int32, (size, size), 0)
    columns = lax.broadcasted_iota(jnp.int32, (size, size), 1)
    return (rows == columns).astype(F32)


def row_norm(matrix):
    return jnp.max(jnp.sum(jnp.abs(matrix), axis=1, keepdims=True), axis=0, keepdims=True)


def fast_inverse(matrix, identity):
    scale = START_SCALE / row_norm(matrix)
    error = identity - scale * matrix
    inverse = scale * (identity + error)
    error16 = error.astype(BF16)
    for _ in range(STEPS):
        error16 = dot1(error16, error16).astype(BF16)
        inverse = inverse + dot1(inverse.astype(BF16), error16)
    parts = split(inverse)
    residual = identity - dot3(split(matrix), parts)
    inverse = inverse + dot1(parts[0], residual.astype(BF16))
    return inverse, row_norm(residual)


def exact_dot(lhs, rhs):
    return lax.dot_general(
        lhs, rhs, NN, precision=lax.Precision.HIGHEST, preferred_element_type=F32
    )


def slow_inverse(matrix, identity, matrix_scr, inverse_scr):
    matrix_scr[...] = matrix
    inverse_scr[...] = identity * (START_SCALE / row_norm(matrix))

    def going(state):
        count, size = state
        return (size > 1e-3) & (count < 100)

    def step(state):
        count, _ = state
        inverse = inverse_scr[...]
        residual = identity - exact_dot(matrix_scr[...], inverse)
        inverse_scr[...] = inverse + exact_dot(inverse, residual)
        return count + 1, jnp.max(row_norm(residual))

    lax.while_loop(going, step, (jnp.int32(0), jnp.float32(1e9)))
    return inverse_scr[...], jnp.zeros((1, 1), F32)


def factor_kernel(
    shift_ref, weight_ref, level_ref, ham_ref, coupling_ref, basis_ref, inverse_ref, link_ref,
    diag_scr, matrix_scr, inverse_scr,
):
    count = ham_ref.shape[0]
    size = ham_ref.shape[1]
    middle = count // 2
    identity = eye_of(size)
    basis = split(basis_ref[...])
    potential = dot3(basis, basis, NT)
    for n in range(count):
        ham = ham_ref[n]
        diag_scr[n] = (
            0.5 * (ham + ham.T)
            + (2.0 + level_ref[n : n + 1, :] + shift_ref[0]) * identity
            + weight_ref[n] * potential
        )

    def eliminate(invert):
        worst = jnp.zeros((1, 1), F32)
        forward = diag_scr[0]
        backward = diag_scr[count - 1]

        def finish(n, matrix, worst):
            inverse, size_left = invert(matrix, identity)
            parts = split(inverse)
            inverse_ref[0, n] = parts[0]
            inverse_ref[1, n] = parts[1]
            return parts, jnp.maximum(worst, size_left)

        def keep(n, link):
            parts = split(link)
            link_ref[0, n] = parts[0]
            link_ref[1, n] = parts[1]
            return parts

        meeting = diag_scr[middle]
        for step in range(max(middle, count - 1 - middle)):
            ahead, behind = step, count - 1 - step
            if ahead < middle:
                parts, worst = finish(ahead, forward, worst)
                coupling = split(-(identity + coupling_ref[ahead + 1]))
                link = keep(ahead + 1, dot3(coupling, parts))
                update = dot3(link, coupling, NT)
                if ahead + 1 < middle:
                    forward = diag_scr[ahead + 1] - update
                else:
                    meeting = meeting - update
            if behind > middle:
                parts, worst = finish(behind, backward, worst)
                raw = -(identity + coupling_ref[behind])
                link = keep(behind, dot3(split(raw.T), parts))
                update = dot3(link, split(raw))
                if behind - 1 > middle:
                    backward = diag_scr[behind - 1] - update
                else:
                    meeting = meeting - update
        _, worst = finish(middle, meeting, worst)
        return worst

    worst = jnp.max(eliminate(fast_inverse))

    @pl.when(jnp.logical_not(worst <= RESIDUAL_BOUND))
    def _():
        eliminate(
            functools.partial(slow_inverse, matrix_scr=matrix_scr, inverse_scr=inverse_scr)
        )


def factorize(shift, weights, levels, ham, coupling, basis):
    count, size = ham.shape[0], ham.shape[1]
    smem = pl.BlockSpec(memory_space=pltpu.SMEM)
    vmem = pl.BlockSpec(memory_space=pltpu.VMEM)
    half = jax.ShapeDtypeStruct((2, count, size, size), BF16)
    return pl.pallas_call(
        factor_kernel,
        out_shape=(half, half),
        in_specs=[smem, smem, vmem, vmem, vmem, vmem],
        out_specs=(vmem, vmem),
        scratch_shapes=[
            pltpu.VMEM((count, size, size), F32),
            pltpu.VMEM((size, size), F32),
            pltpu.VMEM((size, size), F32),
        ],
        compiler_params=pltpu.CompilerParams(vmem_limit_bytes=VMEM_BYTES),
        name="factorize",
    )(shift, weights, levels, ham, coupling, basis)


def solve_kernel(
    place_ref, open_ref, weight_ref, inverse_ref, link_ref, source_ref, projector_ref,
    target_ref, wave_ref, adjoint_ref, share_ref, gram_ref, own_scr, k_scr,
):
    count = source_ref.shape[0]
    channels, width = source_ref.shape[1:]
    middle = count // 2
    me, column = place_ref[0], place_ref[1]
    inverses = [(inverse_ref[0, n], inverse_ref[1, n]) for n in range(count)]
    links = [(link_ref[0, n], link_ref[1, n]) if n != 0 else None for n in range(count)]
    projectors = [split(projector_ref[n]) for n in range(count)]

    def solve(blocks):
        reduced = list(blocks)
        for n in range(1, middle + 1):
            reduced[n] = reduced[n] - dot3(split(reduced[n - 1]), links[n], NT)
        for n in range(count - 1, middle, -1):
            reduced[n - 1] = reduced[n - 1] - dot3(split(reduced[n]), links[n], NT)
        solved = [dot3(split(reduced[n]), inverses[n]) for n in range(count)]
        halves = [None] * count
        halves[middle] = split(solved[middle])
        for n in range(middle, 0, -1):
            solved[n - 1] = solved[n - 1] - dot3(halves[n], links[n])
            halves[n - 1] = split(solved[n - 1])
        for n in range(middle + 1, count):
            solved[n] = solved[n] - dot3(halves[n - 1], links[n])
            halves[n] = split(solved[n])
        return solved, halves

    wave, wave_halves = solve([source_ref[n].T for n in range(count)])
    k_total = dot3(wave_halves[0], projectors[0])
    for n in range(1, count):
        k_total = k_total + dot3(wave_halves[n], projectors[n])
    k_rows = lax.broadcasted_iota(jnp.int32, k_total.shape, 1)
    k_columns = lax.broadcasted_iota(jnp.int32, k_total.shape, 0) + column * width
    opened = (k_rows < open_ref[0]) & (k_columns < open_ref[0])
    residual = split(jnp.where(opened, k_total - target_ref[...].T, 0.0))
    drive = [PENALTY * wave[n] + dot3(residual, projectors[n], NT) for n in range(count)]
    adjoint, _ = solve(drive)

    share = share_ref.shape[0]
    k_scr[...] = k_total.T
    share_ref[...] = k_scr[pl.ds(pl.multiple_of(me * share, share), share), :]
    wave = [value.T for value in wave]
    adjoint = [value.T for value in adjoint]
    for n in range(count):
        own_scr[n] = wave[n]
    wave_ref[...] = own_scr[me]
    for n in range(count):
        own_scr[n] = adjoint[n]
    adjoint_ref[...] = own_scr[me]
    weighted = jnp.concatenate([weight_ref[n] * wave[n] for n in range(count)], axis=1)
    gram = dot3(split(jnp.concatenate(adjoint, axis=1)), split(weighted), NT)
    gram_ref[...] = gram + gram.T


def solve_all(place, opened, weights, inverses, links, sources, projectors, target):
    count, channels, width = sources.shape
    rows = target.shape[0]
    smem = pl.BlockSpec(memory_space=pltpu.SMEM)
    vmem = pl.BlockSpec(memory_space=pltpu.VMEM)
    return pl.pallas_call(
        solve_kernel,
        out_shape=(
            jax.ShapeDtypeStruct((channels, width), F32),
            jax.ShapeDtypeStruct((channels, width), F32),
            jax.ShapeDtypeStruct((rows // count, width), F32),
            jax.ShapeDtypeStruct((channels, channels), F32),
        ),
        in_specs=[smem, smem, smem, vmem, vmem, vmem, vmem, vmem],
        out_specs=(vmem,) * 4,
        scratch_shapes=[
            pltpu.VMEM((count, channels, width), F32),
            pltpu.VMEM((rows, width), F32),
        ],
        compiler_params=pltpu.CompilerParams(vmem_limit_bytes=VMEM_BYTES),
        name="solve",
    )(place, opened, weights, inverses, links, sources, projectors, target)


def total_over(value, axis):
    count = lax.axis_size(axis)
    if count & (count - 1):
        return lax.psum(value, axis)
    step = 1
    while step < count:
        value = value + lax.ppermute(value, axis, [(i, i ^ step) for i in range(count)])
        step = step * 2
    return value


def per_device(
    ham_noise,
    channel_levels,
    coupling_noise,
    corr_weight,
    corr_basis,
    projector,
    energy_shift,
    sources,
    target,
    open_channels,
):
    elements = lax.axis_size("elem")
    size = ham_noise.shape[1]
    extra = jnp.concatenate(
        [channel_levels, jnp.broadcast_to(corr_weight[:, None], (7, size))], axis=0
    )
    matrices = jnp.concatenate([ham_noise[0], coupling_noise[0], extra], axis=0)
    matrices = lax.all_gather(matrices, "elem")
    source_all = lax.all_gather(sources[0, 0], "elem")
    projector_all = lax.all_gather(projector[0], "elem")
    ham = matrices[:, :size]
    coupling = matrices[:, size : 2 * size]
    levels = matrices[:, 2 * size]
    weights = matrices[:, 2 * size + 1, 0]
    inverses, links = factorize(energy_shift, weights, levels, ham, coupling, corr_basis)
    place = jnp.stack([lax.axis_index("elem"), lax.axis_index("rhs")]).astype(jnp.int32)
    wave, adjoint, share, gram = solve_all(
        place, open_channels, weights, inverses, links, source_all, projector_all, target[0]
    )
    gram = total_over(total_over(gram, "rhs"), "energy")
    grad = jnp.dot(gram, corr_basis, precision=lax.Precision.HIGHEST)
    basis_grad = grad * (-1.0 / (lax.axis_size("energy") * elements))
    return wave[None, None], adjoint[None, None], share[None], basis_grad


def solution(mesh):
    return jax.shard_map(
        per_device,
        mesh=mesh,
        in_specs=(
            P(("groups", "elem"), None, None),
            P(("groups", "elem"), None),
            P(("groups", "elem"), None, None),
            P(("groups", "elem")),
            P("groups", None),
            P(("groups", "elem"), None, None),
            P(("groups", "energy")),
            P(("groups", "energy"), "elem", None, "rhs"),
            P(("groups", "energy"), None, "rhs"),
            P(("groups", "energy")),
        ),
        out_specs=(
            P(("groups", "energy"), "elem", None, "rhs"),
            P(("groups", "energy"), "elem", None, "rhs"),
            P(("groups", "energy"), "elem", "rhs"),
            P("groups", None),
        ),
        check_vma=False,
    )
```

```python
import functools

import jax
import jax.numpy as jnp
from jax import lax
from jax.experimental import pallas as pl
from jax.experimental.pallas import tpu as pltpu
from jax.sharding import PartitionSpec as P

PENALTY = 0.5
STEPS = 3
START_SCALE = 1.75
RESIDUAL_BOUND = 0.01
F32 = jnp.float32
BF16 = jnp.bfloat16
NN = (((1,), (0,)), ((), ()))
NT = (((1,), (1,)), ((), ()))
VMEM_BYTES = 48 * 1024 * 1024


def split(value):
    high = value.astype(BF16)
    return high, (value - high.astype(F32)).astype(BF16)


def dot1(lhs, rhs, dims=NN):
    return lax.dot_general(lhs, rhs, dims, preferred_element_type=F32)


def dot3(lhs, rhs, dims=NN):
    return (
        dot1(lhs[0], rhs[0], dims) + dot1(lhs[0], rhs[1], dims) + dot1(lhs[1], rhs[0], dims)
    )


def eye_of(size):
    rows = lax.broadcasted_iota(jnp.int32, (size, size), 0)
    columns = lax.broadcasted_iota(jnp.int32, (size, size), 1)
    return (rows == columns).astype(F32)


def row_norm(matrix):
    return jnp.max(jnp.sum(jnp.abs(matrix), axis=1, keepdims=True), axis=0, keepdims=True)


def fast_inverse(matrix, identity):
    scale = START_SCALE / row_norm(matrix)
    error = identity - scale * matrix
    inverse = scale * (identity + error)
    error16 = error.astype(BF16)
    for _ in range(STEPS):
        error16 = dot1(error16, error16).astype(BF16)
        inverse = inverse + dot1(inverse.astype(BF16), error16)
    parts = split(inverse)
    residual = identity - dot3(split(matrix), parts)
    inverse = inverse + dot1(parts[0], residual.astype(BF16))
    return inverse, row_norm(residual)


def exact_dot(lhs, rhs):
    return lax.dot_general(
        lhs, rhs, NN, precision=lax.Precision.HIGHEST, preferred_element_type=F32
    )


def slow_inverse(matrix, identity, matrix_scr, inverse_scr):
    matrix_scr[...] = matrix
    inverse_scr[...] = identity * (START_SCALE / row_norm(matrix))

    def going(state):
        count, size = state
        return (size > 1e-3) & (count < 100)

    def step(state):
        count, _ = state
        inverse = inverse_scr[...]
        residual = identity - exact_dot(matrix_scr[...], inverse)
        inverse_scr[...] = inverse + exact_dot(inverse, residual)
        return count + 1, jnp.max(row_norm(residual))

    lax.while_loop(going, step, (jnp.int32(0), jnp.float32(1e9)))
    return inverse_scr[...], jnp.zeros((1, 1), F32)


def pack_symmetric(matrix):
    half = matrix.shape[0] // 2
    rows = lax.broadcasted_iota(jnp.int32, (half, half), 0)
    columns = lax.broadcasted_iota(jnp.int32, (half, half), 1)
    first, second = matrix[:half, :half], matrix[half:, half:]
    mixed = jnp.where(rows > columns, first, jnp.where(rows < columns, second, 0.0))
    return jnp.concatenate([matrix[half:, :half], mixed], axis=1)


def unpack_symmetric(packed):
    half = packed.shape[0]
    rows = lax.broadcasted_iota(jnp.int32, (half, half), 0)
    columns = lax.broadcasted_iota(jnp.int32, (half, half), 1)
    corner, mixed = packed[:, :half], packed[:, half:]
    first = jnp.where(rows > columns, mixed, 0.0)
    second = jnp.where(rows < columns, mixed, 0.0)
    return jnp.concatenate(
        [
            jnp.concatenate([first + first.T, corner.T], axis=1),
            jnp.concatenate([corner, second + second.T], axis=1),
        ],
        axis=0,
    )


def diagonal_of(matrix):
    return jnp.sum(matrix * eye_of(matrix.shape[0]), axis=0, keepdims=True)


def pack_kernel(
    place_ref, weight_ref, level_ref, ham_ref, coupling_ref, projector_ref, matrix_ref,
    part_ref, pack_scr,
):
    size = ham_ref.shape[0]
    part = part_ref.shape[0]
    ham_part = part // 2
    ham = 0.5 * (ham_ref[...] + ham_ref[...].T)
    pack_scr[...] = pack_symmetric(ham)
    index = place_ref[0]
    matrix_ref[:ham_part] = pack_scr[pl.ds(pl.multiple_of(index * ham_part, 8), ham_part), :]
    rows = pl.ds(pl.multiple_of(index * part, 8), part)
    matrix_ref[ham_part : ham_part + part] = coupling_ref[rows, :]
    row = lax.broadcasted_iota(jnp.int32, (8, size), 0)
    diagonal = diagonal_of(ham) + level_ref[...] + 2.0
    matrix_ref[ham_part + part :] = jnp.where(row == 0, diagonal, weight_ref[0])
    part_ref[...] = projector_ref[rows, :]


def pack(place, weight, level, ham, coupling, projector, parts):
    size = ham.shape[0]
    part = size // parts
    smem = pl.BlockSpec(memory_space=pltpu.SMEM)
    vmem = pl.BlockSpec(memory_space=pltpu.VMEM)
    return pl.pallas_call(
        pack_kernel,
        out_shape=(
            jax.ShapeDtypeStruct((part // 2 + part + 8, size), F32),
            jax.ShapeDtypeStruct((part, size), F32),
        ),
        in_specs=[smem, smem, vmem, vmem, vmem, vmem],
        out_specs=(vmem, vmem),
        scratch_shapes=[pltpu.VMEM((size // 2, size), F32)],
        compiler_params=pltpu.CompilerParams(vmem_limit_bytes=VMEM_BYTES),
        name="pack",
    )(place, weight, level, ham, coupling, projector)


def factor_kernel(
    shift_ref, matrix_ref, basis_ref, inverse_ref, link_ref, diag_scr, coupling_ref,
    matrix_scr, inverse_scr,
):
    count, parts, height, size = matrix_ref.shape
    part = size // parts
    ham_part = part // 2
    middle = count // 2
    identity = eye_of(size)
    basis = split(basis_ref[...])
    potential = dot3(basis, basis, NT)
    for n in range(count):
        packed = matrix_ref[n, :, :ham_part].reshape(size // 2, size)
        coupling_ref[n] = matrix_ref[n, :, ham_part : ham_part + part].reshape(size, size)
        diagonal = matrix_ref[n, 0, ham_part + part : ham_part + part + 1]
        weight = matrix_ref[n, 0, ham_part + part + 1 : ham_part + part + 2, :1]
        diag_scr[n] = (
            unpack_symmetric(packed)
            + (diagonal + shift_ref[0]) * identity
            + weight * potential
        )

    def eliminate(invert):
        worst = jnp.zeros((1, 1), F32)
        forward = diag_scr[0]
        backward = diag_scr[count - 1]

        def finish(n, matrix, worst):
            inverse, size_left = invert(matrix, identity)
            parts = split(inverse)
            inverse_ref[0, n] = parts[0]
            inverse_ref[1, n] = parts[1]
            return parts, jnp.maximum(worst, size_left)

        def keep(n, link):
            parts = split(link)
            link_ref[0, n] = parts[0]
            link_ref[1, n] = parts[1]
            return parts

        meeting = diag_scr[middle]
        for step in range(max(middle, count - 1 - middle)):
            ahead, behind = step, count - 1 - step
            if ahead < middle:
                parts, worst = finish(ahead, forward, worst)
                coupling = split(-(identity + coupling_ref[ahead + 1]))
                link = keep(ahead + 1, dot3(coupling, parts))
                update = dot3(link, coupling, NT)
                if ahead + 1 < middle:
                    forward = diag_scr[ahead + 1] - update
                else:
                    meeting = meeting - update
            if behind > middle:
                parts, worst = finish(behind, backward, worst)
                raw = -(identity + coupling_ref[behind])
                link = keep(behind, dot3(split(raw.T), parts))
                update = dot3(link, split(raw))
                if behind - 1 > middle:
                    backward = diag_scr[behind - 1] - update
                else:
                    meeting = meeting - update
        _, worst = finish(middle, meeting, worst)
        return worst

    worst = jnp.max(eliminate(fast_inverse))

    @pl.when(jnp.logical_not(worst <= RESIDUAL_BOUND))
    def _():
        eliminate(
            functools.partial(slow_inverse, matrix_scr=matrix_scr, inverse_scr=inverse_scr)
        )


def factorize(shift, matrices, basis):
    count, size = matrices.shape[0], matrices.shape[3]
    smem = pl.BlockSpec(memory_space=pltpu.SMEM)
    vmem = pl.BlockSpec(memory_space=pltpu.VMEM)
    half = jax.ShapeDtypeStruct((2, count, size, size), BF16)
    return pl.pallas_call(
        factor_kernel,
        out_shape=(half, half),
        in_specs=[smem, vmem, vmem],
        out_specs=(vmem, vmem),
        scratch_shapes=[
            pltpu.VMEM((count, size, size), F32),
            pltpu.VMEM((count, size, size), F32),
            pltpu.VMEM((size, size), F32),
            pltpu.VMEM((size, size), F32),
        ],
        compiler_params=pltpu.CompilerParams(vmem_limit_bytes=VMEM_BYTES),
        name="factorize",
    )(shift, matrices, basis)


def solve_kernel(
    place_ref, open_ref, matrix_ref, inverse_ref, link_ref, projector_ref, target_ref,
    *rest,
):
    count = inverse_ref.shape[1]
    source_refs, rest = rest[:count], rest[count:]
    wave_ref, adjoint_ref, share_ref, gram_ref, own_scr, k_scr = rest
    channels, width = source_refs[0].shape
    middle = count // 2
    me, column = place_ref[1], place_ref[2]
    inverses = [(inverse_ref[0, n], inverse_ref[1, n]) for n in range(count)]
    links = [(link_ref[0, n], link_ref[1, n]) if n != 0 else None for n in range(count)]
    projectors = [
        split(projector_ref[n].reshape(channels, projector_ref.shape[3])) for n in range(count)
    ]
    weight_row = matrix_ref.shape[2] - 7
    weights = [matrix_ref[n, 0, weight_row : weight_row + 1, :1] for n in range(count)]
    for n in range(count):
        own_scr[me ^ n] = source_refs[n][...]

    def solve(blocks):
        reduced = list(blocks)
        for n in range(1, middle + 1):
            reduced[n] = reduced[n] - dot3(split(reduced[n - 1]), links[n], NT)
        for n in range(count - 1, middle, -1):
            reduced[n - 1] = reduced[n - 1] - dot3(split(reduced[n]), links[n], NT)
        solved = [dot3(split(reduced[n]), inverses[n]) for n in range(count)]
        halves = [None] * count
        halves[middle] = split(solved[middle])
        for n in range(middle, 0, -1):
            solved[n - 1] = solved[n - 1] - dot3(halves[n], links[n])
            halves[n - 1] = split(solved[n - 1])
        for n in range(middle + 1, count):
            solved[n] = solved[n] - dot3(halves[n - 1], links[n])
            halves[n] = split(solved[n])
        return solved, halves

    wave, wave_halves = solve([own_scr[n].T for n in range(count)])
    k_total = dot3(wave_halves[0], projectors[0])
    for n in range(1, count):
        k_total = k_total + dot3(wave_halves[n], projectors[n])
    k_rows = lax.broadcasted_iota(jnp.int32, k_total.shape, 1)
    k_columns = lax.broadcasted_iota(jnp.int32, k_total.shape, 0) + column * width
    opened = (k_rows < open_ref[0]) & (k_columns < open_ref[0])
    residual = split(jnp.where(opened, k_total - target_ref[...].T, 0.0))
    drive = [PENALTY * wave[n] + dot3(residual, projectors[n], NT) for n in range(count)]
    adjoint, _ = solve(drive)

    share = share_ref.shape[0]
    k_scr[...] = k_total.T
    share_ref[...] = k_scr[pl.ds(pl.multiple_of(me * share, share), share), :]
    wave = [value.T for value in wave]
    adjoint = [value.T for value in adjoint]
    for n in range(count):
        own_scr[n] = wave[n]
    wave_ref[...] = own_scr[me]
    for n in range(count):
        own_scr[n] = adjoint[n]
    adjoint_ref[...] = own_scr[me]
    weighted = jnp.concatenate([weights[n] * wave[n] for n in range(count)], axis=1)
    gram = dot3(split(jnp.concatenate(adjoint, axis=1)), split(weighted), NT)
    gram = gram + gram.T
    half = channels // 2
    gram_ref[:half] = pack_symmetric(gram)
    gram_ref[half:] = jnp.broadcast_to(diagonal_of(gram), (8, channels))


def solve_all(place, opened, matrices, inverses, links, projectors, target, sources):
    count = len(sources)
    channels, width = sources[0].shape
    rows = target.shape[0]
    smem = pl.BlockSpec(memory_space=pltpu.SMEM)
    vmem = pl.BlockSpec(memory_space=pltpu.VMEM)
    return pl.pallas_call(
        solve_kernel,
        out_shape=(
            jax.ShapeDtypeStruct((channels, width), F32),
            jax.ShapeDtypeStruct((channels, width), F32),
            jax.ShapeDtypeStruct((rows // count, width), F32),
            jax.ShapeDtypeStruct((channels // 2 + 8, channels), F32),
        ),
        in_specs=[smem, smem] + [vmem] * (5 + count),
        out_specs=(vmem,) * 4,
        scratch_shapes=[
            pltpu.VMEM((count, channels, width), F32),
            pltpu.VMEM((rows, width), F32),
        ],
        compiler_params=pltpu.CompilerParams(vmem_limit_bytes=VMEM_BYTES),
        name="solve",
    )(place, opened, matrices, inverses, links, projectors, target, *sources)


def gradient_kernel(scale, own_ref, other_ref, basis_ref, out_ref):
    size = basis_ref.shape[0]
    total = own_ref[...] + other_ref[...]
    gram = unpack_symmetric(total[: size // 2])
    gram = gram + total[size // 2 : size // 2 + 1] * eye_of(size)
    out_ref[...] = scale * dot3(split(gram), split(basis_ref[...]))


def gradient(scale, own, other, basis):
    vmem = pl.BlockSpec(memory_space=pltpu.VMEM)
    return pl.pallas_call(
        functools.partial(gradient_kernel, scale),
        out_shape=jax.ShapeDtypeStruct(basis.shape, F32),
        in_specs=[vmem, vmem, vmem],
        out_specs=vmem,
        compiler_params=pltpu.CompilerParams(vmem_limit_bytes=VMEM_BYTES),
        name="gradient",
    )(own, other, basis)


def swap(value, axis, step):
    count = lax.axis_size(axis)
    return lax.ppermute(value, axis, [(i, i ^ step) for i in range(count)])


def gradient_total(gram, scale, basis):
    steps = []
    for axis in ("rhs", "energy"):
        step = 1
        while step < lax.axis_size(axis):
            steps.append((axis, step))
            step = step * 2
    other = jnp.zeros_like(gram)
    for index, (axis, step) in enumerate(steps):
        if index:
            gram = gram + other
        other = swap(gram, axis, step)
    return gradient(scale, gram, other, basis)


def per_device(
    ham_noise,
    channel_levels,
    coupling_noise,
    corr_weight,
    corr_basis,
    projector,
    energy_shift,
    sources,
    target,
    open_channels,
):
    elements, energies, halves = (lax.axis_size(axis) for axis in ("elem", "energy", "rhs"))
    parts = energies * halves
    element, half = lax.axis_index("elem"), lax.axis_index("rhs")
    quarter = lax.axis_index("energy") * halves + half
    place = jnp.stack([quarter, element, half]).astype(jnp.int32)
    matrices, projector_part = pack(
        place, corr_weight, channel_levels, ham_noise[0], coupling_noise[0], projector[0], parts
    )
    own = sources[0, 0]
    matrices = lax.all_gather(matrices, ("elem", "energy", "rhs"))
    projectors = lax.all_gather(projector_part, ("elem", "energy", "rhs"))
    source_all = [own] + [swap(own, "elem", step) for step in range(1, elements)]
    matrices = matrices.reshape((elements, parts) + matrices.shape[1:])
    projectors = projectors.reshape((elements, parts) + projectors.shape[1:])
    inverses, links = factorize(energy_shift, matrices, corr_basis)
    wave, adjoint, share, gram = solve_all(
        place, open_channels, matrices, inverses, links, projectors, target[0], source_all
    )
    basis_grad = gradient_total(gram, -1.0 / (energies * elements), corr_basis)
    return wave[None, None], adjoint[None, None], share[None], basis_grad


def solution(mesh):
    return jax.shard_map(
        per_device,
        mesh=mesh,
        in_specs=(
            P(("groups", "elem"), None, None),
            P(("groups", "elem"), None),
            P(("groups", "elem"), None, None),
            P(("groups", "elem")),
            P("groups", None),
            P(("groups", "elem"), None, None),
            P(("groups", "energy")),
            P(("groups", "energy"), "elem", None, "rhs"),
            P(("groups", "energy"), None, "rhs"),
            P(("groups", "energy")),
        ),
        out_specs=(
            P(("groups", "energy"), "elem", None, "rhs"),
            P(("groups", "energy"), "elem", None, "rhs"),
            P(("groups", "energy"), "elem", "rhs"),
            P("groups", None),
        ),
        check_vma=False,
    )
```

```python
import functools

import jax
import jax.numpy as jnp
from jax import lax
from jax.experimental import pallas as pl
from jax.experimental.pallas import tpu as pltpu
from jax.sharding import PartitionSpec as P

PENALTY = 0.5
STEPS = 3
START_SCALE = 1.75
RESIDUAL_BOUND = 0.01
F32 = jnp.float32
BF16 = jnp.bfloat16
NN = (((1,), (0,)), ((), ()))
NT = (((1,), (1,)), ((), ()))
VMEM_BYTES = 48 * 1024 * 1024


def split(value):
    high = value.astype(BF16)
    return high, (value - high.astype(F32)).astype(BF16)


def dot1(lhs, rhs, dims=NN):
    return lax.dot_general(lhs, rhs, dims, preferred_element_type=F32)


def dot3(lhs, rhs, dims=NN):
    return (
        dot1(lhs[0], rhs[0], dims) + dot1(lhs[0], rhs[1], dims) + dot1(lhs[1], rhs[0], dims)
    )


def eye_of(size):
    rows = lax.broadcasted_iota(jnp.int32, (size, size), 0)
    columns = lax.broadcasted_iota(jnp.int32, (size, size), 1)
    return (rows == columns).astype(F32)


def row_norm(matrix):
    return jnp.max(jnp.sum(jnp.abs(matrix), axis=1, keepdims=True), axis=0, keepdims=True)


def fast_inverse(matrix, identity):
    scale = START_SCALE / row_norm(matrix)
    error = identity - scale * matrix
    inverse = scale * (identity + error)
    error16 = error.astype(BF16)
    for _ in range(STEPS):
        error16 = dot1(error16, error16).astype(BF16)
        inverse = inverse + dot1(inverse.astype(BF16), error16)
    parts = split(inverse)
    residual = identity - dot3(split(matrix), parts)
    inverse = inverse + dot1(parts[0], residual.astype(BF16))
    return inverse, row_norm(residual)


def exact_dot(lhs, rhs):
    return lax.dot_general(
        lhs, rhs, NN, precision=lax.Precision.HIGHEST, preferred_element_type=F32
    )


def slow_inverse(matrix, identity, matrix_scr, inverse_scr):
    matrix_scr[...] = matrix
    inverse_scr[...] = identity * (START_SCALE / row_norm(matrix))

    def going(state):
        count, size = state
        return (size > 1e-3) & (count < 100)

    def step(state):
        count, _ = state
        inverse = inverse_scr[...]
        residual = identity - exact_dot(matrix_scr[...], inverse)
        inverse_scr[...] = inverse + exact_dot(inverse, residual)
        return count + 1, jnp.max(row_norm(residual))

    lax.while_loop(going, step, (jnp.int32(0), jnp.float32(1e9)))
    return inverse_scr[...], jnp.zeros((1, 1), F32)


def pack_symmetric(matrix):
    half = matrix.shape[0] // 2
    rows = lax.broadcasted_iota(jnp.int32, (half, half), 0)
    columns = lax.broadcasted_iota(jnp.int32, (half, half), 1)
    first, second = matrix[:half, :half], matrix[half:, half:]
    mixed = jnp.where(rows > columns, first, jnp.where(rows < columns, second, 0.0))
    return jnp.concatenate([matrix[half:, :half], mixed], axis=1)


def unpack_symmetric(packed):
    half = packed.shape[0]
    rows = lax.broadcasted_iota(jnp.int32, (half, half), 0)
    columns = lax.broadcasted_iota(jnp.int32, (half, half), 1)
    corner, mixed = packed[:, :half], packed[:, half:]
    first = jnp.where(rows > columns, mixed, 0.0)
    second = jnp.where(rows < columns, mixed, 0.0)
    return jnp.concatenate(
        [
            jnp.concatenate([first + first.T, corner.T], axis=1),
            jnp.concatenate([corner, second + second.T], axis=1),
        ],
        axis=0,
    )


def diagonal_of(matrix):
    return jnp.sum(matrix * eye_of(matrix.shape[0]), axis=0, keepdims=True)


def pack_kernel(
    place_ref, weight_ref, level_ref, ham_hbm, coupling_hbm, projector_hbm, whole_ref,
    part_ref, ham_ref, coupling_ref, projector_ref, sems,
):
    copies = [
        pltpu.make_async_copy(source.at[0], target, sems.at[index])
        for index, (source, target) in enumerate(
            ((ham_hbm, ham_ref), (coupling_hbm, coupling_ref), (projector_hbm, projector_ref))
        )
    ]
    for copy in copies:
        copy.start()
    parts = whole_ref.shape[0]
    size = ham_ref.shape[0]
    part = size // parts
    half = part // 2
    row = lax.broadcasted_iota(jnp.int32, (8, size), 0)
    copies[0].wait()
    ham = 0.5 * (ham_ref[...] + ham_ref[...].T)
    packed = pack_symmetric(ham)
    diagonal = diagonal_of(ham) + level_ref[...] + 2.0
    extra = jnp.where(row == 0, diagonal, weight_ref[0])
    copies[1].wait()
    copies[2].wait()
    for n in range(parts):
        whole_ref[n, :half] = packed[n * half : (n + 1) * half]
        whole_ref[n, half : half + part] = coupling_ref[n * part : (n + 1) * part]
        whole_ref[n, half + part : half + 2 * part] = projector_ref[n * part : (n + 1) * part]
        whole_ref[n, half + 2 * part :] = extra
    part_ref[...] = whole_ref[place_ref[0]]


def pack(place, weight, level, ham, coupling, projector, parts):
    size = ham.shape[1]
    part = size // parts
    height = part // 2 + 2 * part + 8
    smem = pl.BlockSpec(memory_space=pltpu.SMEM)
    vmem = pl.BlockSpec(memory_space=pltpu.VMEM)
    hbm = pl.BlockSpec(memory_space=pl.ANY)
    return pl.pallas_call(
        pack_kernel,
        out_shape=(
            jax.ShapeDtypeStruct((parts, height, size), F32),
            jax.ShapeDtypeStruct((height, size), F32),
        ),
        in_specs=[smem, smem, vmem, hbm, hbm, hbm],
        out_specs=(vmem, vmem),
        scratch_shapes=[pltpu.VMEM((size, size), F32)] * 3 + [pltpu.SemaphoreType.DMA((3,))],
        compiler_params=pltpu.CompilerParams(vmem_limit_bytes=VMEM_BYTES),
        name="pack",
    )(place, weight, level, ham, coupling, projector)


def pieces(place_ref, refs):
    for k, ref in enumerate(refs):
        for j in range(ref.shape[0]):
            yield place_ref[1] ^ k, (j if k == 0 else place_ref[0] ^ j), ref, j


def factor_kernel(count, shift_ref, place_ref, *rest):
    refs, rest = rest[:count], rest[count:]
    basis_ref, inverse_ref, link_ref, diag_scr, coupling_ref, pack_scr, extra_scr = rest[:7]
    matrix_scr, inverse_scr = rest[7:]
    size = basis_ref.shape[0]
    parts = refs[0].shape[0]
    part = size // parts
    half = part // 2
    middle = count // 2
    identity = eye_of(size)
    basis = split(basis_ref[...])
    potential = dot3(basis, basis, NT)
    for element, index, ref, j in pieces(place_ref, refs):
        start = pl.multiple_of(index * half, 8)
        pack_scr[element, pl.ds(start, half), :] = ref[j, :half]
        start = pl.multiple_of(index * part, 8)
        coupling_ref[element, pl.ds(start, part), :] = ref[j, half : half + part]
        if j == 0:
            extra_scr[element] = ref[j, half + 2 * part :]
    for n in range(count):
        diag_scr[n] = (
            unpack_symmetric(pack_scr[n])
            + (extra_scr[n, 0:1] + shift_ref[0]) * identity
            + extra_scr[n, 1:2, :1] * potential
        )

    def eliminate(invert):
        worst = jnp.zeros((1, 1), F32)
        forward = diag_scr[0]
        backward = diag_scr[count - 1]

        def finish(n, matrix, worst):
            inverse, size_left = invert(matrix, identity)
            parts = split(inverse)
            inverse_ref[0, n] = parts[0]
            inverse_ref[1, n] = parts[1]
            return parts, jnp.maximum(worst, size_left)

        def keep(n, link):
            parts = split(link)
            link_ref[0, n] = parts[0]
            link_ref[1, n] = parts[1]
            return parts

        meeting = diag_scr[middle]
        for step in range(max(middle, count - 1 - middle)):
            ahead, behind = step, count - 1 - step
            if ahead < middle:
                parts, worst = finish(ahead, forward, worst)
                coupling = split(-(identity + coupling_ref[ahead + 1]))
                link = keep(ahead + 1, dot3(coupling, parts))
                update = dot3(link, coupling, NT)
                if ahead + 1 < middle:
                    forward = diag_scr[ahead + 1] - update
                else:
                    meeting = meeting - update
            if behind > middle:
                parts, worst = finish(behind, backward, worst)
                raw = -(identity + coupling_ref[behind])
                link = keep(behind, dot3(split(raw.T), parts))
                update = dot3(link, split(raw))
                if behind - 1 > middle:
                    backward = diag_scr[behind - 1] - update
                else:
                    meeting = meeting - update
        _, worst = finish(middle, meeting, worst)
        return worst

    worst = jnp.max(eliminate(fast_inverse))

    @pl.when(jnp.logical_not(worst <= RESIDUAL_BOUND))
    def _():
        eliminate(
            functools.partial(slow_inverse, matrix_scr=matrix_scr, inverse_scr=inverse_scr)
        )


def factorize(shift, place, payloads, basis):
    count, size = len(payloads), basis.shape[0]
    smem = pl.BlockSpec(memory_space=pltpu.SMEM)
    vmem = pl.BlockSpec(memory_space=pltpu.VMEM)
    half = jax.ShapeDtypeStruct((2, count, size, size), BF16)
    return pl.pallas_call(
        functools.partial(factor_kernel, count),
        out_shape=(half, half),
        in_specs=[smem, smem] + [vmem] * (count + 1),
        out_specs=(vmem, vmem),
        scratch_shapes=[
            pltpu.VMEM((count, size, size), F32),
            pltpu.VMEM((count, size, size), F32),
            pltpu.VMEM((count, size // 2, size), F32),
            pltpu.VMEM((count, 8, size), F32),
            pltpu.VMEM((size, size), F32),
            pltpu.VMEM((size, size), F32),
        ],
        compiler_params=pltpu.CompilerParams(vmem_limit_bytes=VMEM_BYTES),
        name="factorize",
    )(shift, place, *payloads, basis)


def solve_kernel(count, place_ref, open_ref, inverse_ref, link_ref, target_ref, *rest):
    refs, source_refs, rest = rest[:count], rest[count : 2 * count], rest[2 * count :]
    wave_ref, adjoint_ref, share_ref, gram_ref, own_scr, k_scr, projector_scr, extra_scr = rest
    channels, width = source_refs[0].shape
    middle = count // 2
    me, column = place_ref[1], place_ref[2]
    parts = refs[0].shape[0]
    part = channels // parts
    begin = part // 2 + part
    for element, index, ref, j in pieces(place_ref, refs):
        start = pl.multiple_of(index * part, 8)
        projector_scr[element, pl.ds(start, part), :] = ref[j, begin : begin + part]
        if j == 0:
            extra_scr[element] = ref[j, begin + part :]
    inverses = [(inverse_ref[0, n], inverse_ref[1, n]) for n in range(count)]
    links = [(link_ref[0, n], link_ref[1, n]) if n != 0 else None for n in range(count)]
    projectors = [split(projector_scr[n]) for n in range(count)]
    weights = [extra_scr[n, 1:2, :1] for n in range(count)]
    for n in range(count):
        own_scr[me ^ n] = source_refs[n][...]

    def solve(blocks):
        reduced = list(blocks)
        for n in range(1, middle + 1):
            reduced[n] = reduced[n] - dot3(split(reduced[n - 1]), links[n], NT)
        for n in range(count - 1, middle, -1):
            reduced[n - 1] = reduced[n - 1] - dot3(split(reduced[n]), links[n], NT)
        solved = [dot3(split(reduced[n]), inverses[n]) for n in range(count)]
        halves = [None] * count
        halves[middle] = split(solved[middle])
        for n in range(middle, 0, -1):
            solved[n - 1] = solved[n - 1] - dot3(halves[n], links[n])
            halves[n - 1] = split(solved[n - 1])
        for n in range(middle + 1, count):
            solved[n] = solved[n] - dot3(halves[n - 1], links[n])
            halves[n] = split(solved[n])
        return solved, halves

    wave, wave_halves = solve([own_scr[n].T for n in range(count)])
    k_total = dot3(wave_halves[0], projectors[0])
    for n in range(1, count):
        k_total = k_total + dot3(wave_halves[n], projectors[n])
    k_rows = lax.broadcasted_iota(jnp.int32, k_total.shape, 1)
    k_columns = lax.broadcasted_iota(jnp.int32, k_total.shape, 0) + column * width
    opened = (k_rows < open_ref[0]) & (k_columns < open_ref[0])
    residual = split(jnp.where(opened, k_total - target_ref[...].T, 0.0))
    drive = [PENALTY * wave[n] + dot3(residual, projectors[n], NT) for n in range(count)]
    adjoint, _ = solve(drive)

    share = share_ref.shape[0]
    k_scr[...] = k_total.T
    share_ref[...] = k_scr[pl.ds(pl.multiple_of(me * share, share), share), :]
    wave = [value.T for value in wave]
    adjoint = [value.T for value in adjoint]
    for n in range(count):
        own_scr[n] = wave[n]
    wave_ref[...] = own_scr[me]
    for n in range(count):
        own_scr[n] = adjoint[n]
    adjoint_ref[...] = own_scr[me]
    weighted = jnp.concatenate([weights[n] * wave[n] for n in range(count)], axis=1)
    gram = dot3(split(jnp.concatenate(adjoint, axis=1)), split(weighted), NT)
    gram = gram + gram.T
    half = channels // 2
    gram_ref[:half] = pack_symmetric(gram)
    gram_ref[half:] = jnp.broadcast_to(diagonal_of(gram), (8, channels))


def solve_all(place, opened, inverses, links, target, payloads, sources):
    count = len(sources)
    channels, width = sources[0].shape
    rows = target.shape[0]
    smem = pl.BlockSpec(memory_space=pltpu.SMEM)
    vmem = pl.BlockSpec(memory_space=pltpu.VMEM)
    return pl.pallas_call(
        functools.partial(solve_kernel, count),
        out_shape=(
            jax.ShapeDtypeStruct((channels, width), F32),
            jax.ShapeDtypeStruct((channels, width), F32),
            jax.ShapeDtypeStruct((rows // count, width), F32),
            jax.ShapeDtypeStruct((channels // 2 + 8, channels), F32),
        ),
        in_specs=[smem, smem] + [vmem] * (3 + 2 * count),
        out_specs=(vmem,) * 4,
        scratch_shapes=[
            pltpu.VMEM((count, channels, width), F32),
            pltpu.VMEM((rows, width), F32),
            pltpu.VMEM((count, channels, channels), F32),
            pltpu.VMEM((count, 8, channels), F32),
        ],
        compiler_params=pltpu.CompilerParams(vmem_limit_bytes=VMEM_BYTES),
        name="solve",
    )(place, opened, inverses, links, target, *payloads, *sources)


def gradient_kernel(scale, own_ref, other_ref, basis_ref, out_ref):
    size = basis_ref.shape[0]
    total = own_ref[...] + other_ref[...]
    gram = unpack_symmetric(total[: size // 2])
    gram = gram + total[size // 2 : size // 2 + 1] * eye_of(size)
    out_ref[...] = scale * dot3(split(gram), split(basis_ref[...]))


def gradient(scale, own, other, basis):
    vmem = pl.BlockSpec(memory_space=pltpu.VMEM)
    return pl.pallas_call(
        functools.partial(gradient_kernel, scale),
        out_shape=jax.ShapeDtypeStruct(basis.shape, F32),
        in_specs=[vmem, vmem, vmem],
        out_specs=vmem,
        compiler_params=pltpu.CompilerParams(vmem_limit_bytes=VMEM_BYTES),
        name="gradient",
    )(own, other, basis)


def swap(value, axis, step):
    count = lax.axis_size(axis)
    return lax.ppermute(value, axis, [(i, i ^ step) for i in range(count)])


def gradient_total(gram, scale, basis):
    steps = []
    for axis in ("rhs", "energy"):
        step = 1
        while step < lax.axis_size(axis):
            steps.append((axis, step))
            step = step * 2
    other = jnp.zeros_like(gram)
    for index, (axis, step) in enumerate(steps):
        if index:
            gram = gram + other
        other = swap(gram, axis, step)
    return gradient(scale, gram, other, basis)


def per_device(
    ham_noise,
    channel_levels,
    coupling_noise,
    corr_weight,
    corr_basis,
    projector,
    energy_shift,
    sources,
    target,
    open_channels,
):
    elements, energies, halves = (lax.axis_size(axis) for axis in ("elem", "energy", "rhs"))
    parts = energies * halves
    element, half = lax.axis_index("elem"), lax.axis_index("rhs")
    quarter = half * energies + lax.axis_index("energy")
    place = jnp.stack([quarter, element, half]).astype(jnp.int32)
    own = sources[0, 0]
    whole, mine = pack(
        place, corr_weight, channel_levels, ham_noise, coupling_noise, projector, parts
    )
    order = [*range(2, elements), 1]
    sources_by = {0: own, 1: swap(own, "elem", 1)}
    payloads_by = {0: whole}
    for step in order:
        payload = swap(mine, "elem", step)[None]
        for axis in ("energy", "rhs"):
            distance = 1
            while distance < lax.axis_size(axis):
                other = swap(payload, axis, distance)
                payload = jnp.concatenate([payload, other], axis=0)
                distance = distance * 2
        payloads_by[step] = payload
    for step in order[:-1]:
        sources_by[step] = swap(own, "elem", step)
    payloads = [payloads_by[step] for step in range(elements)]
    source_all = [sources_by[step] for step in range(elements)]
    inverses, links = factorize(energy_shift, place, payloads, corr_basis)
    wave, adjoint, share, gram = solve_all(
        place, open_channels, inverses, links, target[0], payloads, source_all
    )
    basis_grad = gradient_total(gram, -1.0 / (energies * elements), corr_basis)
    return wave[None, None], adjoint[None, None], share[None], basis_grad


def solution(mesh):
    return jax.shard_map(
        per_device,
        mesh=mesh,
        in_specs=(
            P(("groups", "elem"), None, None),
            P(("groups", "elem"), None),
            P(("groups", "elem"), None, None),
            P(("groups", "elem")),
            P("groups", None),
            P(("groups", "elem"), None, None),
            P(("groups", "energy")),
            P(("groups", "energy"), "elem", None, "rhs"),
            P(("groups", "energy"), None, "rhs"),
            P(("groups", "energy")),
        ),
        out_specs=(
            P(("groups", "energy"), "elem", None, "rhs"),
            P(("groups", "energy"), "elem", None, "rhs"),
            P(("groups", "energy"), "elem", "rhs"),
            P("groups", None),
        ),
        check_vma=False,
    )
```

```python
import functools

import jax
import jax.numpy as jnp
from jax import lax
from jax.experimental import pallas as pl
from jax.experimental.pallas import tpu as pltpu
from jax.sharding import PartitionSpec as P

PENALTY = 0.5
STEPS = 2
START_SCALE = 1.85
RESIDUAL_BOUND = 0.01
F32 = jnp.float32
BF16 = jnp.bfloat16
NN = (((1,), (0,)), ((), ()))
NT = (((1,), (1,)), ((), ()))
VMEM_BYTES = 48 * 1024 * 1024
PACK_BYTES = 60 * 1024 * 1024


def split(value):
    high = value.astype(BF16)
    return high, (value - high.astype(F32)).astype(BF16)


def dot1(lhs, rhs, dims=NN):
    return lax.dot_general(lhs, rhs, dims, preferred_element_type=F32)


def dot3(lhs, rhs, dims=NN):
    return (
        dot1(lhs[0], rhs[0], dims) + dot1(lhs[0], rhs[1], dims) + dot1(lhs[1], rhs[0], dims)
    )


def eye_of(size):
    rows = lax.broadcasted_iota(jnp.int32, (size, size), 0)
    columns = lax.broadcasted_iota(jnp.int32, (size, size), 1)
    return (rows == columns).astype(F32)


def row_norm(matrix):
    return jnp.max(jnp.sum(jnp.abs(matrix), axis=1, keepdims=True), axis=0, keepdims=True)


def fast_inverse(matrix, identity):
    scale = START_SCALE / row_norm(matrix)
    error = identity - scale * matrix
    inverse = scale * (identity + error)
    error16 = error.astype(BF16)
    for _ in range(STEPS):
        error16 = dot1(error16, error16).astype(BF16)
        inverse = inverse + dot1(inverse.astype(BF16), error16)
    parts = split(inverse)
    residual = identity - dot3(split(matrix), parts)
    inverse = inverse + dot1(parts[0], residual.astype(BF16))
    return inverse, row_norm(residual)


def exact_dot(lhs, rhs):
    return lax.dot_general(
        lhs, rhs, NN, precision=lax.Precision.HIGHEST, preferred_element_type=F32
    )


def slow_inverse(matrix, identity, matrix_scr, inverse_scr):
    matrix_scr[...] = matrix
    inverse_scr[...] = identity * (START_SCALE / row_norm(matrix))

    def going(state):
        count, size = state
        return (size > 1e-3) & (count < 100)

    def step(state):
        count, _ = state
        inverse = inverse_scr[...]
        residual = identity - exact_dot(matrix_scr[...], inverse)
        inverse_scr[...] = inverse + exact_dot(inverse, residual)
        return count + 1, jnp.max(row_norm(residual))

    lax.while_loop(going, step, (jnp.int32(0), jnp.float32(1e9)))
    return inverse_scr[...], jnp.zeros((1, 1), F32)


def pack_symmetric(matrix):
    half = matrix.shape[0] // 2
    rows = lax.broadcasted_iota(jnp.int32, (half, half), 0)
    columns = lax.broadcasted_iota(jnp.int32, (half, half), 1)
    first, second = matrix[:half, :half], matrix[half:, half:]
    mixed = jnp.where(rows > columns, first, jnp.where(rows < columns, second, 0.0))
    return jnp.concatenate([matrix[half:, :half], mixed], axis=1)


def unpack_symmetric(packed):
    half = packed.shape[0]
    rows = lax.broadcasted_iota(jnp.int32, (half, half), 0)
    columns = lax.broadcasted_iota(jnp.int32, (half, half), 1)
    corner, mixed = packed[:, :half], packed[:, half:]
    first = jnp.where(rows > columns, mixed, 0.0)
    second = jnp.where(rows < columns, mixed, 0.0)
    return jnp.concatenate(
        [
            jnp.concatenate([first + first.T, corner.T], axis=1),
            jnp.concatenate([corner, second + second.T], axis=1),
        ],
        axis=0,
    )


def diagonal_of(matrix):
    return jnp.sum(matrix * eye_of(matrix.shape[0]), axis=0, keepdims=True)


def extra_rows(ham, level, weight):
    row = lax.broadcasted_iota(jnp.int32, (8, ham.shape[1]), 0)
    return jnp.where(row == 0, diagonal_of(ham) + level + 2.0, weight)


def pack_part_kernel(
    place_ref, weight_ref, level_hbm, ham_hbm, coupling_hbm, projector_hbm, out_ref, ham_ref,
    pack_scr, level_ref, sems,
):
    size = ham_ref.shape[0]
    part = (out_ref.shape[0] - 8) * 2 // 5
    half = part // 2
    rows = pl.ds(pl.multiple_of(place_ref[0] * part, 8), part)
    copies = [
        pltpu.make_async_copy(source, target, sems.at[index])
        for index, (source, target) in enumerate(
            (
                (ham_hbm.at[0], ham_ref),
                (level_hbm, level_ref),
                (coupling_hbm.at[0, rows], out_ref.at[half : half + part]),
                (projector_hbm.at[0, rows], out_ref.at[half + part : half + 2 * part]),
            )
        )
    ]
    for copy in copies:
        copy.start()
    copies[0].wait()
    copies[1].wait()
    ham = 0.5 * (ham_ref[...] + ham_ref[...].T)
    pack_scr[...] = pack_symmetric(ham)
    out_ref[:half] = pack_scr[pl.ds(pl.multiple_of(place_ref[0] * half, 8), half), :]
    out_ref[half + 2 * part :] = extra_rows(ham, level_ref[...], weight_ref[0])
    copies[2].wait()
    copies[3].wait()


def pack_part(place, weight, level, ham, coupling, projector, parts):
    size = ham.shape[1]
    part = size // parts
    smem = pl.BlockSpec(memory_space=pltpu.SMEM)
    vmem = pl.BlockSpec(memory_space=pltpu.VMEM)
    anywhere = pl.BlockSpec(memory_space=pl.ANY)
    return pl.pallas_call(
        pack_part_kernel,
        out_shape=jax.ShapeDtypeStruct((part // 2 + 2 * part + 8, size), F32),
        in_specs=[smem, smem] + [anywhere] * 4,
        out_specs=vmem,
        scratch_shapes=[
            pltpu.VMEM((size, size), F32),
            pltpu.VMEM((size // 2, size), F32),
            pltpu.VMEM((1, size), F32),
            pltpu.SemaphoreType.DMA((4,)),
        ],
        compiler_params=pltpu.CompilerParams(vmem_limit_bytes=PACK_BYTES),
        name="pack_part",
    )(place, weight, level, ham, coupling, projector)


def pack_kernel(weight_ref, level_ref, ham_ref, coupling_ref, projector_ref, whole_ref):
    parts = whole_ref.shape[0]
    size = ham_ref.shape[1]
    part = size // parts
    half = part // 2
    ham = 0.5 * (ham_ref[0] + ham_ref[0].T)
    packed = pack_symmetric(ham)
    extra = extra_rows(ham, level_ref[...], weight_ref[0])
    for n in range(parts):
        rows = slice(n * part, (n + 1) * part)
        whole_ref[n, :half] = packed[n * half : (n + 1) * half]
        whole_ref[n, half : half + part] = coupling_ref[0, rows]
        whole_ref[n, half + part : half + 2 * part] = projector_ref[0, rows]
        whole_ref[n, half + 2 * part :] = extra


def pack(weight, level, ham, coupling, projector, parts):
    size = ham.shape[1]
    part = size // parts
    smem = pl.BlockSpec(memory_space=pltpu.SMEM)
    vmem = pl.BlockSpec(memory_space=pltpu.VMEM)
    return pl.pallas_call(
        pack_kernel,
        out_shape=jax.ShapeDtypeStruct((parts, part // 2 + 2 * part + 8, size), F32),
        in_specs=[smem] + [vmem] * 4,
        out_specs=vmem,
        compiler_params=pltpu.CompilerParams(vmem_limit_bytes=VMEM_BYTES),
        name="pack",
    )(weight, level, ham, coupling, projector)


def potential_kernel(basis_ref, out_ref):
    basis = split(basis_ref[...])
    out_ref[...] = dot3(basis, basis, NT)


def potential_of(basis):
    vmem = pl.BlockSpec(memory_space=pltpu.VMEM)
    return pl.pallas_call(
        potential_kernel,
        out_shape=jax.ShapeDtypeStruct((basis.shape[0],) * 2, F32),
        in_specs=[vmem],
        out_specs=vmem,
        compiler_params=pltpu.CompilerParams(vmem_limit_bytes=VMEM_BYTES),
        name="potential",
    )(basis)


def pieces(place_ref, refs):
    for k, ref in enumerate(refs):
        for j in range(ref.shape[0]):
            yield place_ref[1] ^ k, (j if k == 0 else place_ref[0] ^ j), ref, j


def factor_kernel(count, shift_ref, place_ref, *rest):
    refs, rest = rest[:count], rest[count:]
    potential_ref, inverse_ref, link_ref, diag_scr, coupling_ref, pack_scr, extra_scr = rest[:7]
    matrix_scr, inverse_scr = rest[7:]
    size = potential_ref.shape[0]
    parts = refs[0].shape[0]
    part = size // parts
    half = part // 2
    middle = count // 2
    identity = eye_of(size)
    potential = potential_ref[...]
    for element, index, ref, j in pieces(place_ref, refs):
        start = pl.multiple_of(index * half, 8)
        pack_scr[element, pl.ds(start, half), :] = ref[j, :half]
        start = pl.multiple_of(index * part, 8)
        coupling_ref[element, pl.ds(start, part), :] = ref[j, half : half + part]
        if j == 0:
            extra_scr[element] = ref[j, half + 2 * part :]
    for n in range(count):
        diag_scr[n] = (
            unpack_symmetric(pack_scr[n])
            + (extra_scr[n, 0:1] + shift_ref[0]) * identity
            + extra_scr[n, 1:2, :1] * potential
        )

    def eliminate(invert):
        worst = jnp.zeros((1, 1), F32)
        forward = diag_scr[0]
        backward = diag_scr[count - 1]

        def finish(n, matrix, worst):
            inverse, size_left = invert(matrix, identity)
            parts = split(inverse)
            inverse_ref[0, n] = parts[0]
            inverse_ref[1, n] = parts[1]
            return parts, jnp.maximum(worst, size_left)

        def keep(n, link):
            parts = split(link)
            link_ref[0, n] = parts[0]
            link_ref[1, n] = parts[1]
            return parts

        meeting = diag_scr[middle]
        for step in range(max(middle, count - 1 - middle)):
            ahead, behind = step, count - 1 - step
            if ahead < middle:
                parts, worst = finish(ahead, forward, worst)
                coupling = split(-(identity + coupling_ref[ahead + 1]))
                link = keep(ahead + 1, dot3(coupling, parts))
                update = dot3(link, coupling, NT)
                if ahead + 1 < middle:
                    forward = diag_scr[ahead + 1] - update
                else:
                    meeting = meeting - update
            if behind > middle:
                parts, worst = finish(behind, backward, worst)
                raw = -(identity + coupling_ref[behind])
                link = keep(behind, dot3(split(raw.T), parts))
                update = dot3(link, split(raw))
                if behind - 1 > middle:
                    backward = diag_scr[behind - 1] - update
                else:
                    meeting = meeting - update
        _, worst = finish(middle, meeting, worst)
        return worst

    worst = jnp.max(eliminate(fast_inverse))

    @pl.when(jnp.logical_not(worst <= RESIDUAL_BOUND))
    def _():
        eliminate(
            functools.partial(slow_inverse, matrix_scr=matrix_scr, inverse_scr=inverse_scr)
        )


def factorize(shift, place, payloads, potential):
    count, size = len(payloads), potential.shape[0]
    smem = pl.BlockSpec(memory_space=pltpu.SMEM)
    vmem = pl.BlockSpec(memory_space=pltpu.VMEM)
    half = jax.ShapeDtypeStruct((2, count, size, size), BF16)
    return pl.pallas_call(
        functools.partial(factor_kernel, count),
        out_shape=(half, half),
        in_specs=[smem, smem] + [vmem] * (count + 1),
        out_specs=(vmem, vmem),
        scratch_shapes=[
            pltpu.VMEM((count, size, size), F32),
            pltpu.VMEM((count, size, size), F32),
            pltpu.VMEM((count, size // 2, size), F32),
            pltpu.VMEM((count, 8, size), F32),
            pltpu.VMEM((size, size), F32),
            pltpu.VMEM((size, size), F32),
        ],
        compiler_params=pltpu.CompilerParams(vmem_limit_bytes=VMEM_BYTES),
        name="factorize",
    )(shift, place, *payloads, potential)


def solve_kernel(count, place_ref, open_ref, inverse_ref, link_ref, target_ref, *rest):
    refs, source_refs, rest = rest[:count], rest[count : 2 * count], rest[2 * count :]
    wave_ref, adjoint_ref, share_ref, gram_ref, own_scr, k_scr, projector_scr, extra_scr = rest
    channels, width = source_refs[0].shape
    middle = count // 2
    me, column = place_ref[1], place_ref[2]
    parts = refs[0].shape[0]
    part = channels // parts
    begin = part // 2 + part
    for element, index, ref, j in pieces(place_ref, refs):
        start = pl.multiple_of(index * part, 8)
        projector_scr[element, pl.ds(start, part), :] = ref[j, begin : begin + part]
        if j == 0:
            extra_scr[element] = ref[j, begin + part :]
    inverses = [(inverse_ref[0, n], inverse_ref[1, n]) for n in range(count)]
    links = [(link_ref[0, n], link_ref[1, n]) if n != 0 else None for n in range(count)]
    projectors = [split(projector_scr[n]) for n in range(count)]
    weights = [extra_scr[n, 1:2, :1] for n in range(count)]
    for n in range(count):
        own_scr[me ^ n] = source_refs[n][...]

    def solve(blocks):
        reduced = list(blocks)
        for n in range(1, middle + 1):
            reduced[n] = reduced[n] - dot3(split(reduced[n - 1]), links[n], NT)
        for n in range(count - 1, middle, -1):
            reduced[n - 1] = reduced[n - 1] - dot3(split(reduced[n]), links[n], NT)
        solved = [dot3(split(reduced[n]), inverses[n]) for n in range(count)]
        halves = [None] * count
        halves[middle] = split(solved[middle])
        for n in range(middle, 0, -1):
            solved[n - 1] = solved[n - 1] - dot3(halves[n], links[n])
            halves[n - 1] = split(solved[n - 1])
        for n in range(middle + 1, count):
            solved[n] = solved[n] - dot3(halves[n - 1], links[n])
            halves[n] = split(solved[n])
        return solved, halves

    wave, wave_halves = solve([own_scr[n].T for n in range(count)])
    k_total = dot3(wave_halves[0], projectors[0])
    for n in range(1, count):
        k_total = k_total + dot3(wave_halves[n], projectors[n])
    k_rows = lax.broadcasted_iota(jnp.int32, k_total.shape, 1)
    k_columns = lax.broadcasted_iota(jnp.int32, k_total.shape, 0) + column * width
    opened = (k_rows < open_ref[0]) & (k_columns < open_ref[0])
    residual = split(jnp.where(opened, k_total - target_ref[...].T, 0.0))
    drive = [PENALTY * wave[n] + dot3(residual, projectors[n], NT) for n in range(count)]
    adjoint, _ = solve(drive)

    share = share_ref.shape[0]
    k_scr[...] = k_total.T
    share_ref[...] = k_scr[pl.ds(pl.multiple_of(me * share, share), share), :]
    wave = [value.T for value in wave]
    adjoint = [value.T for value in adjoint]
    for n in range(count):
        own_scr[n] = wave[n]
    wave_ref[...] = own_scr[me]
    for n in range(count):
        own_scr[n] = adjoint[n]
    adjoint_ref[...] = own_scr[me]
    weighted = jnp.concatenate([weights[n] * wave[n] for n in range(count)], axis=1)
    gram = dot3(split(jnp.concatenate(adjoint, axis=1)), split(weighted), NT)
    gram = gram + gram.T
    half = channels // 2
    gram_ref[:half] = pack_symmetric(gram)
    gram_ref[half:] = jnp.broadcast_to(diagonal_of(gram), (8, channels))


def solve_all(place, opened, inverses, links, target, payloads, sources):
    count = len(sources)
    channels, width = sources[0].shape
    rows = target.shape[0]
    smem = pl.BlockSpec(memory_space=pltpu.SMEM)
    vmem = pl.BlockSpec(memory_space=pltpu.VMEM)
    return pl.pallas_call(
        functools.partial(solve_kernel, count),
        out_shape=(
            jax.ShapeDtypeStruct((channels, width), F32),
            jax.ShapeDtypeStruct((channels, width), F32),
            jax.ShapeDtypeStruct((rows // count, width), F32),
            jax.ShapeDtypeStruct((channels // 2 + 8, channels), F32),
        ),
        in_specs=[smem, smem] + [vmem] * (3 + 2 * count),
        out_specs=(vmem,) * 4,
        scratch_shapes=[
            pltpu.VMEM((count, channels, width), F32),
            pltpu.VMEM((rows, width), F32),
            pltpu.VMEM((count, channels, channels), F32),
            pltpu.VMEM((count, 8, channels), F32),
        ],
        compiler_params=pltpu.CompilerParams(vmem_limit_bytes=VMEM_BYTES),
        name="solve",
    )(place, opened, inverses, links, target, *payloads, *sources)


def gradient_kernel(scale, own_ref, other_ref, basis_ref, out_ref):
    size = basis_ref.shape[0]
    total = own_ref[...] + other_ref[...]
    gram = unpack_symmetric(total[: size // 2])
    gram = gram + total[size // 2 : size // 2 + 1] * eye_of(size)
    out_ref[...] = scale * dot3(split(gram), split(basis_ref[...]))


def gradient(scale, own, other, basis):
    vmem = pl.BlockSpec(memory_space=pltpu.VMEM)
    return pl.pallas_call(
        functools.partial(gradient_kernel, scale),
        out_shape=jax.ShapeDtypeStruct(basis.shape, F32),
        in_specs=[vmem, vmem, vmem],
        out_specs=vmem,
        compiler_params=pltpu.CompilerParams(vmem_limit_bytes=VMEM_BYTES),
        name="gradient",
    )(own, other, basis)


def swap(value, axis, step):
    count = lax.axis_size(axis)
    return lax.ppermute(value, axis, [(i, i ^ step) for i in range(count)])


def gradient_total(gram, scale, basis):
    steps = []
    for axis in ("rhs", "energy"):
        step = 1
        while step < lax.axis_size(axis):
            steps.append((axis, step))
            step = step * 2
    other = jnp.zeros_like(gram)
    for index, (axis, step) in enumerate(steps):
        if index:
            gram = gram + other
        other = swap(gram, axis, step)
    return gradient(scale, gram, other, basis)


def per_device(
    ham_noise,
    channel_levels,
    coupling_noise,
    corr_weight,
    corr_basis,
    projector,
    energy_shift,
    sources,
    target,
    open_channels,
):
    elements, energies, halves = (lax.axis_size(axis) for axis in ("elem", "energy", "rhs"))
    parts = energies * halves
    element, half = lax.axis_index("elem"), lax.axis_index("rhs")
    quarter = half * energies + lax.axis_index("energy")
    place = jnp.stack([quarter, element, half]).astype(jnp.int32)
    own = sources[0, 0]
    raw = (corr_weight, channel_levels, ham_noise, coupling_noise, projector)
    mine = pack_part(place, *raw, parts)
    whole = pack(*raw, parts)
    potential = potential_of(corr_basis)

    def spread(payload):
        for axis in ("energy", "rhs"):
            distance = 1
            while distance < lax.axis_size(axis):
                payload = jnp.concatenate([payload, swap(payload, axis, distance)], axis=0)
                distance = distance * 2
        return payload

    def reach(value):
        found = {0: value}
        for step in range(1, elements):
            low = step & -step
            found[step] = swap(found[step ^ low], "elem", low)
        return found

    near = reach(mine)
    payloads_by = {0: whole}
    for step in range(1, elements):
        payloads_by[step] = spread(near[step][None])
    sources_by = reach(own)
    payloads = [payloads_by[step] for step in range(elements)]
    source_all = [sources_by[step] for step in range(elements)]
    inverses, links = factorize(energy_shift, place, payloads, potential)
    wave, adjoint, share, gram = solve_all(
        place, open_channels, inverses, links, target[0], payloads, source_all
    )
    basis_grad = gradient_total(gram, -1.0 / (energies * elements), corr_basis)
    return wave[None, None], adjoint[None, None], share[None], basis_grad


def solution(mesh):
    return jax.shard_map(
        per_device,
        mesh=mesh,
        in_specs=(
            P(("groups", "elem"), None, None),
            P(("groups", "elem"), None),
            P(("groups", "elem"), None, None),
            P(("groups", "elem")),
            P("groups", None),
            P(("groups", "elem"), None, None),
            P(("groups", "energy")),
            P(("groups", "energy"), "elem", None, "rhs"),
            P(("groups", "energy"), None, "rhs"),
            P(("groups", "energy")),
        ),
        out_specs=(
            P(("groups", "energy"), "elem", None, "rhs"),
            P(("groups", "energy"), "elem", None, "rhs"),
            P(("groups", "energy"), "elem", "rhs"),
            P("groups", None),
        ),
        check_vma=False,
    )
```

```python
import functools

import jax
import jax.numpy as jnp
from jax import lax
from jax.experimental import pallas as pl
from jax.experimental.pallas import tpu as pltpu
from jax.sharding import PartitionSpec as P

PENALTY = 0.5
START_SCALE = 0.95
SLOW_SCALE = 1.75
RESIDUAL_BOUND = 0.01
F32 = jnp.float32
BF16 = jnp.bfloat16
NN = (((1,), (0,)), ((), ()))
NT = (((1,), (1,)), ((), ()))
VMEM_BYTES = 48 * 1024 * 1024
PACK_BYTES = 60 * 1024 * 1024


def split(value):
    high = value.astype(BF16)
    return high, (value - high.astype(F32)).astype(BF16)


def dot1(lhs, rhs, dims=NN):
    return lax.dot_general(lhs, rhs, dims, preferred_element_type=F32)


def dot3(lhs, rhs, dims=NN):
    return (
        dot1(lhs[0], rhs[0], dims) + dot1(lhs[0], rhs[1], dims) + dot1(lhs[1], rhs[0], dims)
    )


def eye_of(size):
    rows = lax.broadcasted_iota(jnp.int32, (size, size), 0)
    columns = lax.broadcasted_iota(jnp.int32, (size, size), 1)
    return (rows == columns).astype(F32)


def row_norm(matrix):
    return jnp.max(jnp.sum(jnp.abs(matrix), axis=1, keepdims=True), axis=0, keepdims=True)


def fast_inverse(matrix, identity, steps):
    diagonal = matrix * identity
    by_row = START_SCALE / jnp.sum(diagonal, axis=1, keepdims=True)
    by_column = START_SCALE / jnp.sum(diagonal, axis=0, keepdims=True)
    error = identity - by_row * matrix
    inverse = (identity + error) * by_column
    error16 = error.astype(BF16)
    for _ in range(steps):
        error16 = dot1(error16, error16).astype(BF16)
        inverse = inverse + dot1(error16, inverse.astype(BF16))
    parts = split(inverse)
    residual = identity - dot3(split(matrix), parts)
    inverse = inverse + dot1(parts[0], residual.astype(BF16))
    return inverse, row_norm(residual)


def exact_dot(lhs, rhs):
    return lax.dot_general(
        lhs, rhs, NN, precision=lax.Precision.HIGHEST, preferred_element_type=F32
    )


def slow_inverse(matrix, identity, steps, matrix_scr, inverse_scr):
    matrix_scr[...] = matrix
    inverse_scr[...] = identity * (SLOW_SCALE / row_norm(matrix))

    def going(state):
        count, size = state
        return (size > 1e-3) & (count < 100)

    def step(state):
        count, _ = state
        inverse = inverse_scr[...]
        residual = identity - exact_dot(matrix_scr[...], inverse)
        inverse_scr[...] = inverse + exact_dot(inverse, residual)
        return count + 1, jnp.max(row_norm(residual))

    lax.while_loop(going, step, (jnp.int32(0), jnp.float32(1e9)))
    return inverse_scr[...], jnp.zeros((1, 1), F32)


def pack_symmetric(matrix):
    half = matrix.shape[0] // 2
    rows = lax.broadcasted_iota(jnp.int32, (half, half), 0)
    columns = lax.broadcasted_iota(jnp.int32, (half, half), 1)
    first, second = matrix[:half, :half], matrix[half:, half:]
    mixed = jnp.where(rows > columns, first, jnp.where(rows < columns, second, 0.0))
    return jnp.concatenate([matrix[half:, :half], mixed], axis=1)


def unpack_symmetric(packed):
    half = packed.shape[0]
    rows = lax.broadcasted_iota(jnp.int32, (half, half), 0)
    columns = lax.broadcasted_iota(jnp.int32, (half, half), 1)
    corner, mixed = packed[:, :half], packed[:, half:]
    first = jnp.where(rows > columns, mixed, 0.0)
    second = jnp.where(rows < columns, mixed, 0.0)
    return jnp.concatenate(
        [
            jnp.concatenate([first + first.T, corner.T], axis=1),
            jnp.concatenate([corner, second + second.T], axis=1),
        ],
        axis=0,
    )


def diagonal_of(matrix):
    return jnp.sum(matrix * eye_of(matrix.shape[0]), axis=0, keepdims=True)


def extra_rows(ham, level, weight):
    row = lax.broadcasted_iota(jnp.int32, (8, ham.shape[1]), 0)
    return jnp.where(row == 0, diagonal_of(ham) + level + 2.0, weight)


def quarter_index():
    return lax.axis_index("rhs") * lax.axis_size("energy") + lax.axis_index("energy")


def pack_part_kernel(
    weight_ref, level_hbm, ham_hbm, coupling_hbm, projector_hbm, out_ref, part_ref, ham_ref,
    pack_scr, level_ref, sems,
):
    part = part_ref.shape[0]
    half = part // 2
    index = quarter_index()
    rows = pl.ds(pl.multiple_of(index * part, 8), part)
    copies = [
        pltpu.make_async_copy(source, target, sems.at[number])
        for number, (source, target) in enumerate(
            (
                (ham_hbm.at[0], ham_ref),
                (level_hbm, level_ref),
                (coupling_hbm.at[0, rows], out_ref.at[half : half + part]),
                (projector_hbm.at[0, rows], part_ref),
            )
        )
    ]
    for copy in copies:
        copy.start()
    copies[0].wait()
    copies[1].wait()
    ham = 0.5 * (ham_ref[...] + ham_ref[...].T)
    pack_scr[...] = pack_symmetric(ham)
    out_ref[:half] = pack_scr[pl.ds(pl.multiple_of(index * half, 8), half), :]
    out_ref[half + part :] = extra_rows(ham, level_ref[...], weight_ref[0])
    copies[2].wait()
    copies[3].wait()


def pack_part(weight, level, ham, coupling, projector, parts):
    size = ham.shape[1]
    part = size // parts
    smem = pl.BlockSpec(memory_space=pltpu.SMEM)
    vmem = pl.BlockSpec(memory_space=pltpu.VMEM)
    anywhere = pl.BlockSpec(memory_space=pl.ANY)
    return pl.pallas_call(
        pack_part_kernel,
        out_shape=(
            jax.ShapeDtypeStruct((part // 2 + part + 8, size), F32),
            jax.ShapeDtypeStruct((part, size), F32),
        ),
        in_specs=[smem] + [anywhere] * 4,
        out_specs=(vmem, vmem),
        scratch_shapes=[
            pltpu.VMEM((size, size), F32),
            pltpu.VMEM((size // 2, size), F32),
            pltpu.VMEM((1, size), F32),
            pltpu.SemaphoreType.DMA((4,)),
        ],
        compiler_params=pltpu.CompilerParams(vmem_limit_bytes=PACK_BYTES),
        name="pack_part",
    )(weight, level, ham, coupling, projector)


def pack_kernel(weight_ref, level_ref, ham_ref, coupling_ref, whole_ref):
    parts = whole_ref.shape[0]
    size = ham_ref.shape[1]
    part = size // parts
    half = part // 2
    ham = 0.5 * (ham_ref[0] + ham_ref[0].T)
    packed = pack_symmetric(ham)
    extra = extra_rows(ham, level_ref[...], weight_ref[0])
    for n in range(parts):
        whole_ref[n, :half] = packed[n * half : (n + 1) * half]
        whole_ref[n, half : half + part] = coupling_ref[0, n * part : (n + 1) * part]
        whole_ref[n, half + part :] = extra


def pack(weight, level, ham, coupling, parts):
    size = ham.shape[1]
    part = size // parts
    smem = pl.BlockSpec(memory_space=pltpu.SMEM)
    vmem = pl.BlockSpec(memory_space=pltpu.VMEM)
    return pl.pallas_call(
        pack_kernel,
        out_shape=jax.ShapeDtypeStruct((parts, part // 2 + part + 8, size), F32),
        in_specs=[smem] + [vmem] * 3,
        out_specs=vmem,
        compiler_params=pltpu.CompilerParams(vmem_limit_bytes=VMEM_BYTES),
        name="pack",
    )(weight, level, ham, coupling)


def potential_kernel(basis_ref, out_ref):
    basis = split(basis_ref[...])
    out_ref[...] = dot3(basis, basis, NT)


def potential_of(basis):
    vmem = pl.BlockSpec(memory_space=pltpu.VMEM)
    return pl.pallas_call(
        potential_kernel,
        out_shape=jax.ShapeDtypeStruct((basis.shape[0],) * 2, F32),
        in_specs=[vmem],
        out_specs=vmem,
        compiler_params=pltpu.CompilerParams(vmem_limit_bytes=VMEM_BYTES),
        name="potential",
    )(basis)


def pieces(refs):
    element, quarter = lax.axis_index("elem"), quarter_index()
    for k, ref in enumerate(refs):
        for j in range(ref.shape[0]):
            yield element ^ k, (j if k == 0 else quarter ^ j), ref, j


def factor_kernel(count, shift_ref, *rest):
    refs, rest = rest[:count], rest[count:]
    potential_ref, inverse_ref, link_ref, extra_ref, diag_scr, coupling_ref, pack_scr = rest[:7]
    matrix_scr, inverse_scr = rest[7:]
    size = potential_ref.shape[0]
    parts = refs[0].shape[0]
    part = size // parts
    half = part // 2
    middle = count // 2
    identity = eye_of(size)
    potential = potential_ref[...]
    for element, index, ref, j in pieces(refs):
        start = pl.multiple_of(index * half, 8)
        pack_scr[element, pl.ds(start, half), :] = ref[j, :half]
        start = pl.multiple_of(index * part, 8)
        coupling_ref[element, pl.ds(start, part), :] = ref[j, half : half + part]
        if j == 0:
            extra_ref[element] = ref[j, half + part :]
    for n in range(count):
        diag_scr[n] = (
            unpack_symmetric(pack_scr[n])
            + (extra_ref[n, 0:1] + shift_ref[0]) * identity
            + extra_ref[n, 1:2, :1] * potential
        )

    def eliminate(invert):
        worst = jnp.zeros((1, 1), F32)
        forward = diag_scr[0]
        backward = diag_scr[count - 1]

        def finish(n, matrix, worst):
            inverse, size_left = invert(matrix, identity, 2 if n == middle else 1)
            parts = split(inverse)
            inverse_ref[0, n] = parts[0]
            inverse_ref[1, n] = parts[1]
            return parts, jnp.maximum(worst, size_left)

        def keep(n, link):
            parts = split(link)
            link_ref[0, n] = parts[0]
            link_ref[1, n] = parts[1]
            return parts

        meeting = diag_scr[middle]
        for step in range(max(middle, count - 1 - middle)):
            ahead, behind = step, count - 1 - step
            if ahead < middle:
                parts, worst = finish(ahead, forward, worst)
                coupling = split(-(identity + coupling_ref[ahead + 1]))
                link = keep(ahead + 1, dot3(coupling, parts))
                update = dot3(link, coupling, NT)
                if ahead + 1 < middle:
                    forward = diag_scr[ahead + 1] - update
                else:
                    meeting = meeting - update
            if behind > middle:
                parts, worst = finish(behind, backward, worst)
                raw = -(identity + coupling_ref[behind])
                link = keep(behind, dot3(split(raw.T), parts))
                update = dot3(link, split(raw))
                if behind - 1 > middle:
                    backward = diag_scr[behind - 1] - update
                else:
                    meeting = meeting - update
        _, worst = finish(middle, meeting, worst)
        return worst

    worst = jnp.max(eliminate(fast_inverse))

    @pl.when(jnp.logical_not(worst <= RESIDUAL_BOUND))
    def _():
        eliminate(
            functools.partial(slow_inverse, matrix_scr=matrix_scr, inverse_scr=inverse_scr)
        )


def factorize(shift, payloads, potential):
    count, size = len(payloads), potential.shape[0]
    smem = pl.BlockSpec(memory_space=pltpu.SMEM)
    vmem = pl.BlockSpec(memory_space=pltpu.VMEM)
    half = jax.ShapeDtypeStruct((2, count, size, size), BF16)
    return pl.pallas_call(
        functools.partial(factor_kernel, count),
        out_shape=(half, half, jax.ShapeDtypeStruct((count, 8, size), F32)),
        in_specs=[smem] + [vmem] * (count + 1),
        out_specs=(vmem, vmem, vmem),
        scratch_shapes=[
            pltpu.VMEM((count, size, size), F32),
            pltpu.VMEM((count, size, size), F32),
            pltpu.VMEM((count, size // 2, size), F32),
            pltpu.VMEM((size, size), F32),
            pltpu.VMEM((size, size), F32),
        ],
        compiler_params=pltpu.CompilerParams(vmem_limit_bytes=VMEM_BYTES),
        name="factorize",
    )(shift, *payloads, potential)


def load_factors(inverse_ref, link_ref):
    count = inverse_ref.shape[1]
    inverses = [(inverse_ref[0, n], inverse_ref[1, n]) for n in range(count)]
    links = [(link_ref[0, n], link_ref[1, n]) if n != 0 else None for n in range(count)]
    return inverses, links


def solve_blocks(blocks, inverses, links):
    count = len(blocks)
    middle = count // 2
    reduced = list(blocks)
    for n in range(1, middle + 1):
        reduced[n] = reduced[n] - dot3(split(reduced[n - 1]), links[n], NT)
    for n in range(count - 1, middle, -1):
        reduced[n - 1] = reduced[n - 1] - dot3(split(reduced[n]), links[n], NT)
    solved = [dot3(split(reduced[n]), inverses[n]) for n in range(count)]
    for n in range(middle, 0, -1):
        solved[n - 1] = solved[n - 1] - dot3(split(solved[n]), links[n])
    for n in range(middle + 1, count):
        solved[n] = solved[n] - dot3(split(solved[n - 1]), links[n])
    return solved


def wave_kernel(count, inverse_ref, link_ref, *rest):
    source_refs, rest = rest[:count], rest[count:]
    wave_ref, turned_ref, all_ref, own_scr = rest
    me = lax.axis_index("elem")
    for n in range(count):
        own_scr[me ^ n] = source_refs[n][...]
    inverses, links = load_factors(inverse_ref, link_ref)
    wave = solve_blocks([own_scr[n].T for n in range(count)], inverses, links)
    for n in range(count):
        turned_ref[n] = wave[n]
        all_ref[n] = wave[n].T
    wave_ref[...] = all_ref[me]


def solve_waves(inverses, links, sources):
    count = len(sources)
    channels, width = sources[0].shape
    vmem = pl.BlockSpec(memory_space=pltpu.VMEM)
    return pl.pallas_call(
        functools.partial(wave_kernel, count),
        out_shape=(
            jax.ShapeDtypeStruct((channels, width), F32),
            jax.ShapeDtypeStruct((count, width, channels), F32),
            jax.ShapeDtypeStruct((count, channels, width), F32),
        ),
        in_specs=[vmem] * (2 + count),
        out_specs=(vmem,) * 3,
        scratch_shapes=[pltpu.VMEM((count, channels, width), F32)],
        compiler_params=pltpu.CompilerParams(vmem_limit_bytes=VMEM_BYTES),
        name="waves",
    )(inverses, links, *sources)


def adjoint_kernel(
    open_ref, inverse_ref, link_ref, extra_ref, target_ref, own_ref, others_ref, turned_ref,
    all_ref, adjoint_ref, share_ref, gram_ref, own_scr, k_scr, projector_scr,
):
    count, width, channels = turned_ref.shape
    me, column = lax.axis_index("elem"), lax.axis_index("rhs")
    projector_scr[me] = own_ref[0]
    parts, sets, part = others_ref.shape[:3]
    for j in range(parts):
        start = pl.multiple_of((quarter_index() ^ j) * part, 8)
        for k in range(sets):
            projector_scr[me ^ (k + 1), pl.ds(start, part), :] = others_ref[j, k]
    inverses, links = load_factors(inverse_ref, link_ref)
    projectors = [split(projector_scr[n]) for n in range(count)]
    weights = [extra_ref[n, 1:2, :1] for n in range(count)]
    wave = [turned_ref[n] for n in range(count)]
    k_total = dot3(split(wave[0]), projectors[0])
    for n in range(1, count):
        k_total = k_total + dot3(split(wave[n]), projectors[n])
    k_rows = lax.broadcasted_iota(jnp.int32, k_total.shape, 1)
    k_columns = lax.broadcasted_iota(jnp.int32, k_total.shape, 0) + column * width
    opened = (k_rows < open_ref[0]) & (k_columns < open_ref[0])
    residual = split(jnp.where(opened, k_total - target_ref[...].T, 0.0))
    drive = [PENALTY * wave[n] + dot3(residual, projectors[n], NT) for n in range(count)]
    adjoint = [value.T for value in solve_blocks(drive, inverses, links)]

    share = share_ref.shape[0]
    k_scr[...] = k_total.T
    share_ref[...] = k_scr[pl.ds(pl.multiple_of(me * share, share), share), :]
    for n in range(count):
        own_scr[n] = adjoint[n]
    adjoint_ref[...] = own_scr[me]
    weighted = jnp.concatenate([weights[n] * all_ref[n] for n in range(count)], axis=1)
    gram = dot3(split(jnp.concatenate(adjoint, axis=1)), split(weighted), NT)
    gram = gram + gram.T
    half = channels // 2
    gram_ref[:half] = pack_symmetric(gram)
    gram_ref[half:] = jnp.broadcast_to(diagonal_of(gram), (8, channels))


def solve_adjoints(opened, inverses, links, extras, target, projector, others, turned, waves):
    count, channels, width = waves.shape
    rows = target.shape[0]
    smem = pl.BlockSpec(memory_space=pltpu.SMEM)
    vmem = pl.BlockSpec(memory_space=pltpu.VMEM)
    return pl.pallas_call(
        adjoint_kernel,
        out_shape=(
            jax.ShapeDtypeStruct((channels, width), F32),
            jax.ShapeDtypeStruct((rows // count, width), F32),
            jax.ShapeDtypeStruct((channels // 2 + 8, channels), F32),
        ),
        in_specs=[smem] + [vmem] * 8,
        out_specs=(vmem,) * 3,
        scratch_shapes=[
            pltpu.VMEM((count, channels, width), F32),
            pltpu.VMEM((rows, width), F32),
            pltpu.VMEM((count, channels, channels), F32),
        ],
        compiler_params=pltpu.CompilerParams(vmem_limit_bytes=VMEM_BYTES),
        name="adjoints",
    )(opened, inverses, links, extras, target, projector, others, turned, waves)


def gradient_kernel(scale, own_ref, other_ref, basis_ref, out_ref):
    size = basis_ref.shape[0]
    total = own_ref[...] + other_ref[...]
    gram = unpack_symmetric(total[: size // 2])
    gram = gram + total[size // 2 : size // 2 + 1] * eye_of(size)
    out_ref[...] = scale * dot3(split(gram), split(basis_ref[...]))


def gradient(scale, own, other, basis):
    vmem = pl.BlockSpec(memory_space=pltpu.VMEM)
    return pl.pallas_call(
        functools.partial(gradient_kernel, scale),
        out_shape=jax.ShapeDtypeStruct(basis.shape, F32),
        in_specs=[vmem, vmem, vmem],
        out_specs=vmem,
        compiler_params=pltpu.CompilerParams(vmem_limit_bytes=VMEM_BYTES),
        name="gradient",
    )(own, other, basis)


def swap(value, axis, step):
    count = lax.axis_size(axis)
    return lax.ppermute(value, axis, [(i, i ^ step) for i in range(count)])


def gradient_total(gram, scale, basis):
    steps = []
    for axis in ("rhs", "energy"):
        step = 1
        while step < lax.axis_size(axis):
            steps.append((axis, step))
            step = step * 2
    other = jnp.zeros_like(gram)
    for index, (axis, step) in enumerate(steps):
        if index:
            gram = gram + other
        other = swap(gram, axis, step)
    return gradient(scale, gram, other, basis)


def per_device(
    ham_noise,
    channel_levels,
    coupling_noise,
    corr_weight,
    corr_basis,
    projector,
    energy_shift,
    sources,
    target,
    open_channels,
):
    elements, energies, halves = (lax.axis_size(axis) for axis in ("elem", "energy", "rhs"))
    parts = energies * halves
    own = sources[0, 0]
    raw = (corr_weight, channel_levels, ham_noise, coupling_noise)
    mine, my_projector = pack_part(*raw, projector, parts)
    whole = pack(*raw, parts)
    potential = potential_of(corr_basis)

    def spread(payload):
        for axis in ("energy", "rhs"):
            distance = 1
            while distance < lax.axis_size(axis):
                payload = jnp.concatenate([payload, swap(payload, axis, distance)], axis=0)
                distance = distance * 2
        return payload

    def step_of(found, step):
        low = step & -step
        return swap(found[step ^ low], "elem", low)

    def reach(value, after):
        found = {0: value}
        if after is not None:
            found[0], after[1] = lax.optimization_barrier((value, after[1]))
        for step in range(1, elements):
            found[step] = step_of(found, step)
        return found

    matrix_sets = reach(mine, None)
    matrix_sets[1], whole, potential = lax.optimization_barrier(
        (matrix_sets[1], whole, potential)
    )
    projector_sets = reach(my_projector, matrix_sets)
    source_sets = reach(own, projector_sets)
    payloads = [whole] + [spread(matrix_sets[step][None]) for step in range(1, elements)]
    direct = [step for step in range(1, elements) if step & (step - 1) == 0]
    payloads[-1], *held = lax.optimization_barrier(
        (payloads[-1], *[source_sets[step] for step in direct])
    )
    source_sets.update(zip(direct, held))
    inverses, links, extras = factorize(energy_shift, payloads, potential)
    others = jnp.stack([projector_sets[step] for step in range(1, elements)])[None]
    distance = 1
    while distance < energies:
        received = swap(others, "energy", distance)
        if 2 * distance >= energies:
            received, inverses, source_sets[elements - 1] = lax.optimization_barrier(
                (received, inverses, source_sets[elements - 1])
            )
        others = jnp.concatenate([others, received], axis=0)
        distance = distance * 2
    distance = 1
    while distance < halves:
        others = jnp.concatenate([others, swap(others, "rhs", distance)], axis=0)
        distance = distance * 2
    source_all = [source_sets[step] for step in range(elements)]
    wave, turned, waves = solve_waves(inverses, links, source_all)
    adjoint, share, gram = solve_adjoints(
        open_channels, inverses, links, extras, target[0], projector, others, turned, waves
    )
    basis_grad = gradient_total(gram, -1.0 / (energies * elements), corr_basis)
    return wave[None, None], adjoint[None, None], share[None], basis_grad


def solution(mesh):
    return jax.shard_map(
        per_device,
        mesh=mesh,
        in_specs=(
            P(("groups", "elem"), None, None),
            P(("groups", "elem"), None),
            P(("groups", "elem"), None, None),
            P(("groups", "elem")),
            P("groups", None),
            P(("groups", "elem"), None, None),
            P(("groups", "energy")),
            P(("groups", "energy"), "elem", None, "rhs"),
            P(("groups", "energy"), None, "rhs"),
            P(("groups", "energy")),
        ),
        out_specs=(
            P(("groups", "energy"), "elem", None, "rhs"),
            P(("groups", "energy"), "elem", None, "rhs"),
            P(("groups", "energy"), "elem", "rhs"),
            P("groups", None),
        ),
        check_vma=False,
    )
```

```python
import functools

import jax
import jax.numpy as jnp
from jax import lax
from jax.experimental import pallas as pl
from jax.experimental.pallas import tpu as pltpu
from jax.sharding import PartitionSpec as P

PENALTY = 0.5
START_SCALE = 0.95
SLOW_SCALE = 1.75
RESIDUAL_BOUND = 0.01
F32 = jnp.float32
BF16 = jnp.bfloat16
NN = (((1,), (0,)), ((), ()))
NT = (((1,), (1,)), ((), ()))
VMEM_BYTES = 48 * 1024 * 1024
PACK_BYTES = 60 * 1024 * 1024


def split(value):
    high = value.astype(BF16)
    return high, (value - high.astype(F32)).astype(BF16)


def dot1(lhs, rhs, dims=NN):
    return lax.dot_general(lhs, rhs, dims, preferred_element_type=F32)


def dot3(lhs, rhs, dims=NN):
    return (
        dot1(lhs[0], rhs[0], dims) + dot1(lhs[0], rhs[1], dims) + dot1(lhs[1], rhs[0], dims)
    )


def eye_of(size):
    rows = lax.broadcasted_iota(jnp.int32, (size, size), 0)
    columns = lax.broadcasted_iota(jnp.int32, (size, size), 1)
    return (rows == columns).astype(F32)


def row_norm(matrix):
    return jnp.max(jnp.sum(jnp.abs(matrix), axis=1, keepdims=True), axis=0, keepdims=True)


def fast_inverse(matrix, identity, steps):
    diagonal = matrix * identity
    by_row = START_SCALE / jnp.sum(diagonal, axis=1, keepdims=True)
    by_column = START_SCALE / jnp.sum(diagonal, axis=0, keepdims=True)
    error = identity - by_row * matrix
    inverse = (identity + error) * by_column
    error16 = error.astype(BF16)
    for _ in range(steps):
        error16 = dot1(error16, error16).astype(BF16)
        inverse = inverse + dot1(error16, inverse.astype(BF16))
    parts = split(inverse)
    residual = identity - dot3(split(matrix), parts)
    inverse = inverse + dot1(parts[0], residual.astype(BF16))
    return inverse, row_norm(residual)


def exact_dot(lhs, rhs):
    return lax.dot_general(
        lhs, rhs, NN, precision=lax.Precision.HIGHEST, preferred_element_type=F32
    )


def slow_inverse(matrix, identity, steps, matrix_scr, inverse_scr):
    matrix_scr[...] = matrix
    inverse_scr[...] = identity * (SLOW_SCALE / row_norm(matrix))

    def going(state):
        count, size = state
        return (size > 1e-3) & (count < 100)

    def step(state):
        count, _ = state
        inverse = inverse_scr[...]
        residual = identity - exact_dot(matrix_scr[...], inverse)
        inverse_scr[...] = inverse + exact_dot(inverse, residual)
        return count + 1, jnp.max(row_norm(residual))

    lax.while_loop(going, step, (jnp.int32(0), jnp.float32(1e9)))
    return inverse_scr[...], jnp.zeros((1, 1), F32)


def pack_symmetric(matrix):
    half = matrix.shape[0] // 2
    rows = lax.broadcasted_iota(jnp.int32, (half, half), 0)
    columns = lax.broadcasted_iota(jnp.int32, (half, half), 1)
    first, second = matrix[:half, :half], matrix[half:, half:]
    mixed = jnp.where(rows > columns, first, jnp.where(rows < columns, second, 0.0))
    return jnp.concatenate([matrix[half:, :half], mixed], axis=1)


def unpack_symmetric(packed):
    half = packed.shape[0]
    rows = lax.broadcasted_iota(jnp.int32, (half, half), 0)
    columns = lax.broadcasted_iota(jnp.int32, (half, half), 1)
    corner, mixed = packed[:, :half], packed[:, half:]
    first = jnp.where(rows > columns, mixed, 0.0)
    second = jnp.where(rows < columns, mixed, 0.0)
    return jnp.concatenate(
        [
            jnp.concatenate([first + first.T, corner.T], axis=1),
            jnp.concatenate([corner, second + second.T], axis=1),
        ],
        axis=0,
    )


def diagonal_of(matrix):
    return jnp.sum(matrix * eye_of(matrix.shape[0]), axis=0, keepdims=True)


def extra_rows(ham, level, weight):
    row = lax.broadcasted_iota(jnp.int32, (8, ham.shape[1]), 0)
    return jnp.where(row == 0, diagonal_of(ham) + level + 2.0, weight)


def quarter_index():
    return lax.axis_index("rhs") * lax.axis_size("energy") + lax.axis_index("energy")


def pack_part_kernel(
    weight_ref, level_hbm, ham_hbm, coupling_hbm, projector_hbm, out_ref, ham_ref, pack_scr,
    level_ref, sems,
):
    part = (out_ref.shape[0] - 8) * 2 // 5
    half = part // 2
    index = quarter_index()
    rows = pl.ds(pl.multiple_of(index * part, 8), part)
    copies = [
        pltpu.make_async_copy(source, target, sems.at[number])
        for number, (source, target) in enumerate(
            (
                (ham_hbm.at[0], ham_ref),
                (level_hbm, level_ref),
                (coupling_hbm.at[0, rows], out_ref.at[half : half + part]),
                (projector_hbm.at[0, rows], out_ref.at[half + part : half + 2 * part]),
            )
        )
    ]
    for copy in copies:
        copy.start()
    copies[0].wait()
    copies[1].wait()
    ham = 0.5 * (ham_ref[...] + ham_ref[...].T)
    pack_scr[...] = pack_symmetric(ham)
    out_ref[:half] = pack_scr[pl.ds(pl.multiple_of(index * half, 8), half), :]
    out_ref[half + 2 * part :] = extra_rows(ham, level_ref[...], weight_ref[0])
    copies[2].wait()
    copies[3].wait()


def pack_part(weight, level, ham, coupling, projector, parts):
    size = ham.shape[1]
    part = size // parts
    smem = pl.BlockSpec(memory_space=pltpu.SMEM)
    vmem = pl.BlockSpec(memory_space=pltpu.VMEM)
    anywhere = pl.BlockSpec(memory_space=pl.ANY)
    height = part // 2 + 2 * part + 8
    return pl.pallas_call(
        pack_part_kernel,
        out_shape=jax.ShapeDtypeStruct((height, size), F32),
        in_specs=[smem] + [anywhere] * 4,
        out_specs=vmem,
        scratch_shapes=[
            pltpu.VMEM((size, size), F32),
            pltpu.VMEM((size // 2, size), F32),
            pltpu.VMEM((1, size), F32),
            pltpu.SemaphoreType.DMA((4,)),
        ],
        compiler_params=pltpu.CompilerParams(vmem_limit_bytes=PACK_BYTES),
        name="pack_part",
    )(weight, level, ham, coupling, projector)


def pack_kernel(weight_ref, level_ref, ham_ref, coupling_ref, projector_ref, whole_ref):
    parts = whole_ref.shape[0]
    size = ham_ref.shape[1]
    part = size // parts
    half = part // 2
    ham = 0.5 * (ham_ref[0] + ham_ref[0].T)
    packed = pack_symmetric(ham)
    extra = extra_rows(ham, level_ref[...], weight_ref[0])
    for n in range(parts):
        rows = slice(n * part, (n + 1) * part)
        whole_ref[n, :half] = packed[n * half : (n + 1) * half]
        whole_ref[n, half : half + part] = coupling_ref[0, rows]
        whole_ref[n, half + part : half + 2 * part] = projector_ref[0, rows]
        whole_ref[n, half + 2 * part :] = extra


def pack(weight, level, ham, coupling, projector, parts):
    size = ham.shape[1]
    part = size // parts
    smem = pl.BlockSpec(memory_space=pltpu.SMEM)
    vmem = pl.BlockSpec(memory_space=pltpu.VMEM)
    return pl.pallas_call(
        pack_kernel,
        out_shape=jax.ShapeDtypeStruct((parts, part // 2 + 2 * part + 8, size), F32),
        in_specs=[smem] + [vmem] * 4,
        out_specs=vmem,
        compiler_params=pltpu.CompilerParams(vmem_limit_bytes=VMEM_BYTES),
        name="pack",
    )(weight, level, ham, coupling, projector)


def potential_kernel(basis_ref, out_ref):
    basis = split(basis_ref[...])
    out_ref[...] = dot3(basis, basis, NT)


def potential_of(basis):
    vmem = pl.BlockSpec(memory_space=pltpu.VMEM)
    return pl.pallas_call(
        potential_kernel,
        out_shape=jax.ShapeDtypeStruct((basis.shape[0],) * 2, F32),
        in_specs=[vmem],
        out_specs=vmem,
        compiler_params=pltpu.CompilerParams(vmem_limit_bytes=VMEM_BYTES),
        name="potential",
    )(basis)


def pieces(refs):
    element, quarter = lax.axis_index("elem"), quarter_index()
    for j in range(refs[0].shape[1]):
        yield element, j, refs[0].at[0, j]
        step = 1
        for ref in refs[1:]:
            for k in range(ref.shape[0]):
                yield element ^ (step + k), quarter ^ j, ref.at[k, j]
            step = step + ref.shape[0]


def factor_kernel(groups, shift_ref, potential_ref, *rest):
    refs, rest = rest[:groups], rest[groups:]
    inverse_ref, link_ref, extra_ref, diag_scr, coupling_ref, pack_scr, *scratch = rest
    matrix_scr, inverse_scr = scratch
    count = extra_ref.shape[0]
    size = potential_ref.shape[0]
    part = size // refs[0].shape[1]
    half = part // 2
    middle = count // 2
    identity = eye_of(size)
    potential = potential_ref[...]
    for element, index, ref in pieces(refs):
        start = pl.multiple_of(index * half, 8)
        pack_scr[element, pl.ds(start, half), :] = ref[:half]
        start = pl.multiple_of(index * part, 8)
        coupling_ref[element, pl.ds(start, part), :] = ref[half : half + part]
        extra_ref[element] = ref[half + 2 * part :]
    for n in range(count):
        diag_scr[n] = (
            unpack_symmetric(pack_scr[n])
            + (extra_ref[n, 0:1] + shift_ref[0]) * identity
            + extra_ref[n, 1:2, :1] * potential
        )

    def eliminate(invert):
        worst = jnp.zeros((1, 1), F32)
        forward = diag_scr[0]
        backward = diag_scr[count - 1]

        def finish(n, matrix, worst):
            inverse, size_left = invert(matrix, identity, 2 if n == middle else 1)
            parts = split(inverse)
            inverse_ref[0, n] = parts[0]
            inverse_ref[1, n] = parts[1]
            return parts, jnp.maximum(worst, size_left)

        def keep(n, link):
            parts = split(link)
            link_ref[0, n] = parts[0]
            link_ref[1, n] = parts[1]
            return parts

        meeting = diag_scr[middle]
        for step in range(max(middle, count - 1 - middle)):
            ahead, behind = step, count - 1 - step
            if ahead < middle:
                parts, worst = finish(ahead, forward, worst)
                coupling = split(-(identity + coupling_ref[ahead + 1]))
                link = keep(ahead + 1, dot3(coupling, parts))
                update = dot3(link, coupling, NT)
                if ahead + 1 < middle:
                    forward = diag_scr[ahead + 1] - update
                else:
                    meeting = meeting - update
            if behind > middle:
                parts, worst = finish(behind, backward, worst)
                raw = -(identity + coupling_ref[behind])
                link = keep(behind, dot3(split(raw.T), parts))
                update = dot3(link, split(raw))
                if behind - 1 > middle:
                    backward = diag_scr[behind - 1] - update
                else:
                    meeting = meeting - update
        _, worst = finish(middle, meeting, worst)
        return worst

    worst = jnp.max(eliminate(fast_inverse))

    @pl.when(jnp.logical_not(worst <= RESIDUAL_BOUND))
    def _():
        eliminate(
            functools.partial(slow_inverse, matrix_scr=matrix_scr, inverse_scr=inverse_scr)
        )


def factorize(shift, potential, payloads):
    count, size = sum(value.shape[0] for value in payloads), potential.shape[0]
    smem = pl.BlockSpec(memory_space=pltpu.SMEM)
    vmem = pl.BlockSpec(memory_space=pltpu.VMEM)
    half = jax.ShapeDtypeStruct((2, count, size, size), BF16)
    return pl.pallas_call(
        functools.partial(factor_kernel, len(payloads)),
        out_shape=(half, half, jax.ShapeDtypeStruct((count, 8, size), F32)),
        in_specs=[smem] + [vmem] * (1 + len(payloads)),
        out_specs=(vmem, vmem, vmem),
        scratch_shapes=[
            pltpu.VMEM((count, size, size), F32),
            pltpu.VMEM((count, size, size), F32),
            pltpu.VMEM((count, size // 2, size), F32),
            pltpu.VMEM((size, size), F32),
            pltpu.VMEM((size, size), F32),
        ],
        compiler_params=pltpu.CompilerParams(vmem_limit_bytes=VMEM_BYTES),
        name="factorize",
    )(shift, potential, *payloads)


def load_factors(inverse_ref, link_ref):
    count = inverse_ref.shape[1]
    inverses = [(inverse_ref[0, n], inverse_ref[1, n]) for n in range(count)]
    links = [(link_ref[0, n], link_ref[1, n]) if n != 0 else None for n in range(count)]
    return inverses, links


def solve_blocks(blocks, inverses, links):
    count = len(blocks)
    middle = count // 2
    reduced = list(blocks)
    for n in range(1, middle + 1):
        reduced[n] = reduced[n] - dot3(split(reduced[n - 1]), links[n], NT)
    for n in range(count - 1, middle, -1):
        reduced[n - 1] = reduced[n - 1] - dot3(split(reduced[n]), links[n], NT)
    solved = [dot3(split(reduced[n]), inverses[n]) for n in range(count)]
    for n in range(middle, 0, -1):
        solved[n - 1] = solved[n - 1] - dot3(split(solved[n]), links[n])
    for n in range(middle + 1, count):
        solved[n] = solved[n] - dot3(split(solved[n - 1]), links[n])
    return solved


def solve_kernel(
    groups, open_ref, inverse_ref, link_ref, extra_ref, target_ref, *rest
):
    count = inverse_ref.shape[1]
    refs, source_refs, rest = rest[:groups], rest[groups : groups + count], rest[groups + count :]
    wave_ref, adjoint_ref, share_ref, gram_ref, own_scr, k_scr, projector_scr = rest
    channels, width = source_refs[0].shape
    me, column = lax.axis_index("elem"), lax.axis_index("rhs")
    part = channels // refs[0].shape[1]
    begin = part // 2 + part
    for element, index, ref in pieces(refs):
        start = pl.multiple_of(index * part, 8)
        projector_scr[element, pl.ds(start, part), :] = ref[begin : begin + part]
    for n in range(count):
        own_scr[me ^ n] = source_refs[n][...]
    inverses, links = load_factors(inverse_ref, link_ref)
    projectors = [split(projector_scr[n]) for n in range(count)]
    wave = solve_blocks([own_scr[n].T for n in range(count)], inverses, links)
    k_total = dot3(split(wave[0]), projectors[0])
    for n in range(1, count):
        k_total = k_total + dot3(split(wave[n]), projectors[n])
    k_rows = lax.broadcasted_iota(jnp.int32, k_total.shape, 1)
    k_columns = lax.broadcasted_iota(jnp.int32, k_total.shape, 0) + column * width
    opened = (k_rows < open_ref[0]) & (k_columns < open_ref[0])
    residual = split(jnp.where(opened, k_total - target_ref[...].T, 0.0))
    drive = [PENALTY * wave[n] + dot3(residual, projectors[n], NT) for n in range(count)]
    adjoint = [value.T for value in solve_blocks(drive, inverses, links)]
    wave = [value.T for value in wave]

    share = share_ref.shape[0]
    k_scr[...] = k_total.T
    share_ref[...] = k_scr[pl.ds(pl.multiple_of(me * share, share), share), :]
    for n in range(count):
        own_scr[n] = wave[n]
    wave_ref[...] = own_scr[me]
    for n in range(count):
        own_scr[n] = adjoint[n]
    adjoint_ref[...] = own_scr[me]
    weighted = [extra_ref[n, 1:2, :1] * wave[n] for n in range(count)]
    weighted = split(jnp.concatenate(weighted, axis=1))
    gram = dot3(split(jnp.concatenate(adjoint, axis=1)), weighted, NT)
    gram = gram + gram.T
    half = channels // 2
    gram_ref[:half] = pack_symmetric(gram)
    gram_ref[half:] = jnp.broadcast_to(diagonal_of(gram), (8, channels))


def solve_all(opened, inverses, links, extras, target, payloads, sources):
    count = len(sources)
    channels, width = sources[0].shape
    rows = target.shape[0]
    smem = pl.BlockSpec(memory_space=pltpu.SMEM)
    vmem = pl.BlockSpec(memory_space=pltpu.VMEM)
    return pl.pallas_call(
        functools.partial(solve_kernel, len(payloads)),
        out_shape=(
            jax.ShapeDtypeStruct((channels, width), F32),
            jax.ShapeDtypeStruct((channels, width), F32),
            jax.ShapeDtypeStruct((rows // count, width), F32),
            jax.ShapeDtypeStruct((channels // 2 + 8, channels), F32),
        ),
        in_specs=[smem] + [vmem] * (4 + len(payloads) + count),
        out_specs=(vmem,) * 4,
        scratch_shapes=[
            pltpu.VMEM((count, channels, width), F32),
            pltpu.VMEM((rows, width), F32),
            pltpu.VMEM((count, channels, channels), F32),
        ],
        compiler_params=pltpu.CompilerParams(vmem_limit_bytes=VMEM_BYTES),
        name="solve",
    )(opened, inverses, links, extras, target, *payloads, *sources)


def gradient_kernel(scale, own_ref, other_ref, basis_ref, out_ref):
    size = basis_ref.shape[0]
    total = own_ref[...] + other_ref[...]
    gram = unpack_symmetric(total[: size // 2])
    gram = gram + total[size // 2 : size // 2 + 1] * eye_of(size)
    out_ref[...] = scale * dot3(split(gram), split(basis_ref[...]))


def gradient(scale, own, other, basis):
    vmem = pl.BlockSpec(memory_space=pltpu.VMEM)
    return pl.pallas_call(
        functools.partial(gradient_kernel, scale),
        out_shape=jax.ShapeDtypeStruct(basis.shape, F32),
        in_specs=[vmem, vmem, vmem],
        out_specs=vmem,
        compiler_params=pltpu.CompilerParams(vmem_limit_bytes=VMEM_BYTES),
        name="gradient",
    )(own, other, basis)


def swap(value, axis, step):
    count = lax.axis_size(axis)
    return lax.ppermute(value, axis, [(i, i ^ step) for i in range(count)])


def gradient_total(gram, scale, basis):
    steps = []
    for axis in ("rhs", "energy"):
        step = 1
        while step < lax.axis_size(axis):
            steps.append((axis, step))
            step = step * 2
    other = jnp.zeros_like(gram)
    for index, (axis, step) in enumerate(steps):
        if index:
            gram = gram + other
        other = swap(gram, axis, step)
    return gradient(scale, gram, other, basis)


def per_device(
    ham_noise,
    channel_levels,
    coupling_noise,
    corr_weight,
    corr_basis,
    projector,
    energy_shift,
    sources,
    target,
    open_channels,
):
    elements, energies, halves = (lax.axis_size(axis) for axis in ("elem", "energy", "rhs"))
    parts = energies * halves
    raw = (corr_weight, channel_levels, ham_noise, coupling_noise, projector)
    mine = pack_part(*raw, parts)
    whole = pack(*raw, parts)
    potential = potential_of(corr_basis)

    def reach(found, step):
        low = step & -step
        return swap(found[step ^ low], "elem", low)

    def spread(payload, axis):
        distance = 1
        while distance < lax.axis_size(axis):
            payload = jnp.concatenate([payload, swap(payload, axis, distance)], axis=1)
            distance = distance * 2
        return payload

    steps = range(1, elements)
    near = {0: mine}
    for step in steps:
        near[step] = reach(near, step)
    near[1], whole, potential = lax.optimization_barrier((near[1], whole, potential))
    far = elements // 2
    own, near[far] = lax.optimization_barrier((sources[0, 0], near[far]))
    source_sets = {0: own}
    for step in steps:
        source_sets[step] = reach(source_sets, step)
    sets = [spread(near[step][None, None], "energy") for step in steps]
    sets[0], source_sets[far] = lax.optimization_barrier((sets[0], source_sets[far]))
    groups = [sets[:-1], sets[-1:]] if len(sets) > 1 else [sets]
    payloads = [spread(jnp.concatenate(group, axis=0), "rhs") for group in groups]
    direct = [step for step in steps if step & (step - 1) == 0]
    payloads[-1], *held = lax.optimization_barrier(
        (payloads[-1], *[source_sets[step] for step in direct])
    )
    source_sets.update(zip(direct, held))
    payloads = [whole[None], *payloads]
    inverses, links, extras = factorize(energy_shift, potential, payloads)
    source_all = [source_sets[step] for step in range(elements)]
    wave, adjoint, share, gram = solve_all(
        open_channels, inverses, links, extras, target[0], payloads, source_all
    )
    basis_grad = gradient_total(gram, -1.0 / (energies * elements), corr_basis)
    return wave[None, None], adjoint[None, None], share[None], basis_grad


def solution(mesh):
    return jax.shard_map(
        per_device,
        mesh=mesh,
        in_specs=(
            P(("groups", "elem"), None, None),
            P(("groups", "elem"), None),
            P(("groups", "elem"), None, None),
            P(("groups", "elem")),
            P("groups", None),
            P(("groups", "elem"), None, None),
            P(("groups", "energy")),
            P(("groups", "energy"), "elem", None, "rhs"),
            P(("groups", "energy"), None, "rhs"),
            P(("groups", "energy")),
        ),
        out_specs=(
            P(("groups", "energy"), "elem", None, "rhs"),
            P(("groups", "energy"), "elem", None, "rhs"),
            P(("groups", "energy"), "elem", "rhs"),
            P("groups", None),
        ),
        check_vma=False,
    )
```

```python
import functools

import jax
import jax.numpy as jnp
from jax import lax
from jax.experimental import pallas as pl
from jax.experimental.pallas import tpu as pltpu
from jax.sharding import PartitionSpec as P

PENALTY = 0.5
START_SCALE = 0.95
SLOW_SCALE = 1.75
RESIDUAL_BOUND = 0.01
F32 = jnp.float32
BF16 = jnp.bfloat16
NN = (((1,), (0,)), ((), ()))
NT = (((1,), (1,)), ((), ()))
VMEM_BYTES = 48 * 1024 * 1024
PACK_BYTES = 60 * 1024 * 1024


def split(value):
    high = value.astype(BF16)
    return high, (value - high.astype(F32)).astype(BF16)


def dot1(lhs, rhs, dims=NN):
    return lax.dot_general(lhs, rhs, dims, preferred_element_type=F32)


def dot3(lhs, rhs, dims=NN):
    return (
        dot1(lhs[0], rhs[0], dims) + dot1(lhs[0], rhs[1], dims) + dot1(lhs[1], rhs[0], dims)
    )


def eye_of(size):
    rows = lax.broadcasted_iota(jnp.int32, (size, size), 0)
    columns = lax.broadcasted_iota(jnp.int32, (size, size), 1)
    return (rows == columns).astype(F32)


def row_norm(matrix):
    return jnp.max(jnp.sum(jnp.abs(matrix), axis=1, keepdims=True), axis=0, keepdims=True)


def fast_inverse(matrix, identity, steps):
    diagonal = matrix * identity
    by_row = START_SCALE / jnp.sum(diagonal, axis=1, keepdims=True)
    by_column = START_SCALE / jnp.sum(diagonal, axis=0, keepdims=True)
    error = identity - by_row * matrix
    inverse = (identity + error) * by_column
    error16 = error.astype(BF16)
    for _ in range(steps):
        error16 = dot1(error16, error16).astype(BF16)
        inverse = inverse + dot1(error16, inverse.astype(BF16))
    parts = split(inverse)
    residual = identity - dot3(split(matrix), parts)
    inverse = inverse + dot1(parts[0], residual.astype(BF16))
    return inverse, row_norm(residual)


def exact_dot(lhs, rhs):
    return lax.dot_general(
        lhs, rhs, NN, precision=lax.Precision.HIGHEST, preferred_element_type=F32
    )


def slow_inverse(matrix, identity, steps, matrix_scr, inverse_scr):
    matrix_scr[...] = matrix
    inverse_scr[...] = identity * (SLOW_SCALE / row_norm(matrix))

    def going(state):
        count, size = state
        return (size > 1e-3) & (count < 100)

    def step(state):
        count, _ = state
        inverse = inverse_scr[...]
        residual = identity - exact_dot(matrix_scr[...], inverse)
        inverse_scr[...] = inverse + exact_dot(inverse, residual)
        return count + 1, jnp.max(row_norm(residual))

    lax.while_loop(going, step, (jnp.int32(0), jnp.float32(1e9)))
    return inverse_scr[...], jnp.zeros((1, 1), F32)


def pack_symmetric(matrix):
    half = matrix.shape[0] // 2
    rows = lax.broadcasted_iota(jnp.int32, (half, half), 0)
    columns = lax.broadcasted_iota(jnp.int32, (half, half), 1)
    first, second = matrix[:half, :half], matrix[half:, half:]
    mixed = jnp.where(rows > columns, first, jnp.where(rows < columns, second, 0.0))
    return jnp.concatenate([matrix[half:, :half], mixed], axis=1)


def unpack_symmetric(packed):
    half = packed.shape[0]
    rows = lax.broadcasted_iota(jnp.int32, (half, half), 0)
    columns = lax.broadcasted_iota(jnp.int32, (half, half), 1)
    corner, mixed = packed[:, :half], packed[:, half:]
    first = jnp.where(rows > columns, mixed, 0.0)
    second = jnp.where(rows < columns, mixed, 0.0)
    return jnp.concatenate(
        [
            jnp.concatenate([first + first.T, corner.T], axis=1),
            jnp.concatenate([corner, second + second.T], axis=1),
        ],
        axis=0,
    )


def diagonal_of(matrix):
    return jnp.sum(matrix * eye_of(matrix.shape[0]), axis=0, keepdims=True)


def extra_rows(ham, level, weight):
    row = lax.broadcasted_iota(jnp.int32, (8, ham.shape[1]), 0)
    return jnp.where(row == 0, diagonal_of(ham) + level + 2.0, weight)


def quarter_index():
    return lax.axis_index("rhs") * lax.axis_size("energy") + lax.axis_index("energy")


def pack_part_kernel(
    weight_ref, level_hbm, ham_hbm, coupling_hbm, projector_hbm, out_ref, ham_ref, pack_scr,
    level_ref, sems,
):
    part = (out_ref.shape[0] - 8) * 2 // 5
    half = part // 2
    index = quarter_index()
    rows = pl.ds(pl.multiple_of(index * part, 8), part)
    copies = [
        pltpu.make_async_copy(source, target, sems.at[number])
        for number, (source, target) in enumerate(
            (
                (ham_hbm.at[0], ham_ref),
                (level_hbm, level_ref),
                (coupling_hbm.at[0, rows], out_ref.at[half : half + part]),
                (projector_hbm.at[0, rows], out_ref.at[half + part : half + 2 * part]),
            )
        )
    ]
    for copy in copies:
        copy.start()
    copies[0].wait()
    copies[1].wait()
    ham = 0.5 * (ham_ref[...] + ham_ref[...].T)
    pack_scr[...] = pack_symmetric(ham)
    out_ref[:half] = pack_scr[pl.ds(pl.multiple_of(index * half, 8), half), :]
    out_ref[half + 2 * part :] = extra_rows(ham, level_ref[...], weight_ref[0])
    copies[2].wait()
    copies[3].wait()


def pack_part(weight, level, ham, coupling, projector, parts):
    size = ham.shape[1]
    part = size // parts
    smem = pl.BlockSpec(memory_space=pltpu.SMEM)
    vmem = pl.BlockSpec(memory_space=pltpu.VMEM)
    anywhere = pl.BlockSpec(memory_space=pl.ANY)
    height = part // 2 + 2 * part + 8
    return pl.pallas_call(
        pack_part_kernel,
        out_shape=jax.ShapeDtypeStruct((height, size), F32),
        in_specs=[smem] + [anywhere] * 4,
        out_specs=vmem,
        scratch_shapes=[
            pltpu.VMEM((size, size), F32),
            pltpu.VMEM((size // 2, size), F32),
            pltpu.VMEM((1, size), F32),
            pltpu.SemaphoreType.DMA((4,)),
        ],
        compiler_params=pltpu.CompilerParams(vmem_limit_bytes=PACK_BYTES),
        name="pack_part",
    )(weight, level, ham, coupling, projector)


def pack_kernel(weight_ref, level_ref, ham_ref, coupling_ref, projector_ref, whole_ref):
    parts = whole_ref.shape[0]
    size = ham_ref.shape[1]
    part = size // parts
    half = part // 2
    ham = 0.5 * (ham_ref[0] + ham_ref[0].T)
    packed = pack_symmetric(ham)
    extra = extra_rows(ham, level_ref[...], weight_ref[0])
    for n in range(parts):
        rows = slice(n * part, (n + 1) * part)
        whole_ref[n, :half] = packed[n * half : (n + 1) * half]
        whole_ref[n, half : half + part] = coupling_ref[0, rows]
        whole_ref[n, half + part : half + 2 * part] = projector_ref[0, rows]
        whole_ref[n, half + 2 * part :] = extra


def pack(weight, level, ham, coupling, projector, parts):
    size = ham.shape[1]
    part = size // parts
    smem = pl.BlockSpec(memory_space=pltpu.SMEM)
    vmem = pl.BlockSpec(memory_space=pltpu.VMEM)
    return pl.pallas_call(
        pack_kernel,
        out_shape=jax.ShapeDtypeStruct((parts, part // 2 + 2 * part + 8, size), F32),
        in_specs=[smem] + [vmem] * 4,
        out_specs=vmem,
        compiler_params=pltpu.CompilerParams(vmem_limit_bytes=VMEM_BYTES),
        name="pack",
    )(weight, level, ham, coupling, projector)


def potential_kernel(basis_ref, out_ref):
    basis = split(basis_ref[...])
    out_ref[...] = dot3(basis, basis, NT)


def potential_of(basis):
    vmem = pl.BlockSpec(memory_space=pltpu.VMEM)
    return pl.pallas_call(
        potential_kernel,
        out_shape=jax.ShapeDtypeStruct((basis.shape[0],) * 2, F32),
        in_specs=[vmem],
        out_specs=vmem,
        compiler_params=pltpu.CompilerParams(vmem_limit_bytes=VMEM_BYTES),
        name="potential",
    )(basis)


def pieces(refs):
    element, quarter = lax.axis_index("elem"), quarter_index()
    for j in range(refs[0].shape[1]):
        yield element, j, refs[0].at[0, j]
        step = 1
        for ref in refs[1:]:
            for k in range(ref.shape[0]):
                yield element ^ (step + k), quarter ^ j, ref.at[k, j]
            step = step + ref.shape[0]


def factor_kernel(groups, shift_ref, potential_ref, *rest):
    refs, rest = rest[:groups], rest[groups:]
    inverse_ref, link_ref, extra_ref, diag_scr, coupling_ref, pack_scr, *scratch = rest
    matrix_scr, inverse_scr = scratch
    count = extra_ref.shape[0]
    size = potential_ref.shape[0]
    part = size // refs[0].shape[1]
    half = part // 2
    middle = count // 2
    identity = eye_of(size)
    potential = potential_ref[...]
    for element, index, ref in pieces(refs):
        start = pl.multiple_of(index * half, 8)
        pack_scr[element, pl.ds(start, half), :] = ref[:half]
        start = pl.multiple_of(index * part, 8)
        coupling_ref[element, pl.ds(start, part), :] = ref[half : half + part]
        extra_ref[element] = ref[half + 2 * part :]
    for n in range(count):
        diag_scr[n] = (
            unpack_symmetric(pack_scr[n])
            + (extra_ref[n, 0:1] + shift_ref[0]) * identity
            + extra_ref[n, 1:2, :1] * potential
        )

    def eliminate(invert):
        worst = jnp.zeros((1, 1), F32)
        forward = diag_scr[0]
        backward = diag_scr[count - 1]

        def finish(n, matrix, worst):
            inverse, size_left = invert(matrix, identity, 2 if n == middle else 1)
            parts = split(inverse)
            inverse_ref[0, n] = parts[0]
            inverse_ref[1, n] = parts[1]
            return parts, jnp.maximum(worst, size_left)

        def keep(n, link):
            parts = split(link)
            link_ref[0, n] = parts[0]
            link_ref[1, n] = parts[1]
            return parts

        meeting = diag_scr[middle]
        for step in range(max(middle, count - 1 - middle)):
            ahead, behind = step, count - 1 - step
            if ahead < middle:
                parts, worst = finish(ahead, forward, worst)
                coupling = split(-(identity + coupling_ref[ahead + 1]))
                link = keep(ahead + 1, dot3(coupling, parts))
                update = dot3(link, coupling, NT)
                if ahead + 1 < middle:
                    forward = diag_scr[ahead + 1] - update
                else:
                    meeting = meeting - update
            if behind > middle:
                parts, worst = finish(behind, backward, worst)
                raw = -(identity + coupling_ref[behind])
                link = keep(behind, dot3(split(raw.T), parts))
                update = dot3(link, split(raw))
                if behind - 1 > middle:
                    backward = diag_scr[behind - 1] - update
                else:
                    meeting = meeting - update
        _, worst = finish(middle, meeting, worst)
        return worst

    worst = jnp.max(eliminate(fast_inverse))

    @pl.when(jnp.logical_not(worst <= RESIDUAL_BOUND))
    def _():
        eliminate(
            functools.partial(slow_inverse, matrix_scr=matrix_scr, inverse_scr=inverse_scr)
        )


def factorize(shift, potential, payloads):
    count, size = sum(value.shape[0] for value in payloads), potential.shape[0]
    smem = pl.BlockSpec(memory_space=pltpu.SMEM)
    vmem = pl.BlockSpec(memory_space=pltpu.VMEM)
    half = jax.ShapeDtypeStruct((2, count, size, size), BF16)
    return pl.pallas_call(
        functools.partial(factor_kernel, len(payloads)),
        out_shape=(half, half, jax.ShapeDtypeStruct((count, 8, size), F32)),
        in_specs=[smem] + [vmem] * (1 + len(payloads)),
        out_specs=(vmem, vmem, vmem),
        scratch_shapes=[
            pltpu.VMEM((count, size, size), F32),
            pltpu.VMEM((count, size, size), F32),
            pltpu.VMEM((count, size // 2, size), F32),
            pltpu.VMEM((size, size), F32),
            pltpu.VMEM((size, size), F32),
        ],
        compiler_params=pltpu.CompilerParams(vmem_limit_bytes=VMEM_BYTES),
        name="factorize",
    )(shift, potential, *payloads)


def load_factors(inverse_ref, link_ref):
    count = inverse_ref.shape[1]
    inverses = [(inverse_ref[0, n], inverse_ref[1, n]) for n in range(count)]
    links = [(link_ref[0, n], link_ref[1, n]) if n != 0 else None for n in range(count)]
    return inverses, links


def solve_blocks(blocks, inverses, links):
    count = len(blocks)
    middle = count // 2
    reduced = list(blocks)
    for n in range(1, middle + 1):
        reduced[n] = reduced[n] - dot3(split(reduced[n - 1]), links[n], NT)
    for n in range(count - 1, middle, -1):
        reduced[n - 1] = reduced[n - 1] - dot3(split(reduced[n]), links[n], NT)
    solved = [dot3(split(reduced[n]), inverses[n]) for n in range(count)]
    for n in range(middle, 0, -1):
        solved[n - 1] = solved[n - 1] - dot3(split(solved[n]), links[n])
    for n in range(middle + 1, count):
        solved[n] = solved[n] - dot3(split(solved[n - 1]), links[n])
    return solved


def solve_kernel(
    groups, open_ref, inverse_ref, link_ref, extra_ref, target_ref, *rest
):
    count = inverse_ref.shape[1]
    refs, rest = rest[:groups], rest[groups:]
    *source_refs, wave_ref, adjoint_ref, share_ref, gram_ref, own_scr, k_scr, projector_scr = rest
    channels, width = source_refs[0].shape[1:]
    me, column = lax.axis_index("elem"), lax.axis_index("rhs")
    part = channels // refs[0].shape[1]
    begin = part // 2 + part
    for element, index, ref in pieces(refs):
        start = pl.multiple_of(index * part, 8)
        projector_scr[element, pl.ds(start, part), :] = ref[begin : begin + part]
    order, distance = [0], count // 2
    while distance:
        order = order + [n ^ distance for n in order]
        distance = distance // 2
    for place, n in enumerate(order):
        half = source_refs[0].shape[0]
        own_scr[me ^ n] = source_refs[place // half][place % half]
    inverses, links = load_factors(inverse_ref, link_ref)
    projectors = [split(projector_scr[n]) for n in range(count)]
    wave = solve_blocks([own_scr[n].T for n in range(count)], inverses, links)
    k_total = dot3(split(wave[0]), projectors[0])
    for n in range(1, count):
        k_total = k_total + dot3(split(wave[n]), projectors[n])
    k_rows = lax.broadcasted_iota(jnp.int32, k_total.shape, 1)
    k_columns = lax.broadcasted_iota(jnp.int32, k_total.shape, 0) + column * width
    opened = (k_rows < open_ref[0]) & (k_columns < open_ref[0])
    residual = split(jnp.where(opened, k_total - target_ref[...].T, 0.0))
    drive = [PENALTY * wave[n] + dot3(residual, projectors[n], NT) for n in range(count)]
    adjoint = [value.T for value in solve_blocks(drive, inverses, links)]
    wave = [value.T for value in wave]

    share = share_ref.shape[0]
    k_scr[...] = k_total.T
    share_ref[...] = k_scr[pl.ds(pl.multiple_of(me * share, share), share), :]
    for n in range(count):
        own_scr[n] = wave[n]
    wave_ref[...] = own_scr[me]
    for n in range(count):
        own_scr[n] = adjoint[n]
    adjoint_ref[...] = own_scr[me]
    weighted = [extra_ref[n, 1:2, :1] * wave[n] for n in range(count)]
    weighted = split(jnp.concatenate(weighted, axis=1))
    gram = dot3(split(jnp.concatenate(adjoint, axis=1)), weighted, NT)
    gram = gram + gram.T
    half = channels // 2
    gram_ref[:half] = pack_symmetric(gram)
    gram_ref[half:] = jnp.broadcast_to(diagonal_of(gram), (8, channels))


def solve_all(opened, inverses, links, extras, target, payloads, sources):
    count, channels, width = inverses.shape[1], *sources[0].shape[1:]
    rows = target.shape[0]
    smem = pl.BlockSpec(memory_space=pltpu.SMEM)
    vmem = pl.BlockSpec(memory_space=pltpu.VMEM)
    return pl.pallas_call(
        functools.partial(solve_kernel, len(payloads)),
        out_shape=(
            jax.ShapeDtypeStruct((channels, width), F32),
            jax.ShapeDtypeStruct((channels, width), F32),
            jax.ShapeDtypeStruct((rows // count, width), F32),
            jax.ShapeDtypeStruct((channels // 2 + 8, channels), F32),
        ),
        in_specs=[smem] + [vmem] * (4 + len(payloads) + len(sources)),
        out_specs=(vmem,) * 4,
        scratch_shapes=[
            pltpu.VMEM((count, channels, width), F32),
            pltpu.VMEM((rows, width), F32),
            pltpu.VMEM((count, channels, channels), F32),
        ],
        compiler_params=pltpu.CompilerParams(vmem_limit_bytes=VMEM_BYTES),
        name="solve",
    )(opened, inverses, links, extras, target, *payloads, *sources)


def gradient_kernel(scale, own_ref, other_ref, basis_ref, out_ref):
    size = basis_ref.shape[0]
    total = own_ref[...] + other_ref[...]
    gram = unpack_symmetric(total[: size // 2])
    gram = gram + total[size // 2 : size // 2 + 1] * eye_of(size)
    out_ref[...] = scale * dot3(split(gram), split(basis_ref[...]))


def gradient(scale, own, other, basis):
    vmem = pl.BlockSpec(memory_space=pltpu.VMEM)
    return pl.pallas_call(
        functools.partial(gradient_kernel, scale),
        out_shape=jax.ShapeDtypeStruct(basis.shape, F32),
        in_specs=[vmem, vmem, vmem],
        out_specs=vmem,
        compiler_params=pltpu.CompilerParams(vmem_limit_bytes=VMEM_BYTES),
        name="gradient",
    )(own, other, basis)


def swap(value, axis, step):
    count = lax.axis_size(axis)
    return lax.ppermute(value, axis, [(i, i ^ step) for i in range(count)])


def gradient_total(gram, scale, basis):
    steps = []
    for axis in ("rhs", "energy"):
        step = 1
        while step < lax.axis_size(axis):
            steps.append((axis, step))
            step = step * 2
    other = jnp.zeros_like(gram)
    for index, (axis, step) in enumerate(steps):
        if index:
            gram = gram + other
        other = swap(gram, axis, step)
    return gradient(scale, gram, other, basis)


def per_device(
    ham_noise,
    channel_levels,
    coupling_noise,
    corr_weight,
    corr_basis,
    projector,
    energy_shift,
    sources,
    target,
    open_channels,
):
    elements, energies, halves = (lax.axis_size(axis) for axis in ("elem", "energy", "rhs"))
    parts = energies * halves
    raw = (corr_weight, channel_levels, ham_noise, coupling_noise, projector)
    mine = pack_part(*raw, parts)
    whole = pack(*raw, parts)
    potential = potential_of(corr_basis)

    def reach(found, step):
        low = step & -step
        return swap(found[step ^ low], "elem", low)

    def spread(payload, axis):
        distance = 1
        while distance < lax.axis_size(axis):
            payload = jnp.concatenate([payload, swap(payload, axis, distance)], axis=1)
            distance = distance * 2
        return payload

    steps = range(1, elements)
    near, far = {0: mine}, elements // 2
    for step in steps:
        near[step] = reach(near, step)
        if step == far:
            near[far], whole, potential = lax.optimization_barrier((near[far], whole, potential))
    own, near[elements - 1] = lax.optimization_barrier((sources[0, 0], near[elements - 1]))
    sets = [spread(near[step][None, None], "energy") for step in steps]
    source_all, distance = [own[None]], far
    while distance:
        source_all = [jnp.concatenate(source_all, axis=0)]
        source_all.append(swap(source_all[0], "elem", distance))
        if distance == far:
            sets[0], source_all[1] = lax.optimization_barrier((sets[0], source_all[1]))
        distance = distance // 2
    groups = [sets[:-1], sets[-1:]] if len(sets) > 1 else [sets]
    payloads = [spread(jnp.concatenate(group, axis=0), "rhs") for group in groups]
    payloads = [whole[None], *payloads]
    inverses, links, extras = factorize(energy_shift, potential, payloads)
    wave, adjoint, share, gram = solve_all(
        open_channels, inverses, links, extras, target[0], payloads, source_all
    )
    basis_grad = gradient_total(gram, -1.0 / (energies * elements), corr_basis)
    return wave[None, None], adjoint[None, None], share[None], basis_grad


def solution(mesh):
    return jax.shard_map(
        per_device,
        mesh=mesh,
        in_specs=(
            P(("groups", "elem"), None, None),
            P(("groups", "elem"), None),
            P(("groups", "elem"), None, None),
            P(("groups", "elem")),
            P("groups", None),
            P(("groups", "elem"), None, None),
            P(("groups", "energy")),
            P(("groups", "energy"), "elem", None, "rhs"),
            P(("groups", "energy"), None, "rhs"),
            P(("groups", "energy")),
        ),
        out_specs=(
            P(("groups", "energy"), "elem", None, "rhs"),
            P(("groups", "energy"), "elem", None, "rhs"),
            P(("groups", "energy"), "elem", "rhs"),
            P("groups", None),
        ),
        check_vma=False,
    )
```

```python
import functools

import jax
import jax.numpy as jnp
from jax import lax
from jax.experimental import pallas as pl
from jax.experimental.pallas import tpu as pltpu
from jax.sharding import PartitionSpec as P

PENALTY = 0.5
START_SCALE = 0.95
SLOW_SCALE = 1.75
RESIDUAL_BOUND = 0.01
F32 = jnp.float32
BF16 = jnp.bfloat16
NN = (((1,), (0,)), ((), ()))
NT = (((1,), (1,)), ((), ()))
VMEM_BYTES = 48 * 1024 * 1024
PACK_BYTES = 60 * 1024 * 1024


def split(value):
    high = value.astype(BF16)
    return high, (value - high.astype(F32)).astype(BF16)


def dot1(lhs, rhs, dims=NN):
    return lax.dot_general(lhs, rhs, dims, preferred_element_type=F32)


def dot3(lhs, rhs, dims=NN):
    return (
        dot1(lhs[0], rhs[0], dims) + dot1(lhs[0], rhs[1], dims) + dot1(lhs[1], rhs[0], dims)
    )


def eye_of(size):
    rows = lax.broadcasted_iota(jnp.int32, (size, size), 0)
    columns = lax.broadcasted_iota(jnp.int32, (size, size), 1)
    return (rows == columns).astype(F32)


def row_norm(matrix):
    return jnp.max(jnp.sum(jnp.abs(matrix), axis=1, keepdims=True), axis=0, keepdims=True)


def fast_inverse(matrix, identity, steps):
    diagonal = matrix * identity
    by_row = START_SCALE / jnp.sum(diagonal, axis=1, keepdims=True)
    by_column = START_SCALE / jnp.sum(diagonal, axis=0, keepdims=True)
    error = identity - by_row * matrix
    inverse = (identity + error) * by_column
    error16 = error.astype(BF16)
    for _ in range(steps):
        error16 = dot1(error16, error16).astype(BF16)
        inverse = inverse + dot1(error16, inverse.astype(BF16))
    return inverse, identity - dot3(split(matrix), split(inverse))


def exact_dot(lhs, rhs):
    return lax.dot_general(
        lhs, rhs, NN, precision=lax.Precision.HIGHEST, preferred_element_type=F32
    )


def slow_inverse(matrix, identity, steps, matrix_scr, inverse_scr):
    matrix_scr[...] = matrix
    inverse_scr[...] = identity * (SLOW_SCALE / row_norm(matrix))

    def going(state):
        count, size = state
        return (size > 1e-3) & (count < 100)

    def step(state):
        count, _ = state
        inverse = inverse_scr[...]
        residual = identity - exact_dot(matrix_scr[...], inverse)
        inverse_scr[...] = inverse + exact_dot(inverse, residual)
        return count + 1, jnp.max(row_norm(residual))

    lax.while_loop(going, step, (jnp.int32(0), jnp.float32(1e9)))
    return inverse_scr[...], None


def correct(product, residual16):
    if residual16 is None:
        return product
    return product + dot1(product.astype(BF16), residual16)


def pack_symmetric(matrix):
    half = matrix.shape[0] // 2
    rows = lax.broadcasted_iota(jnp.int32, (half, half), 0)
    columns = lax.broadcasted_iota(jnp.int32, (half, half), 1)
    first, second = matrix[:half, :half], matrix[half:, half:]
    mixed = jnp.where(rows > columns, first, jnp.where(rows < columns, second, 0.0))
    return jnp.concatenate([matrix[half:, :half], mixed], axis=1)


def unpack_symmetric(packed):
    half = packed.shape[0]
    rows = lax.broadcasted_iota(jnp.int32, (half, half), 0)
    columns = lax.broadcasted_iota(jnp.int32, (half, half), 1)
    corner, mixed = packed[:, :half], packed[:, half:]
    first = jnp.where(rows > columns, mixed, 0.0)
    second = jnp.where(rows < columns, mixed, 0.0)
    return jnp.concatenate(
        [
            jnp.concatenate([first + first.T, corner.T], axis=1),
            jnp.concatenate([corner, second + second.T], axis=1),
        ],
        axis=0,
    )


def diagonal_of(matrix):
    return jnp.sum(matrix * eye_of(matrix.shape[0]), axis=0, keepdims=True)


def extra_rows(ham, level, weight):
    row = lax.broadcasted_iota(jnp.int32, (8, ham.shape[1]), 0)
    return jnp.where(row == 0, diagonal_of(ham) + level + 2.0, weight)


def quarter_index():
    return lax.axis_index("rhs") * lax.axis_size("energy") + lax.axis_index("energy")


def pack_part_kernel(
    weight_ref, level_hbm, ham_hbm, coupling_hbm, projector_hbm, out_ref, ham_ref, pack_scr,
    level_ref, sems,
):
    part = (out_ref.shape[0] - 8) * 2 // 5
    half = part // 2
    index = quarter_index()
    rows = pl.ds(pl.multiple_of(index * part, 8), part)
    copies = [
        pltpu.make_async_copy(source, target, sems.at[number])
        for number, (source, target) in enumerate(
            (
                (ham_hbm.at[0], ham_ref),
                (level_hbm, level_ref),
                (coupling_hbm.at[0, rows], out_ref.at[half : half + part]),
                (projector_hbm.at[0, rows], out_ref.at[half + part : half + 2 * part]),
            )
        )
    ]
    for copy in copies:
        copy.start()
    copies[0].wait()
    copies[1].wait()
    ham = 0.5 * (ham_ref[...] + ham_ref[...].T)
    pack_scr[...] = pack_symmetric(ham)
    out_ref[:half] = pack_scr[pl.ds(pl.multiple_of(index * half, 8), half), :]
    out_ref[half + 2 * part :] = extra_rows(ham, level_ref[...], weight_ref[0])
    copies[2].wait()
    copies[3].wait()


def pack_part(weight, level, ham, coupling, projector, parts):
    size = ham.shape[1]
    part = size // parts
    smem = pl.BlockSpec(memory_space=pltpu.SMEM)
    vmem = pl.BlockSpec(memory_space=pltpu.VMEM)
    anywhere = pl.BlockSpec(memory_space=pl.ANY)
    height = part // 2 + 2 * part + 8
    return pl.pallas_call(
        pack_part_kernel,
        out_shape=jax.ShapeDtypeStruct((height, size), F32),
        in_specs=[smem] + [anywhere] * 4,
        out_specs=vmem,
        scratch_shapes=[
            pltpu.VMEM((size, size), F32),
            pltpu.VMEM((size // 2, size), F32),
            pltpu.VMEM((1, size), F32),
            pltpu.SemaphoreType.DMA((4,)),
        ],
        compiler_params=pltpu.CompilerParams(vmem_limit_bytes=PACK_BYTES),
        name="pack_part",
    )(weight, level, ham, coupling, projector)


def pack_kernel(weight_ref, level_ref, ham_ref, coupling_ref, projector_ref, whole_ref):
    parts = whole_ref.shape[0]
    size = ham_ref.shape[1]
    part = size // parts
    half = part // 2
    ham = 0.5 * (ham_ref[0] + ham_ref[0].T)
    packed = pack_symmetric(ham)
    extra = extra_rows(ham, level_ref[...], weight_ref[0])
    for n in range(parts):
        rows = slice(n * part, (n + 1) * part)
        whole_ref[n, :half] = packed[n * half : (n + 1) * half]
        whole_ref[n, half : half + part] = coupling_ref[0, rows]
        whole_ref[n, half + part : half + 2 * part] = projector_ref[0, rows]
        whole_ref[n, half + 2 * part :] = extra


def pack(weight, level, ham, coupling, projector, parts):
    size = ham.shape[1]
    part = size // parts
    smem = pl.BlockSpec(memory_space=pltpu.SMEM)
    vmem = pl.BlockSpec(memory_space=pltpu.VMEM)
    return pl.pallas_call(
        pack_kernel,
        out_shape=jax.ShapeDtypeStruct((parts, part // 2 + 2 * part + 8, size), F32),
        in_specs=[smem] + [vmem] * 4,
        out_specs=vmem,
        compiler_params=pltpu.CompilerParams(vmem_limit_bytes=VMEM_BYTES),
        name="pack",
    )(weight, level, ham, coupling, projector)


def potential_kernel(basis_ref, out_ref):
    basis = split(basis_ref[...])
    out_ref[...] = dot3(basis, basis, NT)


def potential_of(basis):
    vmem = pl.BlockSpec(memory_space=pltpu.VMEM)
    return pl.pallas_call(
        potential_kernel,
        out_shape=jax.ShapeDtypeStruct((basis.shape[0],) * 2, F32),
        in_specs=[vmem],
        out_specs=vmem,
        compiler_params=pltpu.CompilerParams(vmem_limit_bytes=VMEM_BYTES),
        name="potential",
    )(basis)


def pieces(refs):
    element, quarter = lax.axis_index("elem"), quarter_index()
    for j in range(refs[0].shape[1]):
        yield element, j, refs[0].at[0, j]
        step = 1
        for ref in refs[1:]:
            for k in range(ref.shape[0]):
                yield element ^ (step + k), quarter ^ j, ref.at[k, j]
            step = step + ref.shape[0]


def factor_kernel(groups, shift_ref, potential_ref, *rest):
    refs, rest = rest[:groups], rest[groups:]
    inverse_ref, link_ref, extra_ref, diag_scr, coupling_ref, pack_scr, *scratch = rest
    matrix_scr, inverse_scr = scratch
    count = extra_ref.shape[0]
    size = potential_ref.shape[0]
    part = size // refs[0].shape[1]
    half = part // 2
    middle = count // 2
    identity = eye_of(size)
    potential = potential_ref[...]
    for element, index, ref in pieces(refs):
        start = pl.multiple_of(index * half, 8)
        pack_scr[element, pl.ds(start, half), :] = ref[:half]
        start = pl.multiple_of(index * part, 8)
        coupling_ref[element, pl.ds(start, part), :] = ref[half : half + part]
        extra_ref[element] = ref[half + 2 * part :]
    for n in range(count):
        diag_scr[n] = (
            unpack_symmetric(pack_scr[n])
            + (extra_ref[n, 0:1] + shift_ref[0]) * identity
            + extra_ref[n, 1:2, :1] * potential
        )

    def eliminate(invert):
        worst = jnp.zeros((1, 1), F32)
        forward = diag_scr[0]
        backward = diag_scr[count - 1]

        def finish(n, matrix, worst):
            inverse, residual = invert(matrix, identity, 2 if n == middle else 1)
            residual16 = None
            if residual is not None:
                worst = jnp.maximum(worst, row_norm(residual))
                residual16 = residual.astype(BF16)
            final = split(correct(inverse, residual16))
            inverse_ref[0, n] = final[0]
            inverse_ref[1, n] = final[1]
            return split(inverse), residual16, worst

        def connect(n, coupling, inverse, residual16):
            parts = split(correct(dot3(coupling, inverse), residual16))
            link_ref[0, n] = parts[0]
            link_ref[1, n] = parts[1]
            return parts

        meeting = diag_scr[middle]
        for step in range(max(middle, count - 1 - middle)):
            ahead, behind = step, count - 1 - step
            if ahead < middle:
                parts, residual16, worst = finish(ahead, forward, worst)
                coupling = split(-(identity + coupling_ref[ahead + 1]))
                link = connect(ahead + 1, coupling, parts, residual16)
                update = dot3(link, coupling, NT)
                if ahead + 1 < middle:
                    forward = diag_scr[ahead + 1] - update
                else:
                    meeting = meeting - update
            if behind > middle:
                parts, residual16, worst = finish(behind, backward, worst)
                raw = -(identity + coupling_ref[behind])
                link = connect(behind, split(raw.T), parts, residual16)
                update = dot3(link, split(raw))
                if behind - 1 > middle:
                    backward = diag_scr[behind - 1] - update
                else:
                    meeting = meeting - update
        _, _, worst = finish(middle, meeting, worst)
        return worst

    worst = jnp.max(eliminate(fast_inverse))

    @pl.when(jnp.logical_not(worst <= RESIDUAL_BOUND))
    def _():
        eliminate(
            functools.partial(slow_inverse, matrix_scr=matrix_scr, inverse_scr=inverse_scr)
        )


def factorize(shift, potential, payloads):
    count, size = sum(value.shape[0] for value in payloads), potential.shape[0]
    smem = pl.BlockSpec(memory_space=pltpu.SMEM)
    vmem = pl.BlockSpec(memory_space=pltpu.VMEM)
    half = jax.ShapeDtypeStruct((2, count, size, size), BF16)
    return pl.pallas_call(
        functools.partial(factor_kernel, len(payloads)),
        out_shape=(half, half, jax.ShapeDtypeStruct((count, 8, size), F32)),
        in_specs=[smem] + [vmem] * (1 + len(payloads)),
        out_specs=(vmem, vmem, vmem),
        scratch_shapes=[
            pltpu.VMEM((count, size, size), F32),
            pltpu.VMEM((count, size, size), F32),
            pltpu.VMEM((count, size // 2, size), F32),
            pltpu.VMEM((size, size), F32),
            pltpu.VMEM((size, size), F32),
        ],
        compiler_params=pltpu.CompilerParams(vmem_limit_bytes=VMEM_BYTES),
        name="factorize",
    )(shift, potential, *payloads)


def load_factors(inverse_ref, link_ref):
    count = inverse_ref.shape[1]
    inverses = [(inverse_ref[0, n], inverse_ref[1, n]) for n in range(count)]
    links = [(link_ref[0, n], link_ref[1, n]) if n != 0 else None for n in range(count)]
    return inverses, links


def solve_blocks(blocks, inverses, links):
    count = len(blocks)
    middle = count // 2
    reduced = list(blocks)
    for n in range(1, middle + 1):
        reduced[n] = reduced[n] - dot3(split(reduced[n - 1]), links[n], NT)
    for n in range(count - 1, middle, -1):
        reduced[n - 1] = reduced[n - 1] - dot3(split(reduced[n]), links[n], NT)
    solved = [dot3(split(reduced[n]), inverses[n]) for n in range(count)]
    for n in range(middle, 0, -1):
        solved[n - 1] = solved[n - 1] - dot3(split(solved[n]), links[n])
    for n in range(middle + 1, count):
        solved[n] = solved[n] - dot3(split(solved[n - 1]), links[n])
    return solved


def solve_kernel(
    groups, open_ref, inverse_ref, link_ref, extra_ref, target_ref, *rest
):
    count = inverse_ref.shape[1]
    refs, rest = rest[:groups], rest[groups:]
    *source_refs, wave_ref, adjoint_ref, share_ref, gram_ref, own_scr, k_scr, projector_scr = rest
    channels, width = source_refs[0].shape[1:]
    me, column = lax.axis_index("elem"), lax.axis_index("rhs")
    part = channels // refs[0].shape[1]
    begin = part // 2 + part
    for element, index, ref in pieces(refs):
        start = pl.multiple_of(index * part, 8)
        projector_scr[element, pl.ds(start, part), :] = ref[begin : begin + part]
    order, distance = [0], count // 2
    while distance:
        order = order + [n ^ distance for n in order]
        distance = distance // 2
    for place, n in enumerate(order):
        half = source_refs[0].shape[0]
        own_scr[me ^ n] = source_refs[place // half][place % half]
    inverses, links = load_factors(inverse_ref, link_ref)
    projectors = [split(projector_scr[n]) for n in range(count)]
    wave = solve_blocks([own_scr[n].T for n in range(count)], inverses, links)
    k_total = dot3(split(wave[0]), projectors[0])
    for n in range(1, count):
        k_total = k_total + dot3(split(wave[n]), projectors[n])
    k_rows = lax.broadcasted_iota(jnp.int32, k_total.shape, 1)
    k_columns = lax.broadcasted_iota(jnp.int32, k_total.shape, 0) + column * width
    opened = (k_rows < open_ref[0]) & (k_columns < open_ref[0])
    residual = split(jnp.where(opened, k_total - target_ref[...].T, 0.0))
    drive = [PENALTY * wave[n] + dot3(residual, projectors[n], NT) for n in range(count)]
    adjoint = [value.T for value in solve_blocks(drive, inverses, links)]
    wave = [value.T for value in wave]

    share = share_ref.shape[0]
    k_scr[...] = k_total.T
    share_ref[...] = k_scr[pl.ds(pl.multiple_of(me * share, share), share), :]
    for n in range(count):
        own_scr[n] = wave[n]
    wave_ref[...] = own_scr[me]
    for n in range(count):
        own_scr[n] = adjoint[n]
    adjoint_ref[...] = own_scr[me]
    weighted = [extra_ref[n, 1:2, :1] * wave[n] for n in range(count)]
    weighted = split(jnp.concatenate(weighted, axis=1))
    gram = dot3(split(jnp.concatenate(adjoint, axis=1)), weighted, NT)
    gram = gram + gram.T
    half = channels // 2
    gram_ref[:half] = pack_symmetric(gram)
    gram_ref[half:] = jnp.broadcast_to(diagonal_of(gram), (8, channels))


def solve_all(opened, inverses, links, extras, target, payloads, sources):
    count, channels, width = inverses.shape[1], *sources[0].shape[1:]
    rows = target.shape[0]
    smem = pl.BlockSpec(memory_space=pltpu.SMEM)
    vmem = pl.BlockSpec(memory_space=pltpu.VMEM)
    return pl.pallas_call(
        functools.partial(solve_kernel, len(payloads)),
        out_shape=(
            jax.ShapeDtypeStruct((channels, width), F32),
            jax.ShapeDtypeStruct((channels, width), F32),
            jax.ShapeDtypeStruct((rows // count, width), F32),
            jax.ShapeDtypeStruct((channels // 2 + 8, channels), F32),
        ),
        in_specs=[smem] + [vmem] * (4 + len(payloads) + len(sources)),
        out_specs=(vmem,) * 4,
        scratch_shapes=[
            pltpu.VMEM((count, channels, width), F32),
            pltpu.VMEM((rows, width), F32),
            pltpu.VMEM((count, channels, channels), F32),
        ],
        compiler_params=pltpu.CompilerParams(vmem_limit_bytes=VMEM_BYTES),
        name="solve",
    )(opened, inverses, links, extras, target, *payloads, *sources)


def gradient_kernel(scale, own_ref, other_ref, basis_ref, out_ref):
    size = basis_ref.shape[0]
    total = own_ref[...] + other_ref[...]
    gram = unpack_symmetric(total[: size // 2])
    gram = gram + total[size // 2 : size // 2 + 1] * eye_of(size)
    out_ref[...] = scale * dot3(split(gram), split(basis_ref[...]))


def gradient(scale, own, other, basis):
    vmem = pl.BlockSpec(memory_space=pltpu.VMEM)
    return pl.pallas_call(
        functools.partial(gradient_kernel, scale),
        out_shape=jax.ShapeDtypeStruct(basis.shape, F32),
        in_specs=[vmem, vmem, vmem],
        out_specs=vmem,
        compiler_params=pltpu.CompilerParams(vmem_limit_bytes=VMEM_BYTES),
        name="gradient",
    )(own, other, basis)


def swap(value, axis, step):
    count = lax.axis_size(axis)
    return lax.ppermute(value, axis, [(i, i ^ step) for i in range(count)])


def gradient_total(gram, scale, basis):
    steps = []
    for axis in ("rhs", "energy"):
        step = 1
        while step < lax.axis_size(axis):
            steps.append((axis, step))
            step = step * 2
    other = jnp.zeros_like(gram)
    for index, (axis, step) in enumerate(steps):
        if index:
            gram = gram + other
        other = swap(gram, axis, step)
    return gradient(scale, gram, other, basis)


def per_device(
    ham_noise,
    channel_levels,
    coupling_noise,
    corr_weight,
    corr_basis,
    projector,
    energy_shift,
    sources,
    target,
    open_channels,
):
    elements, energies, halves = (lax.axis_size(axis) for axis in ("elem", "energy", "rhs"))
    parts = energies * halves
    raw = (corr_weight, channel_levels, ham_noise, coupling_noise, projector)
    mine = pack_part(*raw, parts)
    whole = pack(*raw, parts)
    potential = potential_of(corr_basis)

    def reach(found, step):
        low = step & -step
        return swap(found[step ^ low], "elem", low)

    def spread(payload, axis):
        distance = 1
        while distance < lax.axis_size(axis):
            payload = jnp.concatenate([payload, swap(payload, axis, distance)], axis=1)
            distance = distance * 2
        return payload

    steps = range(1, elements)
    far = elements // 2
    own = sources[:, 0]
    beyond = swap(own, "elem", far)
    near = {0: mine, 1: swap(mine, "elem", 1)}
    near[0], beyond = lax.optimization_barrier((mine, beyond))
    for step in steps[1:]:
        near[step] = reach(near, step)
        if step == far:
            near[far], whole, potential = lax.optimization_barrier((near[far], whole, potential))
    sets = [spread(near[step][None, None], "energy") for step in steps]
    source_all, distance = [own, beyond], far // 2
    while distance:
        source_all = [jnp.concatenate(source_all, axis=0)]
        source_all.append(swap(source_all[0], "elem", distance))
        distance = distance // 2
    groups = [sets[:-1], sets[-1:]] if len(sets) > 1 else [sets]
    payloads = [spread(jnp.concatenate(group, axis=0), "rhs") for group in groups]
    payloads = [whole[None], *payloads]
    inverses, links, extras = factorize(energy_shift, potential, payloads)
    wave, adjoint, share, gram = solve_all(
        open_channels, inverses, links, extras, target[0], payloads, source_all
    )
    basis_grad = gradient_total(gram, -1.0 / (energies * elements), corr_basis)
    return wave[None, None], adjoint[None, None], share[None], basis_grad


def solution(mesh):
    return jax.shard_map(
        per_device,
        mesh=mesh,
        in_specs=(
            P(("groups", "elem"), None, None),
            P(("groups", "elem"), None),
            P(("groups", "elem"), None, None),
            P(("groups", "elem")),
            P("groups", None),
            P(("groups", "elem"), None, None),
            P(("groups", "energy")),
            P(("groups", "energy"), "elem", None, "rhs"),
            P(("groups", "energy"), None, "rhs"),
            P(("groups", "energy")),
        ),
        out_specs=(
            P(("groups", "energy"), "elem", None, "rhs"),
            P(("groups", "energy"), "elem", None, "rhs"),
            P(("groups", "energy"), "elem", "rhs"),
            P("groups", None),
        ),
        check_vma=False,
    )
```

```python
import functools

import jax
import jax.numpy as jnp
from jax import lax
from jax.experimental import pallas as pl
from jax.experimental.pallas import tpu as pltpu
from jax.sharding import PartitionSpec as P

PENALTY = 0.5
START_SCALE = 0.95
SLOW_SCALE = 1.75
RESIDUAL_BOUND = 0.01
F32 = jnp.float32
BF16 = jnp.bfloat16
NN = (((1,), (0,)), ((), ()))
NT = (((1,), (1,)), ((), ()))
VMEM_BYTES = 48 * 1024 * 1024
PACK_BYTES = 60 * 1024 * 1024


def split(value):
    high = value.astype(BF16)
    return high, (value - high.astype(F32)).astype(BF16)


def dot1(lhs, rhs, dims=NN):
    return lax.dot_general(lhs, rhs, dims, preferred_element_type=F32)


def dot3(lhs, rhs, dims=NN):
    return (
        dot1(lhs[0], rhs[0], dims) + dot1(lhs[0], rhs[1], dims) + dot1(lhs[1], rhs[0], dims)
    )


def eye_of(size):
    rows = lax.broadcasted_iota(jnp.int32, (size, size), 0)
    columns = lax.broadcasted_iota(jnp.int32, (size, size), 1)
    return (rows == columns).astype(F32)


def row_norm(matrix):
    return jnp.max(jnp.sum(jnp.abs(matrix), axis=1, keepdims=True), axis=0, keepdims=True)


def fast_inverse(matrix, identity, steps):
    diagonal = matrix * identity
    by_row = START_SCALE / jnp.sum(diagonal, axis=1, keepdims=True)
    by_column = START_SCALE / jnp.sum(diagonal, axis=0, keepdims=True)
    error = identity - by_row * matrix
    inverse = (identity + error) * by_column
    error16 = error.astype(BF16)
    for _ in range(steps):
        error16 = dot1(error16, error16).astype(BF16)
        inverse = inverse + dot1(error16, inverse.astype(BF16))
    return inverse, identity - dot3(split(matrix), split(inverse))


def exact_dot(lhs, rhs):
    return lax.dot_general(
        lhs, rhs, NN, precision=lax.Precision.HIGHEST, preferred_element_type=F32
    )


def slow_inverse(matrix, identity, steps, matrix_scr, inverse_scr):
    matrix_scr[...] = matrix
    inverse_scr[...] = identity * (SLOW_SCALE / row_norm(matrix))

    def going(state):
        count, size = state
        return (size > 1e-3) & (count < 100)

    def step(state):
        count, _ = state
        inverse = inverse_scr[...]
        residual = identity - exact_dot(matrix_scr[...], inverse)
        inverse_scr[...] = inverse + exact_dot(inverse, residual)
        return count + 1, jnp.max(row_norm(residual))

    lax.while_loop(going, step, (jnp.int32(0), jnp.float32(1e9)))
    return inverse_scr[...], None


def correct(product, residual16):
    if residual16 is None:
        return product
    return product + dot1(product.astype(BF16), residual16)


def pack_symmetric(matrix):
    half = matrix.shape[0] // 2
    rows = lax.broadcasted_iota(jnp.int32, (half, half), 0)
    columns = lax.broadcasted_iota(jnp.int32, (half, half), 1)
    first, second = matrix[:half, :half], matrix[half:, half:]
    mixed = jnp.where(rows > columns, first, jnp.where(rows < columns, second, 0.0))
    return jnp.concatenate([matrix[half:, :half], mixed], axis=1)


def unpack_symmetric(packed):
    half = packed.shape[0]
    rows = lax.broadcasted_iota(jnp.int32, (half, half), 0)
    columns = lax.broadcasted_iota(jnp.int32, (half, half), 1)
    corner, mixed = packed[:, :half], packed[:, half:]
    first = jnp.where(rows > columns, mixed, 0.0)
    second = jnp.where(rows < columns, mixed, 0.0)
    return jnp.concatenate(
        [
            jnp.concatenate([first + first.T, corner.T], axis=1),
            jnp.concatenate([corner, second + second.T], axis=1),
        ],
        axis=0,
    )


def diagonal_of(matrix):
    return jnp.sum(matrix * eye_of(matrix.shape[0]), axis=0, keepdims=True)


def extra_rows(ham, level, weight):
    row = lax.broadcasted_iota(jnp.int32, (8, ham.shape[1]), 0)
    return jnp.where(row == 0, diagonal_of(ham) + level + 2.0, weight)


def quarter_index():
    return lax.axis_index("rhs") * lax.axis_size("energy") + lax.axis_index("energy")


def pack_part_kernel(
    weight_ref, level_hbm, ham_hbm, coupling_hbm, projector_hbm, out_ref, ham_ref, pack_scr,
    level_ref, sems,
):
    part = (out_ref.shape[0] - 8) * 2 // 5
    half = part // 2
    index = quarter_index()
    rows = pl.ds(pl.multiple_of(index * part, 8), part)
    copies = [
        pltpu.make_async_copy(source, target, sems.at[number])
        for number, (source, target) in enumerate(
            (
                (ham_hbm.at[0], ham_ref),
                (level_hbm, level_ref),
                (coupling_hbm.at[0, rows], out_ref.at[half : half + part]),
                (projector_hbm.at[0, rows], out_ref.at[half + part : half + 2 * part]),
            )
        )
    ]
    for copy in copies:
        copy.start()
    copies[0].wait()
    copies[1].wait()
    ham = 0.5 * (ham_ref[...] + ham_ref[...].T)
    pack_scr[...] = pack_symmetric(ham)
    out_ref[:half] = pack_scr[pl.ds(pl.multiple_of(index * half, 8), half), :]
    out_ref[half + 2 * part :] = extra_rows(ham, level_ref[...], weight_ref[0])
    copies[2].wait()
    copies[3].wait()


def pack_part(weight, level, ham, coupling, projector, parts):
    size = ham.shape[1]
    part = size // parts
    smem = pl.BlockSpec(memory_space=pltpu.SMEM)
    vmem = pl.BlockSpec(memory_space=pltpu.VMEM)
    anywhere = pl.BlockSpec(memory_space=pl.ANY)
    height = part // 2 + 2 * part + 8
    return pl.pallas_call(
        pack_part_kernel,
        out_shape=jax.ShapeDtypeStruct((height, size), F32),
        in_specs=[smem] + [anywhere] * 4,
        out_specs=vmem,
        scratch_shapes=[
            pltpu.VMEM((size, size), F32),
            pltpu.VMEM((size // 2, size), F32),
            pltpu.VMEM((1, size), F32),
            pltpu.SemaphoreType.DMA((4,)),
        ],
        compiler_params=pltpu.CompilerParams(vmem_limit_bytes=PACK_BYTES),
        name="pack_part",
    )(weight, level, ham, coupling, projector)


def pack_kernel(weight_ref, level_ref, ham_ref, coupling_ref, projector_ref, whole_ref):
    parts = whole_ref.shape[0]
    size = ham_ref.shape[1]
    part = size // parts
    half = part // 2
    ham = 0.5 * (ham_ref[0] + ham_ref[0].T)
    packed = pack_symmetric(ham)
    extra = extra_rows(ham, level_ref[...], weight_ref[0])
    for n in range(parts):
        rows = slice(n * part, (n + 1) * part)
        whole_ref[n, :half] = packed[n * half : (n + 1) * half]
        whole_ref[n, half : half + part] = coupling_ref[0, rows]
        whole_ref[n, half + part : half + 2 * part] = projector_ref[0, rows]
        whole_ref[n, half + 2 * part :] = extra


def pack(weight, level, ham, coupling, projector, parts):
    size = ham.shape[1]
    part = size // parts
    smem = pl.BlockSpec(memory_space=pltpu.SMEM)
    vmem = pl.BlockSpec(memory_space=pltpu.VMEM)
    return pl.pallas_call(
        pack_kernel,
        out_shape=jax.ShapeDtypeStruct((parts, part // 2 + 2 * part + 8, size), F32),
        in_specs=[smem] + [vmem] * 4,
        out_specs=vmem,
        compiler_params=pltpu.CompilerParams(vmem_limit_bytes=VMEM_BYTES),
        name="pack",
    )(weight, level, ham, coupling, projector)


def potential_kernel(basis_ref, out_ref):
    basis = split(basis_ref[...])
    out_ref[...] = dot3(basis, basis, NT)


def potential_of(basis):
    vmem = pl.BlockSpec(memory_space=pltpu.VMEM)
    return pl.pallas_call(
        potential_kernel,
        out_shape=jax.ShapeDtypeStruct((basis.shape[0],) * 2, F32),
        in_specs=[vmem],
        out_specs=vmem,
        compiler_params=pltpu.CompilerParams(vmem_limit_bytes=VMEM_BYTES),
        name="potential",
    )(basis)


def mirrored():
    return lax.axis_index("elem") >= lax.axis_size("elem") // 2


def position(step):
    mask = jnp.where(mirrored(), lax.axis_size("elem") - 1, 0)
    return lax.axis_index("elem") ^ step ^ mask


def pieces(refs, first):
    quarter = quarter_index()
    step = first
    for ref in refs:
        for k in range(ref.shape[0]):
            for j in range(ref.shape[1]):
                yield position(step), (j if step == 0 else quarter ^ j), ref.at[k, j]
            step = step + 1


def assemble(refs, first, base, shift, potential, identity, pack_scr, coupling_scr, extra_ref):
    size = potential.shape[0]
    part = size // refs[0].shape[1]
    half = part // 2
    for place, index, ref in pieces(refs, first):
        start = pl.multiple_of(index * half, 8)
        pack_scr[place - base, pl.ds(start, half), :] = ref[:half]
        start = pl.multiple_of(index * part, 8)
        coupling_scr[place - base, pl.ds(start, part), :] = ref[half : half + part]
        extra_ref[place - base] = ref[half + 2 * part :]
    return [
        unpack_symmetric(pack_scr[n])
        + (extra_ref[n, 0:1] + shift) * identity
        + extra_ref[n, 1:2, :1] * potential
        for n in range(extra_ref.shape[0])
    ]


def block_of(raw, identity):
    block = -(identity + raw)
    return jnp.where(mirrored(), block.T, block)


def store(ref, n, value):
    parts = split(value)
    ref[0, n] = parts[0]
    ref[1, n] = parts[1]
    return parts


def run_checked(eliminate, matrix_scr, inverse_scr):
    worst = jnp.max(eliminate(fast_inverse))

    @pl.when(jnp.logical_not(worst <= RESIDUAL_BOUND))
    def _():
        eliminate(
            functools.partial(slow_inverse, matrix_scr=matrix_scr, inverse_scr=inverse_scr)
        )


def invert_into(invert, ref, n, matrix, identity, steps, worst):
    inverse, residual = invert(matrix, identity, steps)
    residual16 = None
    if residual is not None:
        worst = jnp.maximum(worst, row_norm(residual))
        residual16 = residual.astype(BF16)
    store(ref, n, correct(inverse, residual16))
    return split(inverse), residual16, worst


def near_kernel(groups, shift_ref, potential_ref, *rest):
    refs, rest = rest[:groups], rest[groups:]
    inverse_ref, link_ref, extra_ref, last_ref, diag_scr, pack_scr, coupling_scr, *scratch = rest
    count = extra_ref.shape[0]
    potential = potential_ref[...]
    identity = eye_of(potential.shape[0])
    blocks = assemble(
        refs, 0, 0, shift_ref[0], potential, identity, pack_scr, coupling_scr, extra_ref
    )
    for n in range(count):
        diag_scr[n] = blocks[n]
    last_ref[...] = coupling_scr[count - 1]
    offset = mirrored().astype(jnp.int32)

    def eliminate(invert):
        worst = jnp.zeros((1, 1), F32)
        matrix = diag_scr[0]
        for n in range(count):
            parts, residual16, worst = invert_into(
                invert, inverse_ref, n, matrix, identity, 1, worst
            )
            if n + 1 < count:
                coupling = split(block_of(coupling_scr[n + 1 - offset], identity))
                link = correct(dot3(coupling, parts), residual16)
                matrix = diag_scr[n + 1] - dot3(store(link_ref, n + 1, link), coupling, NT)
        return worst

    run_checked(eliminate, *scratch)


def far_kernel(
    groups, shift_ref, potential_ref, near_inverse_ref, last_ref, *rest
):
    refs, rest = rest[:groups], rest[groups:]
    inverse_ref, link_ref, extra_ref, diag_scr, pack_scr, coupling_scr, *scratch = rest
    count = extra_ref.shape[0]
    near = near_inverse_ref.shape[1]
    potential = potential_ref[...]
    identity = eye_of(potential.shape[0])
    blocks = assemble(
        refs, near, near, shift_ref[0], potential, identity, pack_scr, coupling_scr, extra_ref
    )
    offset = mirrored().astype(jnp.int32)
    coupling = split(
        block_of(jnp.where(mirrored(), last_ref[...], coupling_scr[0]), identity)
    )
    inner = (near_inverse_ref[0, near - 1], near_inverse_ref[1, near - 1])
    link = store(link_ref, 0, dot3(coupling, inner))
    diag_scr[0] = blocks[0] - dot3(link, coupling, NT)
    for n in range(1, count):
        diag_scr[n] = blocks[n]

    def eliminate(invert):
        worst = jnp.zeros((1, 1), F32)
        matrix = diag_scr[count - 1]
        for n in range(count - 1, 0, -1):
            parts, residual16, worst = invert_into(
                invert, inverse_ref, n, matrix, identity, 1, worst
            )
            raw = block_of(coupling_scr[n - offset], identity)
            link = correct(dot3(split(raw.T), parts), residual16)
            matrix = diag_scr[n - 1] - dot3(store(link_ref, n, link), split(raw))
        _, _, worst = invert_into(invert, inverse_ref, 0, matrix, identity, 2, worst)
        return worst

    run_checked(eliminate, *scratch)


def factor_call(kernel, name, shift, potential, given, payloads, with_last):
    size = potential.shape[0]
    count = sum(value.shape[0] for value in payloads)
    smem = pl.BlockSpec(memory_space=pltpu.SMEM)
    vmem = pl.BlockSpec(memory_space=pltpu.VMEM)
    pair = jax.ShapeDtypeStruct((2, count, size, size), BF16)
    shapes = [pair, pair, jax.ShapeDtypeStruct((count, 8, size), F32)]
    if with_last:
        shapes.append(jax.ShapeDtypeStruct((size, size), F32))
    return pl.pallas_call(
        functools.partial(kernel, len(payloads)),
        out_shape=tuple(shapes),
        in_specs=[smem] + [vmem] * (1 + len(given) + len(payloads)),
        out_specs=(vmem,) * len(shapes),
        scratch_shapes=[
            pltpu.VMEM((count, size, size), F32),
            pltpu.VMEM((count, size // 2, size), F32),
            pltpu.VMEM((count, size, size), F32),
            pltpu.VMEM((size, size), F32),
            pltpu.VMEM((size, size), F32),
        ],
        compiler_params=pltpu.CompilerParams(vmem_limit_bytes=VMEM_BYTES),
        cost_estimate=pl.CostEstimate(
            flops=80 * count * size**3, bytes_accessed=24 * count * size**2, transcendentals=0
        ),
        name=name,
    )(shift, potential, *given, *payloads)


def load_pairs(near_ref, far_ref):
    return [
        (ref[0, n], ref[1, n]) for ref in (near_ref, far_ref) for n in range(ref.shape[1])
    ]


def solve_blocks(blocks, inverses, links):
    count = len(blocks)
    middle = count // 2
    reduced = list(blocks)
    for n in range(1, middle + 1):
        reduced[n] = reduced[n] - dot3(split(reduced[n - 1]), links[n], NT)
    for n in range(count - 1, middle, -1):
        reduced[n - 1] = reduced[n - 1] - dot3(split(reduced[n]), links[n], NT)
    solved = [dot3(split(reduced[n]), inverses[n]) for n in range(count)]
    for n in range(middle, 0, -1):
        solved[n - 1] = solved[n - 1] - dot3(split(solved[n]), links[n])
    for n in range(middle + 1, count):
        solved[n] = solved[n] - dot3(split(solved[n - 1]), links[n])
    return solved


def solve_kernel(groups, open_ref, *rest):
    factor_refs, target_ref, refs, rest = rest[:6], rest[6], rest[7 : 7 + groups], rest[7 + groups :]
    *source_refs, wave_ref, adjoint_ref, share_ref, gram_ref, own_scr, k_scr, projector_scr = rest
    channels, width = source_refs[0].shape[1:]
    count = projector_scr.shape[0]
    me, column = lax.axis_index("elem"), lax.axis_index("rhs")
    part = channels // refs[0].shape[1]
    begin = part // 2 + part
    for place, index, ref in pieces(refs, 0):
        start = pl.multiple_of(index * part, 8)
        projector_scr[place, pl.ds(start, part), :] = ref[begin : begin + part]
    order, distance = [0], count // 2
    while distance:
        order = order + [n ^ distance for n in order]
        distance = distance // 2
    for number, n in enumerate(order):
        half = source_refs[0].shape[0]
        own_scr[position(n)] = source_refs[number // half][number % half]
    inverses = load_pairs(factor_refs[0], factor_refs[1])
    links = load_pairs(factor_refs[2], factor_refs[3])
    extras = [ref[n] for ref in factor_refs[4:6] for n in range(ref.shape[0])]
    projectors = [split(projector_scr[n]) for n in range(count)]
    wave = solve_blocks([own_scr[n].T for n in range(count)], inverses, links)
    k_total = dot3(split(wave[0]), projectors[0])
    for n in range(1, count):
        k_total = k_total + dot3(split(wave[n]), projectors[n])
    k_rows = lax.broadcasted_iota(jnp.int32, k_total.shape, 1)
    k_columns = lax.broadcasted_iota(jnp.int32, k_total.shape, 0) + column * width
    opened = (k_rows < open_ref[0]) & (k_columns < open_ref[0])
    residual = split(jnp.where(opened, k_total - target_ref[...].T, 0.0))
    drive = [PENALTY * wave[n] + dot3(residual, projectors[n], NT) for n in range(count)]
    adjoint = [value.T for value in solve_blocks(drive, inverses, links)]
    wave = [value.T for value in wave]

    share = share_ref.shape[0]
    k_scr[...] = k_total.T
    share_ref[...] = k_scr[pl.ds(pl.multiple_of(me * share, share), share), :]
    for n in range(count):
        own_scr[n] = wave[n]
    wave_ref[...] = own_scr[position(0)]
    for n in range(count):
        own_scr[n] = adjoint[n]
    adjoint_ref[...] = own_scr[position(0)]
    weighted = [extras[n][1:2, :1] * wave[n] for n in range(count)]
    weighted = split(jnp.concatenate(weighted, axis=1))
    gram = dot3(split(jnp.concatenate(adjoint, axis=1)), weighted, NT)
    gram = gram + gram.T
    half = channels // 2
    gram_ref[:half] = pack_symmetric(gram)
    gram_ref[half:] = jnp.broadcast_to(diagonal_of(gram), (8, channels))


def solve_all(opened, factors, target, payloads, sources):
    count = sum(value.shape[0] for value in payloads)
    channels, width = sources[0].shape[1:]
    rows = target.shape[0]
    smem = pl.BlockSpec(memory_space=pltpu.SMEM)
    vmem = pl.BlockSpec(memory_space=pltpu.VMEM)
    return pl.pallas_call(
        functools.partial(solve_kernel, len(payloads)),
        out_shape=(
            jax.ShapeDtypeStruct((channels, width), F32),
            jax.ShapeDtypeStruct((channels, width), F32),
            jax.ShapeDtypeStruct((rows // count, width), F32),
            jax.ShapeDtypeStruct((channels // 2 + 8, channels), F32),
        ),
        in_specs=[smem] + [vmem] * (7 + len(payloads) + len(sources)),
        out_specs=(vmem,) * 4,
        scratch_shapes=[
            pltpu.VMEM((count, channels, width), F32),
            pltpu.VMEM((rows, width), F32),
            pltpu.VMEM((count, channels, channels), F32),
        ],
        compiler_params=pltpu.CompilerParams(vmem_limit_bytes=VMEM_BYTES),
        name="solve",
    )(opened, *factors, target, *payloads, *sources)


def gradient_kernel(scale, own_ref, other_ref, basis_ref, out_ref):
    size = basis_ref.shape[0]
    total = own_ref[...] + other_ref[...]
    gram = unpack_symmetric(total[: size // 2])
    gram = gram + total[size // 2 : size // 2 + 1] * eye_of(size)
    out_ref[...] = scale * dot3(split(gram), split(basis_ref[...]))


def gradient(scale, own, other, basis):
    vmem = pl.BlockSpec(memory_space=pltpu.VMEM)
    return pl.pallas_call(
        functools.partial(gradient_kernel, scale),
        out_shape=jax.ShapeDtypeStruct(basis.shape, F32),
        in_specs=[vmem, vmem, vmem],
        out_specs=vmem,
        compiler_params=pltpu.CompilerParams(vmem_limit_bytes=VMEM_BYTES),
        name="gradient",
    )(own, other, basis)


def swap(value, axis, step):
    count = lax.axis_size(axis)
    return lax.ppermute(value, axis, [(i, i ^ step) for i in range(count)])


def gradient_total(gram, scale, basis):
    steps = []
    for axis in ("rhs", "energy"):
        step = 1
        while step < lax.axis_size(axis):
            steps.append((axis, step))
            step = step * 2
    other = jnp.zeros_like(gram)
    for index, (axis, step) in enumerate(steps):
        if index:
            gram = gram + other
        other = swap(gram, axis, step)
    return gradient(scale, gram, other, basis)


def per_device(
    ham_noise,
    channel_levels,
    coupling_noise,
    corr_weight,
    corr_basis,
    projector,
    energy_shift,
    sources,
    target,
    open_channels,
):
    elements, energies, halves = (lax.axis_size(axis) for axis in ("elem", "energy", "rhs"))
    parts = energies * halves
    raw = (corr_weight, channel_levels, ham_noise, coupling_noise, projector)
    mine = pack_part(*raw, parts)
    whole = pack(*raw, parts)
    potential = potential_of(corr_basis)

    def reach(found, step):
        low = step & -step
        return swap(found[step ^ low], "elem", low)

    def spread(payload, axis):
        distance = 1
        while distance < lax.axis_size(axis):
            payload = jnp.concatenate([payload, swap(payload, axis, distance)], axis=1)
            distance = distance * 2
        return payload

    steps = range(1, elements)
    far = elements // 2
    near = {0: mine}
    for step in steps:
        near[step] = reach(near, step)
        if step == far:
            near[far], near[1], whole, potential = lax.optimization_barrier(
                (near[far], near[1], whole, potential)
            )
    payloads = [whole[None]]
    beyond = swap(sources[:, 0], "elem", far)
    near[elements - 1], beyond = lax.optimization_barrier((near[elements - 1], beyond))
    sets = [spread(near[step][None, None], "energy") for step in steps[:-1]]
    if far > 1:
        sets[0], sets[far - 1], near[elements - 1] = lax.optimization_barrier(
            (sets[0], sets[far - 1], near[elements - 1])
        )
    sets.append(spread(near[elements - 1][None, None], "energy"))
    source_all, distance = [sources[:, 0], beyond], far // 2
    while distance:
        source_all = [jnp.concatenate(source_all, axis=0)]
        source_all.append(swap(source_all[0], "elem", distance))
        distance = distance // 2
    if far > 1:
        payloads.append(spread(jnp.concatenate(sets[: far - 1], axis=0), "rhs"))
    inverse_a, link_a, extra_a, last = factor_call(
        near_kernel, "near", energy_shift, potential, (), payloads, True
    )
    sets[far - 1], inverse_a = lax.optimization_barrier((sets[far - 1], inverse_a))
    payloads.append(spread(jnp.concatenate(sets[far - 1 :], axis=0), "rhs"))
    inverse_b, link_b, extra_b = factor_call(
        far_kernel, "far", energy_shift, potential, (inverse_a, last), payloads[-1:], False
    )
    factors = (inverse_a, inverse_b, link_a, link_b, extra_a, extra_b)
    wave, adjoint, share, gram = solve_all(
        open_channels, factors, target[0], payloads, source_all
    )
    basis_grad = gradient_total(gram, -1.0 / (energies * elements), corr_basis)
    return wave[None, None], adjoint[None, None], share[None], basis_grad


def solution(mesh):
    return jax.shard_map(
        per_device,
        mesh=mesh,
        in_specs=(
            P(("groups", "elem"), None, None),
            P(("groups", "elem"), None),
            P(("groups", "elem"), None, None),
            P(("groups", "elem")),
            P("groups", None),
            P(("groups", "elem"), None, None),
            P(("groups", "energy")),
            P(("groups", "energy"), "elem", None, "rhs"),
            P(("groups", "energy"), None, "rhs"),
            P(("groups", "energy")),
        ),
        out_specs=(
            P(("groups", "energy"), "elem", None, "rhs"),
            P(("groups", "energy"), "elem", None, "rhs"),
            P(("groups", "energy"), "elem", "rhs"),
            P("groups", None),
        ),
        check_vma=False,
    )
```

```python
import functools

import jax
import jax.numpy as jnp
from jax import lax
from jax.experimental import pallas as pl
from jax.experimental.pallas import tpu as pltpu
from jax.sharding import PartitionSpec as P

PENALTY = 0.5
START_SCALE = 0.95
SLOW_SCALE = 1.75
RESIDUAL_BOUND = 0.01
F32 = jnp.float32
BF16 = jnp.bfloat16
NN = (((1,), (0,)), ((), ()))
NT = (((1,), (1,)), ((), ()))
VMEM_BYTES = 48 * 1024 * 1024
PACK_BYTES = 60 * 1024 * 1024


def split(value):
    high = value.astype(BF16)
    return high, (value - high.astype(F32)).astype(BF16)


def dot1(lhs, rhs, dims=NN):
    return lax.dot_general(lhs, rhs, dims, preferred_element_type=F32)


def dot3(lhs, rhs, dims=NN):
    return (
        dot1(lhs[0], rhs[0], dims) + dot1(lhs[0], rhs[1], dims) + dot1(lhs[1], rhs[0], dims)
    )


def eye_of(size):
    rows = lax.broadcasted_iota(jnp.int32, (size, size), 0)
    columns = lax.broadcasted_iota(jnp.int32, (size, size), 1)
    return (rows == columns).astype(F32)


def row_norm(matrix):
    return jnp.max(jnp.sum(jnp.abs(matrix), axis=1, keepdims=True), axis=0, keepdims=True)


def fast_inverse(matrix, identity, steps):
    diagonal = matrix * identity
    by_row = START_SCALE / jnp.sum(diagonal, axis=1, keepdims=True)
    by_column = START_SCALE / jnp.sum(diagonal, axis=0, keepdims=True)
    error = identity - by_row * matrix
    inverse = (identity + error) * by_column
    error16 = error.astype(BF16)
    for _ in range(steps):
        error16 = dot1(error16, error16).astype(BF16)
        inverse = inverse + dot1(error16, inverse.astype(BF16))
    return inverse, identity - dot3(split(matrix), split(inverse))


def exact_dot(lhs, rhs):
    return lax.dot_general(
        lhs, rhs, NN, precision=lax.Precision.HIGHEST, preferred_element_type=F32
    )


def slow_inverse(matrix, identity, steps, matrix_scr, inverse_scr):
    matrix_scr[...] = matrix
    inverse_scr[...] = identity * (SLOW_SCALE / row_norm(matrix))

    def going(state):
        count, size = state
        return (size > 1e-3) & (count < 100)

    def step(state):
        count, _ = state
        inverse = inverse_scr[...]
        residual = identity - exact_dot(matrix_scr[...], inverse)
        inverse_scr[...] = inverse + exact_dot(inverse, residual)
        return count + 1, jnp.max(row_norm(residual))

    lax.while_loop(going, step, (jnp.int32(0), jnp.float32(1e9)))
    return inverse_scr[...], None


def correct(product, residual16):
    if residual16 is None:
        return product
    return product + dot1(product.astype(BF16), residual16)


def pack_symmetric(matrix):
    half = matrix.shape[0] // 2
    rows = lax.broadcasted_iota(jnp.int32, (half, half), 0)
    columns = lax.broadcasted_iota(jnp.int32, (half, half), 1)
    first, second = matrix[:half, :half], matrix[half:, half:]
    mixed = jnp.where(rows > columns, first, jnp.where(rows < columns, second, 0.0))
    return jnp.concatenate([matrix[half:, :half], mixed], axis=1)


def unpack_symmetric(packed):
    half = packed.shape[0]
    rows = lax.broadcasted_iota(jnp.int32, (half, half), 0)
    columns = lax.broadcasted_iota(jnp.int32, (half, half), 1)
    corner, mixed = packed[:, :half], packed[:, half:]
    first = jnp.where(rows > columns, mixed, 0.0)
    second = jnp.where(rows < columns, mixed, 0.0)
    return jnp.concatenate(
        [
            jnp.concatenate([first + first.T, corner.T], axis=1),
            jnp.concatenate([corner, second + second.T], axis=1),
        ],
        axis=0,
    )


def diagonal_of(matrix):
    return jnp.sum(matrix * eye_of(matrix.shape[0]), axis=0, keepdims=True)


def extra_rows(ham, level, weight):
    row = lax.broadcasted_iota(jnp.int32, (8, ham.shape[1]), 0)
    return jnp.where(row == 0, diagonal_of(ham) + level + 2.0, weight)


def quarter_index():
    return lax.axis_index("rhs") * lax.axis_size("energy") + lax.axis_index("energy")


def pack_part_kernel(
    weight_ref, level_hbm, ham_hbm, coupling_hbm, projector_hbm, out_ref, ham_ref, pack_scr,
    level_ref, sems,
):
    part = (out_ref.shape[0] - 8) * 2 // 5
    half = part // 2
    index = quarter_index()
    rows = pl.ds(pl.multiple_of(index * part, 8), part)
    copies = [
        pltpu.make_async_copy(source, target, sems.at[number])
        for number, (source, target) in enumerate(
            (
                (ham_hbm.at[0], ham_ref),
                (level_hbm, level_ref),
                (coupling_hbm.at[0, rows], out_ref.at[half : half + part]),
                (projector_hbm.at[0, rows], out_ref.at[half + part : half + 2 * part]),
            )
        )
    ]
    for copy in copies:
        copy.start()
    copies[0].wait()
    copies[1].wait()
    ham = 0.5 * (ham_ref[...] + ham_ref[...].T)
    pack_scr[...] = pack_symmetric(ham)
    out_ref[:half] = pack_scr[pl.ds(pl.multiple_of(index * half, 8), half), :]
    out_ref[half + 2 * part :] = extra_rows(ham, level_ref[...], weight_ref[0])
    copies[2].wait()
    copies[3].wait()


def pack_part(weight, level, ham, coupling, projector, parts):
    size = ham.shape[1]
    part = size // parts
    smem = pl.BlockSpec(memory_space=pltpu.SMEM)
    vmem = pl.BlockSpec(memory_space=pltpu.VMEM)
    anywhere = pl.BlockSpec(memory_space=pl.ANY)
    height = part // 2 + 2 * part + 8
    return pl.pallas_call(
        pack_part_kernel,
        out_shape=jax.ShapeDtypeStruct((height, size), F32),
        in_specs=[smem] + [anywhere] * 4,
        out_specs=vmem,
        scratch_shapes=[
            pltpu.VMEM((size, size), F32),
            pltpu.VMEM((size // 2, size), F32),
            pltpu.VMEM((1, size), F32),
            pltpu.SemaphoreType.DMA((4,)),
        ],
        compiler_params=pltpu.CompilerParams(vmem_limit_bytes=PACK_BYTES),
        name="pack_part",
    )(weight, level, ham, coupling, projector)


def pack_kernel(weight_ref, level_ref, ham_ref, coupling_ref, projector_ref, whole_ref):
    parts = whole_ref.shape[0]
    size = ham_ref.shape[1]
    part = size // parts
    half = part // 2
    ham = 0.5 * (ham_ref[0] + ham_ref[0].T)
    packed = pack_symmetric(ham)
    extra = extra_rows(ham, level_ref[...], weight_ref[0])
    for n in range(parts):
        rows = slice(n * part, (n + 1) * part)
        whole_ref[n, :half] = packed[n * half : (n + 1) * half]
        whole_ref[n, half : half + part] = coupling_ref[0, rows]
        whole_ref[n, half + part : half + 2 * part] = projector_ref[0, rows]
        whole_ref[n, half + 2 * part :] = extra


def pack(weight, level, ham, coupling, projector, parts):
    size = ham.shape[1]
    part = size // parts
    smem = pl.BlockSpec(memory_space=pltpu.SMEM)
    vmem = pl.BlockSpec(memory_space=pltpu.VMEM)
    return pl.pallas_call(
        pack_kernel,
        out_shape=jax.ShapeDtypeStruct((parts, part // 2 + 2 * part + 8, size), F32),
        in_specs=[smem] + [vmem] * 4,
        out_specs=vmem,
        compiler_params=pltpu.CompilerParams(vmem_limit_bytes=VMEM_BYTES),
        name="pack",
    )(weight, level, ham, coupling, projector)


def potential_kernel(basis_ref, out_ref):
    basis = split(basis_ref[...])
    out_ref[...] = dot3(basis, basis, NT)


def potential_of(basis):
    vmem = pl.BlockSpec(memory_space=pltpu.VMEM)
    return pl.pallas_call(
        potential_kernel,
        out_shape=jax.ShapeDtypeStruct((basis.shape[0],) * 2, F32),
        in_specs=[vmem],
        out_specs=vmem,
        compiler_params=pltpu.CompilerParams(vmem_limit_bytes=VMEM_BYTES),
        name="potential",
    )(basis)


def pieces(refs):
    element, quarter = lax.axis_index("elem"), quarter_index()
    for j in range(refs[0].shape[1]):
        yield element, j, refs[0].at[0, j]
        step = 1
        for ref in refs[1:]:
            for k in range(ref.shape[0]):
                yield element ^ (step + k), quarter ^ j, ref.at[k, j]
            step = step + ref.shape[0]


def factor_kernel(groups, shift_ref, potential_ref, *rest):
    refs, rest = rest[:groups], rest[groups:]
    inverse_ref, link_ref, extra_ref, diag_scr, coupling_ref, pack_scr, *scratch = rest
    matrix_scr, inverse_scr = scratch
    count = extra_ref.shape[0]
    size = potential_ref.shape[0]
    part = size // refs[0].shape[1]
    half = part // 2
    middle = count // 2
    identity = eye_of(size)
    potential = potential_ref[...]
    for element, index, ref in pieces(refs):
        start = pl.multiple_of(index * half, 8)
        pack_scr[element, pl.ds(start, half), :] = ref[:half]
        start = pl.multiple_of(index * part, 8)
        coupling_ref[element, pl.ds(start, part), :] = ref[half : half + part]
        extra_ref[element] = ref[half + 2 * part :]
    for n in range(count):
        diag_scr[n] = (
            unpack_symmetric(pack_scr[n])
            + (extra_ref[n, 0:1] + shift_ref[0]) * identity
            + extra_ref[n, 1:2, :1] * potential
        )

    def eliminate(invert):
        worst = jnp.zeros((1, 1), F32)
        forward = diag_scr[0]
        backward = diag_scr[count - 1]

        def finish(n, matrix, worst):
            inverse, residual = invert(matrix, identity, 2 if n == middle else 1)
            residual16 = None
            if residual is not None:
                worst = jnp.maximum(worst, row_norm(residual))
                residual16 = residual.astype(BF16)
            final = split(correct(inverse, residual16))
            inverse_ref[0, n] = final[0]
            inverse_ref[1, n] = final[1]
            return split(inverse), residual16, worst

        def connect(n, coupling, inverse, residual16):
            parts = split(correct(dot3(coupling, inverse), residual16))
            link_ref[0, n] = parts[0]
            link_ref[1, n] = parts[1]
            return parts

        meeting = diag_scr[middle]
        for step in range(max(middle, count - 1 - middle)):
            ahead, behind = step, count - 1 - step
            if ahead < middle:
                parts, residual16, worst = finish(ahead, forward, worst)
                coupling = split(-(identity + coupling_ref[ahead + 1]))
                link = connect(ahead + 1, coupling, parts, residual16)
                update = dot3(link, coupling, NT)
                if ahead + 1 < middle:
                    forward = diag_scr[ahead + 1] - update
                else:
                    meeting = meeting - update
            if behind > middle:
                parts, residual16, worst = finish(behind, backward, worst)
                raw = -(identity + coupling_ref[behind])
                link = connect(behind, split(raw.T), parts, residual16)
                update = dot3(link, split(raw))
                if behind - 1 > middle:
                    backward = diag_scr[behind - 1] - update
                else:
                    meeting = meeting - update
        _, _, worst = finish(middle, meeting, worst)
        return worst

    worst = jnp.max(eliminate(fast_inverse))

    @pl.when(jnp.logical_not(worst <= RESIDUAL_BOUND))
    def _():
        eliminate(
            functools.partial(slow_inverse, matrix_scr=matrix_scr, inverse_scr=inverse_scr)
        )


def factorize(shift, potential, payloads):
    count, size = sum(value.shape[0] for value in payloads), potential.shape[0]
    smem = pl.BlockSpec(memory_space=pltpu.SMEM)
    vmem = pl.BlockSpec(memory_space=pltpu.VMEM)
    half = jax.ShapeDtypeStruct((2, count, size, size), BF16)
    return pl.pallas_call(
        functools.partial(factor_kernel, len(payloads)),
        out_shape=(half, half, jax.ShapeDtypeStruct((count, 8, size), F32)),
        in_specs=[smem] + [vmem] * (1 + len(payloads)),
        out_specs=(vmem, vmem, vmem),
        scratch_shapes=[
            pltpu.VMEM((count, size, size), F32),
            pltpu.VMEM((count, size, size), F32),
            pltpu.VMEM((count, size // 2, size), F32),
            pltpu.VMEM((size, size), F32),
            pltpu.VMEM((size, size), F32),
        ],
        compiler_params=pltpu.CompilerParams(vmem_limit_bytes=VMEM_BYTES),
        name="factorize",
    )(shift, potential, *payloads)


def load_factors(inverse_ref, link_ref):
    count = inverse_ref.shape[1]
    inverses = [(inverse_ref[0, n], inverse_ref[1, n]) for n in range(count)]
    links = [(link_ref[0, n], link_ref[1, n]) if n != 0 else None for n in range(count)]
    return inverses, links


def solve_blocks(blocks, inverses, links):
    count = len(blocks)
    middle = count // 2
    reduced = list(blocks)
    for n in range(1, middle + 1):
        reduced[n] = reduced[n] - dot3(split(reduced[n - 1]), links[n], NT)
    for n in range(count - 1, middle, -1):
        reduced[n - 1] = reduced[n - 1] - dot3(split(reduced[n]), links[n], NT)
    solved = [dot3(split(reduced[n]), inverses[n]) for n in range(count)]
    for n in range(middle, 0, -1):
        solved[n - 1] = solved[n - 1] - dot3(split(solved[n]), links[n])
    for n in range(middle + 1, count):
        solved[n] = solved[n] - dot3(split(solved[n - 1]), links[n])
    return solved


def solve_kernel(
    groups, open_ref, inverse_ref, link_ref, extra_ref, target_ref, *rest
):
    count = inverse_ref.shape[1]
    refs, rest = rest[:groups], rest[groups:]
    *source_refs, wave_ref, adjoint_ref, share_ref, gram_ref, own_scr, k_scr, projector_scr = rest
    channels, width = source_refs[0].shape[1:]
    me, column = lax.axis_index("elem"), lax.axis_index("rhs")
    part = channels // refs[0].shape[1]
    begin = part // 2 + part
    for element, index, ref in pieces(refs):
        start = pl.multiple_of(index * part, 8)
        projector_scr[element, pl.ds(start, part), :] = ref[begin : begin + part]
    order, distance = [0], count // 2
    while distance:
        order = order + [n ^ distance for n in order]
        distance = distance // 2
    for place, n in enumerate(order):
        half = source_refs[0].shape[0]
        own_scr[me ^ n] = source_refs[place // half][place % half]
    inverses, links = load_factors(inverse_ref, link_ref)
    projectors = [split(projector_scr[n]) for n in range(count)]
    wave = solve_blocks([own_scr[n].T for n in range(count)], inverses, links)
    k_total = dot3(split(wave[0]), projectors[0])
    for n in range(1, count):
        k_total = k_total + dot3(split(wave[n]), projectors[n])
    k_rows = lax.broadcasted_iota(jnp.int32, k_total.shape, 1)
    k_columns = lax.broadcasted_iota(jnp.int32, k_total.shape, 0) + column * width
    opened = (k_rows < open_ref[0]) & (k_columns < open_ref[0])
    residual = split(jnp.where(opened, k_total - target_ref[...].T, 0.0))
    drive = [PENALTY * wave[n] + dot3(residual, projectors[n], NT) for n in range(count)]
    adjoint = [value.T for value in solve_blocks(drive, inverses, links)]
    wave = [value.T for value in wave]

    share = share_ref.shape[0]
    k_scr[...] = k_total.T
    share_ref[...] = k_scr[pl.ds(pl.multiple_of(me * share, share), share), :]
    for n in range(count):
        own_scr[n] = wave[n]
    wave_ref[...] = own_scr[me]
    for n in range(count):
        own_scr[n] = adjoint[n]
    adjoint_ref[...] = own_scr[me]
    weighted = [extra_ref[n, 1:2, :1] * wave[n] for n in range(count)]
    weighted = split(jnp.concatenate(weighted, axis=1))
    gram = dot3(split(jnp.concatenate(adjoint, axis=1)), weighted, NT)
    gram = gram + gram.T
    half = channels // 2
    gram_ref[:half] = pack_symmetric(gram)
    gram_ref[half:] = jnp.broadcast_to(diagonal_of(gram), (8, channels))


def solve_all(opened, inverses, links, extras, target, payloads, sources):
    count, channels, width = inverses.shape[1], *sources[0].shape[1:]
    rows = target.shape[0]
    smem = pl.BlockSpec(memory_space=pltpu.SMEM)
    vmem = pl.BlockSpec(memory_space=pltpu.VMEM)
    return pl.pallas_call(
        functools.partial(solve_kernel, len(payloads)),
        out_shape=(
            jax.ShapeDtypeStruct((channels, width), F32),
            jax.ShapeDtypeStruct((channels, width), F32),
            jax.ShapeDtypeStruct((rows // count, width), F32),
            jax.ShapeDtypeStruct((channels // 2 + 8, channels), F32),
        ),
        in_specs=[smem] + [vmem] * (4 + len(payloads) + len(sources)),
        out_specs=(vmem,) * 4,
        scratch_shapes=[
            pltpu.VMEM((count, channels, width), F32),
            pltpu.VMEM((rows, width), F32),
            pltpu.VMEM((count, channels, channels), F32),
        ],
        compiler_params=pltpu.CompilerParams(vmem_limit_bytes=VMEM_BYTES),
        name="solve",
    )(opened, inverses, links, extras, target, *payloads, *sources)


def gradient_kernel(scale, own_ref, other_ref, basis_ref, out_ref):
    size = basis_ref.shape[0]
    total = own_ref[...] + other_ref[...]
    gram = unpack_symmetric(total[: size // 2])
    gram = gram + total[size // 2 : size // 2 + 1] * eye_of(size)
    out_ref[...] = scale * dot3(split(gram), split(basis_ref[...]))


def gradient(scale, own, other, basis):
    vmem = pl.BlockSpec(memory_space=pltpu.VMEM)
    return pl.pallas_call(
        functools.partial(gradient_kernel, scale),
        out_shape=jax.ShapeDtypeStruct(basis.shape, F32),
        in_specs=[vmem, vmem, vmem],
        out_specs=vmem,
        compiler_params=pltpu.CompilerParams(vmem_limit_bytes=VMEM_BYTES),
        name="gradient",
    )(own, other, basis)


def swap(value, axis, step):
    count = lax.axis_size(axis)
    return lax.ppermute(value, axis, [(i, i ^ step) for i in range(count)])


def gradient_total(gram, scale, basis):
    steps = []
    for axis in ("rhs", "energy"):
        step = 1
        while step < lax.axis_size(axis):
            steps.append((axis, step))
            step = step * 2
    other = jnp.zeros_like(gram)
    for index, (axis, step) in enumerate(steps):
        if index:
            gram = gram + other
        other = swap(gram, axis, step)
    return gradient(scale, gram, other, basis)


def per_device(
    ham_noise,
    channel_levels,
    coupling_noise,
    corr_weight,
    corr_basis,
    projector,
    energy_shift,
    sources,
    target,
    open_channels,
):
    elements, energies, halves = (lax.axis_size(axis) for axis in ("elem", "energy", "rhs"))
    parts = energies * halves
    raw = (corr_weight, channel_levels, ham_noise, coupling_noise, projector)
    mine = pack_part(*raw, parts)
    whole = pack(*raw, parts)
    potential = potential_of(corr_basis)

    def reach(found, step):
        low = step & -step
        return swap(found[step ^ low], "elem", low)

    def spread(payload, axis):
        distance = 1
        while distance < lax.axis_size(axis):
            payload = jnp.concatenate([payload, swap(payload, axis, distance)], axis=1)
            distance = distance * 2
        return payload

    steps = range(1, elements)
    far = elements // 2
    near = {0: mine}
    for step in steps:
        near[step] = reach(near, step)
        if step == 1:
            near[1], whole, potential = lax.optimization_barrier((near[1], whole, potential))
    own, near[far] = lax.optimization_barrier((sources[:, 0], near[far]))
    source_sets = {0: own}
    for step in steps:
        source_sets[step] = reach(source_sets, step)
    sets = [spread(near[step][None, None], "energy") for step in steps]
    sets[0], source_sets[far] = lax.optimization_barrier((sets[0], source_sets[far]))
    groups = [sets[:-1], sets[-1:]] if len(sets) > 1 else [sets]
    payloads = [spread(jnp.concatenate(group, axis=0), "rhs") for group in groups]
    payloads = [whole[None], *payloads]
    order, distance = [0], far
    while distance:
        order = order + [n ^ distance for n in order]
        distance = distance // 2
    source_all = [source_sets[n] for n in order]
    inverses, links, extras = factorize(energy_shift, potential, payloads)
    wave, adjoint, share, gram = solve_all(
        open_channels, inverses, links, extras, target[0], payloads, source_all
    )
    basis_grad = gradient_total(gram, -1.0 / (energies * elements), corr_basis)
    return wave[None, None], adjoint[None, None], share[None], basis_grad


def solution(mesh):
    return jax.shard_map(
        per_device,
        mesh=mesh,
        in_specs=(
            P(("groups", "elem"), None, None),
            P(("groups", "elem"), None),
            P(("groups", "elem"), None, None),
            P(("groups", "elem")),
            P("groups", None),
            P(("groups", "elem"), None, None),
            P(("groups", "energy")),
            P(("groups", "energy"), "elem", None, "rhs"),
            P(("groups", "energy"), None, "rhs"),
            P(("groups", "energy")),
        ),
        out_specs=(
            P(("groups", "energy"), "elem", None, "rhs"),
            P(("groups", "energy"), "elem", None, "rhs"),
            P(("groups", "energy"), "elem", "rhs"),
            P("groups", None),
        ),
        check_vma=False,
    )
```

```python
import functools

import jax
import jax.numpy as jnp
from jax import lax
from jax.experimental import pallas as pl
from jax.experimental.pallas import tpu as pltpu
from jax.sharding import PartitionSpec as P

PENALTY = 0.5
START_SCALE = 0.95
SLOW_SCALE = 1.75
RESIDUAL_BOUND = 0.01
F32 = jnp.float32
BF16 = jnp.bfloat16
NN = (((1,), (0,)), ((), ()))
NT = (((1,), (1,)), ((), ()))
VMEM_BYTES = 48 * 1024 * 1024
PACK_BYTES = 60 * 1024 * 1024


def split(value):
    high = value.astype(BF16)
    return high, (value - high.astype(F32)).astype(BF16)


def dot1(lhs, rhs, dims=NN):
    return lax.dot_general(lhs, rhs, dims, preferred_element_type=F32)


def dot3(lhs, rhs, dims=NN):
    return (
        dot1(lhs[0], rhs[0], dims) + dot1(lhs[0], rhs[1], dims) + dot1(lhs[1], rhs[0], dims)
    )


def eye_of(size):
    rows = lax.broadcasted_iota(jnp.int32, (size, size), 0)
    columns = lax.broadcasted_iota(jnp.int32, (size, size), 1)
    return (rows == columns).astype(F32)


def row_norm(matrix):
    return jnp.max(jnp.sum(jnp.abs(matrix), axis=1, keepdims=True), axis=0, keepdims=True)


def fast_inverse(matrix, identity, steps):
    diagonal = matrix * identity
    by_row = START_SCALE / jnp.sum(diagonal, axis=1, keepdims=True)
    by_column = START_SCALE / jnp.sum(diagonal, axis=0, keepdims=True)
    error = identity - by_row * matrix
    inverse = (identity + error) * by_column
    error16 = error.astype(BF16)
    for _ in range(steps):
        error16 = dot1(error16, error16).astype(BF16)
        inverse = inverse + dot1(error16, inverse.astype(BF16))
    return inverse, identity - dot3(split(matrix), split(inverse))


def exact_dot(lhs, rhs):
    return lax.dot_general(
        lhs, rhs, NN, precision=lax.Precision.HIGHEST, preferred_element_type=F32
    )


def slow_inverse(matrix, identity, steps, matrix_scr, inverse_scr):
    matrix_scr[...] = matrix
    inverse_scr[...] = identity * (SLOW_SCALE / row_norm(matrix))

    def going(state):
        count, size = state
        return (size > 1e-3) & (count < 100)

    def step(state):
        count, _ = state
        inverse = inverse_scr[...]
        residual = identity - exact_dot(matrix_scr[...], inverse)
        inverse_scr[...] = inverse + exact_dot(inverse, residual)
        return count + 1, jnp.max(row_norm(residual))

    lax.while_loop(going, step, (jnp.int32(0), jnp.float32(1e9)))
    return inverse_scr[...], None


def correct(product, residual16):
    if residual16 is None:
        return product
    return product + dot1(product.astype(BF16), residual16)


def pack_symmetric(matrix):
    half = matrix.shape[0] // 2
    rows = lax.broadcasted_iota(jnp.int32, (half, half), 0)
    columns = lax.broadcasted_iota(jnp.int32, (half, half), 1)
    first, second = matrix[:half, :half], matrix[half:, half:]
    mixed = jnp.where(rows > columns, first, jnp.where(rows < columns, second, 0.0))
    return jnp.concatenate([matrix[half:, :half], mixed], axis=1)


def unpack_symmetric(packed):
    half = packed.shape[0]
    rows = lax.broadcasted_iota(jnp.int32, (half, half), 0)
    columns = lax.broadcasted_iota(jnp.int32, (half, half), 1)
    corner, mixed = packed[:, :half], packed[:, half:]
    first = jnp.where(rows > columns, mixed, 0.0)
    second = jnp.where(rows < columns, mixed, 0.0)
    return jnp.concatenate(
        [
            jnp.concatenate([first + first.T, corner.T], axis=1),
            jnp.concatenate([corner, second + second.T], axis=1),
        ],
        axis=0,
    )


def diagonal_of(matrix):
    return jnp.sum(matrix * eye_of(matrix.shape[0]), axis=0, keepdims=True)


def extra_rows(ham, level, weight):
    row = lax.broadcasted_iota(jnp.int32, (8, ham.shape[1]), 0)
    return jnp.where(row == 0, diagonal_of(ham) + level + 2.0, weight)


def quarter_index():
    return lax.axis_index("rhs") * lax.axis_size("energy") + lax.axis_index("energy")


def pack_part_kernel(
    weight_ref, level_hbm, ham_hbm, coupling_hbm, projector_hbm, out_ref, ham_ref, pack_scr,
    level_ref, sems,
):
    part = (out_ref.shape[0] - 8) * 2 // 5
    half = part // 2
    index = quarter_index()
    rows = pl.ds(pl.multiple_of(index * part, 8), part)
    copies = [
        pltpu.make_async_copy(source, target, sems.at[number])
        for number, (source, target) in enumerate(
            (
                (ham_hbm.at[0], ham_ref),
                (level_hbm, level_ref),
                (coupling_hbm.at[0, rows], out_ref.at[half : half + part]),
                (projector_hbm.at[0, rows], out_ref.at[half + part : half + 2 * part]),
            )
        )
    ]
    for copy in copies:
        copy.start()
    copies[0].wait()
    copies[1].wait()
    ham = 0.5 * (ham_ref[...] + ham_ref[...].T)
    pack_scr[...] = pack_symmetric(ham)
    out_ref[:half] = pack_scr[pl.ds(pl.multiple_of(index * half, 8), half), :]
    out_ref[half + 2 * part :] = extra_rows(ham, level_ref[...], weight_ref[0])
    copies[2].wait()
    copies[3].wait()


def pack_part(weight, level, ham, coupling, projector, parts):
    size = ham.shape[1]
    part = size // parts
    smem = pl.BlockSpec(memory_space=pltpu.SMEM)
    vmem = pl.BlockSpec(memory_space=pltpu.VMEM)
    anywhere = pl.BlockSpec(memory_space=pl.ANY)
    height = part // 2 + 2 * part + 8
    return pl.pallas_call(
        pack_part_kernel,
        out_shape=jax.ShapeDtypeStruct((height, size), F32),
        in_specs=[smem] + [anywhere] * 4,
        out_specs=vmem,
        scratch_shapes=[
            pltpu.VMEM((size, size), F32),
            pltpu.VMEM((size // 2, size), F32),
            pltpu.VMEM((1, size), F32),
            pltpu.SemaphoreType.DMA((4,)),
        ],
        compiler_params=pltpu.CompilerParams(vmem_limit_bytes=PACK_BYTES),
        name="pack_part",
    )(weight, level, ham, coupling, projector)


def pack_kernel(weight_ref, level_ref, ham_ref, coupling_ref, projector_ref, whole_ref):
    parts = whole_ref.shape[0]
    size = ham_ref.shape[1]
    part = size // parts
    half = part // 2
    ham = 0.5 * (ham_ref[0] + ham_ref[0].T)
    packed = pack_symmetric(ham)
    extra = extra_rows(ham, level_ref[...], weight_ref[0])
    for n in range(parts):
        rows = slice(n * part, (n + 1) * part)
        whole_ref[n, :half] = packed[n * half : (n + 1) * half]
        whole_ref[n, half : half + part] = coupling_ref[0, rows]
        whole_ref[n, half + part : half + 2 * part] = projector_ref[0, rows]
        whole_ref[n, half + 2 * part :] = extra


def pack(weight, level, ham, coupling, projector, parts):
    size = ham.shape[1]
    part = size // parts
    smem = pl.BlockSpec(memory_space=pltpu.SMEM)
    vmem = pl.BlockSpec(memory_space=pltpu.VMEM)
    return pl.pallas_call(
        pack_kernel,
        out_shape=jax.ShapeDtypeStruct((parts, part // 2 + 2 * part + 8, size), F32),
        in_specs=[smem] + [vmem] * 4,
        out_specs=vmem,
        compiler_params=pltpu.CompilerParams(vmem_limit_bytes=VMEM_BYTES),
        name="pack",
    )(weight, level, ham, coupling, projector)


def potential_kernel(shift_ref, open_ref, basis_ref, out_ref, scalar_ref):
    basis = split(basis_ref[...])
    out_ref[...] = dot3(basis, basis, NT)
    row = lax.broadcasted_iota(jnp.int32, scalar_ref.shape, 0)
    scalar_ref[...] = jnp.where(row == 0, shift_ref[0], open_ref[0].astype(F32))


def potential_of(shift, opened, basis):
    smem = pl.BlockSpec(memory_space=pltpu.SMEM)
    vmem = pl.BlockSpec(memory_space=pltpu.VMEM)
    size = basis.shape[0]
    return pl.pallas_call(
        potential_kernel,
        out_shape=(
            jax.ShapeDtypeStruct((size, size), F32),
            jax.ShapeDtypeStruct((8, size), F32),
        ),
        in_specs=[smem, smem, vmem],
        out_specs=(vmem, vmem),
        compiler_params=pltpu.CompilerParams(vmem_limit_bytes=VMEM_BYTES),
        name="potential",
    )(shift, opened, basis)


def pieces(refs):
    element, quarter = lax.axis_index("elem"), quarter_index()
    for j in range(refs[0].shape[1]):
        yield element, j, refs[0].at[0, j]
        step = 1
        for ref in refs[1:]:
            for k in range(ref.shape[0]):
                yield element ^ (step + k), quarter ^ j, ref.at[k, j]
            step = step + ref.shape[0]


def factor_kernel(groups, scalar_ref, potential_ref, *rest):
    refs, rest = rest[:groups], rest[groups:]
    inverse_ref, link_ref, extra_ref, diag_scr, coupling_ref, pack_scr, *scratch = rest
    matrix_scr, inverse_scr = scratch
    count = extra_ref.shape[0]
    size = potential_ref.shape[0]
    part = size // refs[0].shape[1]
    half = part // 2
    middle = count // 2
    identity = eye_of(size)
    potential = potential_ref[...]
    for element, index, ref in pieces(refs):
        start = pl.multiple_of(index * half, 8)
        pack_scr[element, pl.ds(start, half), :] = ref[:half]
        start = pl.multiple_of(index * part, 8)
        coupling_ref[element, pl.ds(start, part), :] = ref[half : half + part]
        extra_ref[element] = ref[half + 2 * part :]
    for n in range(count):
        diag_scr[n] = (
            unpack_symmetric(pack_scr[n])
            + (extra_ref[n, 0:1] + scalar_ref[0:1]) * identity
            + extra_ref[n, 1:2, :1] * potential
        )

    def eliminate(invert):
        worst = jnp.zeros((1, 1), F32)
        forward = diag_scr[0]
        backward = diag_scr[count - 1]

        def finish(n, matrix, worst):
            inverse, residual = invert(matrix, identity, 2 if n == middle else 1)
            residual16 = None
            if residual is not None:
                worst = jnp.maximum(worst, row_norm(residual))
                residual16 = residual.astype(BF16)
            final = split(correct(inverse, residual16))
            inverse_ref[0, n] = final[0]
            inverse_ref[1, n] = final[1]
            return split(inverse), residual16, worst

        def connect(n, coupling, inverse, residual16):
            parts = split(correct(dot3(coupling, inverse), residual16))
            link_ref[0, n] = parts[0]
            link_ref[1, n] = parts[1]
            return parts

        meeting = diag_scr[middle]
        for step in range(max(middle, count - 1 - middle)):
            ahead, behind = step, count - 1 - step
            if ahead < middle:
                parts, residual16, worst = finish(ahead, forward, worst)
                coupling = split(-(identity + coupling_ref[ahead + 1]))
                link = connect(ahead + 1, coupling, parts, residual16)
                update = dot3(link, coupling, NT)
                if ahead + 1 < middle:
                    forward = diag_scr[ahead + 1] - update
                else:
                    meeting = meeting - update
            if behind > middle:
                parts, residual16, worst = finish(behind, backward, worst)
                raw = -(identity + coupling_ref[behind])
                link = connect(behind, split(raw.T), parts, residual16)
                update = dot3(link, split(raw))
                if behind - 1 > middle:
                    backward = diag_scr[behind - 1] - update
                else:
                    meeting = meeting - update
        _, _, worst = finish(middle, meeting, worst)
        return worst

    worst = jnp.max(eliminate(fast_inverse))

    @pl.when(jnp.logical_not(worst <= RESIDUAL_BOUND))
    def _():
        eliminate(
            functools.partial(slow_inverse, matrix_scr=matrix_scr, inverse_scr=inverse_scr)
        )


def factorize(scalars, potential, payloads):
    count, size = sum(value.shape[0] for value in payloads), potential.shape[0]
    vmem = pl.BlockSpec(memory_space=pltpu.VMEM)
    half = jax.ShapeDtypeStruct((2, count, size, size), BF16)
    return pl.pallas_call(
        functools.partial(factor_kernel, len(payloads)),
        out_shape=(half, half, jax.ShapeDtypeStruct((count, 8, size), F32)),
        in_specs=[vmem] * (2 + len(payloads)),
        out_specs=(vmem, vmem, vmem),
        scratch_shapes=[
            pltpu.VMEM((count, size, size), F32),
            pltpu.VMEM((count, size, size), F32),
            pltpu.VMEM((count, size // 2, size), F32),
            pltpu.VMEM((size, size), F32),
            pltpu.VMEM((size, size), F32),
        ],
        compiler_params=pltpu.CompilerParams(vmem_limit_bytes=VMEM_BYTES),
        name="factorize",
    )(scalars, potential, *payloads)


def load_factors(inverse_ref, link_ref):
    count = inverse_ref.shape[1]
    inverses = [(inverse_ref[0, n], inverse_ref[1, n]) for n in range(count)]
    links = [(link_ref[0, n], link_ref[1, n]) if n != 0 else None for n in range(count)]
    return inverses, links


def solve_blocks(blocks, inverses, links):
    count = len(blocks)
    middle = count // 2
    reduced = list(blocks)
    for n in range(1, middle + 1):
        reduced[n] = reduced[n] - dot3(split(reduced[n - 1]), links[n], NT)
    for n in range(count - 1, middle, -1):
        reduced[n - 1] = reduced[n - 1] - dot3(split(reduced[n]), links[n], NT)
    solved = [dot3(split(reduced[n]), inverses[n]) for n in range(count)]
    for n in range(middle, 0, -1):
        solved[n - 1] = solved[n - 1] - dot3(split(solved[n]), links[n])
    for n in range(middle + 1, count):
        solved[n] = solved[n] - dot3(split(solved[n - 1]), links[n])
    return solved


def solve_kernel(
    groups, scalar_ref, inverse_ref, link_ref, extra_ref, target_ref, *rest
):
    count = inverse_ref.shape[1]
    refs, rest = rest[:groups], rest[groups:]
    *source_refs, wave_ref, adjoint_ref, share_ref, gram_ref, own_scr, k_scr, projector_scr = rest
    channels, width = source_refs[0].shape[1:]
    me, column = lax.axis_index("elem"), lax.axis_index("rhs")
    part = channels // refs[0].shape[1]
    begin = part // 2 + part
    for element, index, ref in pieces(refs):
        start = pl.multiple_of(index * part, 8)
        projector_scr[element, pl.ds(start, part), :] = ref[begin : begin + part]
    order, distance = [0], count // 2
    while distance:
        order = order + [n ^ distance for n in order]
        distance = distance // 2
    for place, n in enumerate(order):
        half = source_refs[0].shape[0]
        own_scr[me ^ n] = source_refs[place // half][place % half]
    inverses, links = load_factors(inverse_ref, link_ref)
    projectors = [split(projector_scr[n]) for n in range(count)]
    wave = solve_blocks([own_scr[n].T for n in range(count)], inverses, links)
    k_total = dot3(split(wave[0]), projectors[0])
    for n in range(1, count):
        k_total = k_total + dot3(split(wave[n]), projectors[n])
    k_rows = lax.broadcasted_iota(jnp.int32, k_total.shape, 1)
    k_columns = lax.broadcasted_iota(jnp.int32, k_total.shape, 0) + column * width
    limit = scalar_ref[1:2, :1]
    opened = (k_rows.astype(F32) < limit) & (k_columns.astype(F32) < limit)
    residual = split(jnp.where(opened, k_total - target_ref[...].T, 0.0))
    drive = [PENALTY * wave[n] + dot3(residual, projectors[n], NT) for n in range(count)]
    adjoint = [value.T for value in solve_blocks(drive, inverses, links)]
    wave = [value.T for value in wave]

    share = share_ref.shape[0]
    k_scr[...] = k_total.T
    share_ref[...] = k_scr[pl.ds(pl.multiple_of(me * share, share), share), :]
    for n in range(count):
        own_scr[n] = wave[n]
    wave_ref[...] = own_scr[me]
    for n in range(count):
        own_scr[n] = adjoint[n]
    adjoint_ref[...] = own_scr[me]
    weighted = [extra_ref[n, 1:2, :1] * wave[n] for n in range(count)]
    weighted = split(jnp.concatenate(weighted, axis=1))
    gram = dot3(split(jnp.concatenate(adjoint, axis=1)), weighted, NT)
    gram = gram + gram.T
    half = channels // 2
    gram_ref[:half] = pack_symmetric(gram)
    gram_ref[half:] = jnp.broadcast_to(diagonal_of(gram), (8, channels))


def solve_all(scalars, inverses, links, extras, target, payloads, sources):
    count, channels, width = inverses.shape[1], *sources[0].shape[1:]
    rows = target.shape[0]
    vmem = pl.BlockSpec(memory_space=pltpu.VMEM)
    return pl.pallas_call(
        functools.partial(solve_kernel, len(payloads)),
        out_shape=(
            jax.ShapeDtypeStruct((channels, width), F32),
            jax.ShapeDtypeStruct((channels, width), F32),
            jax.ShapeDtypeStruct((rows // count, width), F32),
            jax.ShapeDtypeStruct((channels // 2 + 8, channels), F32),
        ),
        in_specs=[vmem] * (5 + len(payloads) + len(sources)),
        out_specs=(vmem,) * 4,
        scratch_shapes=[
            pltpu.VMEM((count, channels, width), F32),
            pltpu.VMEM((rows, width), F32),
            pltpu.VMEM((count, channels, channels), F32),
        ],
        compiler_params=pltpu.CompilerParams(vmem_limit_bytes=VMEM_BYTES),
        name="solve",
    )(scalars, inverses, links, extras, target, *payloads, *sources)


def gradient_kernel(scale, own_ref, other_ref, basis_ref, out_ref):
    size = basis_ref.shape[0]
    total = own_ref[...] + other_ref[...]
    gram = unpack_symmetric(total[: size // 2])
    gram = gram + total[size // 2 : size // 2 + 1] * eye_of(size)
    out_ref[...] = scale * dot3(split(gram), split(basis_ref[...]))


def gradient(scale, own, other, basis):
    vmem = pl.BlockSpec(memory_space=pltpu.VMEM)
    return pl.pallas_call(
        functools.partial(gradient_kernel, scale),
        out_shape=jax.ShapeDtypeStruct(basis.shape, F32),
        in_specs=[vmem, vmem, vmem],
        out_specs=vmem,
        compiler_params=pltpu.CompilerParams(vmem_limit_bytes=VMEM_BYTES),
        name="gradient",
    )(own, other, basis)


def swap(value, axis, step):
    count = lax.axis_size(axis)
    return lax.ppermute(value, axis, [(i, i ^ step) for i in range(count)])


def gradient_total(gram, scale, basis):
    steps = []
    for axis in ("rhs", "energy"):
        step = 1
        while step < lax.axis_size(axis):
            steps.append((axis, step))
            step = step * 2
    other = jnp.zeros_like(gram)
    for index, (axis, step) in enumerate(steps):
        if index:
            gram = gram + other
        other = swap(gram, axis, step)
    return gradient(scale, gram, other, basis)


def per_device(
    ham_noise,
    channel_levels,
    coupling_noise,
    corr_weight,
    corr_basis,
    projector,
    energy_shift,
    sources,
    target,
    open_channels,
):
    elements, energies, halves = (lax.axis_size(axis) for axis in ("elem", "energy", "rhs"))
    parts = energies * halves
    raw = (corr_weight, channel_levels, ham_noise, coupling_noise, projector)
    mine = pack_part(*raw, parts)
    whole = pack(*raw, parts)
    potential, scalars = potential_of(energy_shift, open_channels, corr_basis)

    def reach(found, step):
        low = step & -step
        return swap(found[step ^ low], "elem", low)

    def spread(payload, axis):
        distance = 1
        while distance < lax.axis_size(axis):
            payload = jnp.concatenate([payload, swap(payload, axis, distance)], axis=1)
            distance = distance * 2
        return payload

    steps = range(1, elements)
    far = elements // 2
    near = {0: mine}
    for step in steps:
        near[step] = reach(near, step)
        if step == 1:
            near[1], whole, potential = lax.optimization_barrier((near[1], whole, potential))
    own, near[far] = lax.optimization_barrier((sources[:, 0], near[far]))
    late, near[elements - 1] = lax.optimization_barrier((own, near[elements - 1]))
    source_sets = {0: own, 1: swap(late, "elem", 1)}
    for step in steps[1:]:
        source_sets[step] = reach(source_sets, step)
    sets = [spread(near[step][None, None], "energy") for step in steps]
    sets[0], source_sets[1], source_sets[far] = lax.optimization_barrier(
        (sets[0], source_sets[1], source_sets[far])
    )
    groups = [sets[:-1], sets[-1:]] if len(sets) > 1 else [sets]
    payloads = [spread(jnp.concatenate(group, axis=0), "rhs") for group in groups]
    payloads = [whole[None], *payloads]
    order, distance = [0], far
    while distance:
        order = order + [n ^ distance for n in order]
        distance = distance // 2
    source_all = [source_sets[n] for n in order]
    inverses, links, extras = factorize(scalars, potential, payloads)
    wave, adjoint, share, gram = solve_all(
        scalars, inverses, links, extras, target[0], payloads, source_all
    )
    basis_grad = gradient_total(gram, -1.0 / (energies * elements), corr_basis)
    return wave[None, None], adjoint[None, None], share[None], basis_grad


def solution(mesh):
    return jax.shard_map(
        per_device,
        mesh=mesh,
        in_specs=(
            P(("groups", "elem"), None, None),
            P(("groups", "elem"), None),
            P(("groups", "elem"), None, None),
            P(("groups", "elem")),
            P("groups", None),
            P(("groups", "elem"), None, None),
            P(("groups", "energy")),
            P(("groups", "energy"), "elem", None, "rhs"),
            P(("groups", "energy"), None, "rhs"),
            P(("groups", "energy")),
        ),
        out_specs=(
            P(("groups", "energy"), "elem", None, "rhs"),
            P(("groups", "energy"), "elem", None, "rhs"),
            P(("groups", "energy"), "elem", "rhs"),
            P("groups", None),
        ),
        check_vma=False,
    )
```

```python
import functools

import jax
import jax.numpy as jnp
from jax import lax
from jax.experimental import pallas as pl
from jax.experimental.pallas import tpu as pltpu
from jax.sharding import PartitionSpec as P

PENALTY = 0.5
START_SCALE = 0.95
SLOW_SCALE = 1.75
RESIDUAL_BOUND = 0.01
F32 = jnp.float32
BF16 = jnp.bfloat16
NN = (((1,), (0,)), ((), ()))
NT = (((1,), (1,)), ((), ()))
VMEM_BYTES = 48 * 1024 * 1024
PACK_BYTES = 60 * 1024 * 1024


def split(value):
    high = value.astype(BF16)
    return high, (value - high.astype(F32)).astype(BF16)


def dot1(lhs, rhs, dims=NN):
    return lax.dot_general(lhs, rhs, dims, preferred_element_type=F32)


def dot3(lhs, rhs, dims=NN):
    return (
        dot1(lhs[0], rhs[0], dims) + dot1(lhs[0], rhs[1], dims) + dot1(lhs[1], rhs[0], dims)
    )


def eye_of(size):
    rows = lax.broadcasted_iota(jnp.int32, (size, size), 0)
    columns = lax.broadcasted_iota(jnp.int32, (size, size), 1)
    return (rows == columns).astype(F32)


def row_norm(matrix):
    return jnp.max(jnp.sum(jnp.abs(matrix), axis=1, keepdims=True), axis=0, keepdims=True)


def fast_inverse(matrix, identity, steps):
    diagonal = matrix * identity
    by_row = START_SCALE / jnp.sum(diagonal, axis=1, keepdims=True)
    by_column = START_SCALE / jnp.sum(diagonal, axis=0, keepdims=True)
    error = identity - by_row * matrix
    inverse = (identity + error) * by_column
    error16 = error.astype(BF16)
    for _ in range(steps):
        error16 = dot1(error16, error16).astype(BF16)
        inverse = inverse + dot1(error16, inverse.astype(BF16))
    return inverse, identity - dot3(split(matrix), split(inverse))


def exact_dot(lhs, rhs):
    return lax.dot_general(
        lhs, rhs, NN, precision=lax.Precision.HIGHEST, preferred_element_type=F32
    )


def slow_inverse(matrix, identity, steps, matrix_scr, inverse_scr):
    matrix_scr[...] = matrix
    inverse_scr[...] = identity * (SLOW_SCALE / row_norm(matrix))

    def going(state):
        count, size = state
        return (size > 1e-3) & (count < 100)

    def step(state):
        count, _ = state
        inverse = inverse_scr[...]
        residual = identity - exact_dot(matrix_scr[...], inverse)
        inverse_scr[...] = inverse + exact_dot(inverse, residual)
        return count + 1, jnp.max(row_norm(residual))

    lax.while_loop(going, step, (jnp.int32(0), jnp.float32(1e9)))
    return inverse_scr[...], None


def correct(product, residual16):
    if residual16 is None:
        return product
    return product + dot1(product.astype(BF16), residual16)


def pack_symmetric(matrix):
    half = matrix.shape[0] // 2
    rows = lax.broadcasted_iota(jnp.int32, (half, half), 0)
    columns = lax.broadcasted_iota(jnp.int32, (half, half), 1)
    first, second = matrix[:half, :half], matrix[half:, half:]
    mixed = jnp.where(rows > columns, first, jnp.where(rows < columns, second, 0.0))
    return jnp.concatenate([matrix[half:, :half], mixed], axis=1)


def unpack_symmetric(packed):
    half = packed.shape[0]
    rows = lax.broadcasted_iota(jnp.int32, (half, half), 0)
    columns = lax.broadcasted_iota(jnp.int32, (half, half), 1)
    corner, mixed = packed[:, :half], packed[:, half:]
    first = jnp.where(rows > columns, mixed, 0.0)
    second = jnp.where(rows < columns, mixed, 0.0)
    return jnp.concatenate(
        [
            jnp.concatenate([first + first.T, corner.T], axis=1),
            jnp.concatenate([corner, second + second.T], axis=1),
        ],
        axis=0,
    )


def diagonal_of(matrix):
    return jnp.sum(matrix * eye_of(matrix.shape[0]), axis=0, keepdims=True)


def extra_rows(ham, level, weight):
    row = lax.broadcasted_iota(jnp.int32, (8, ham.shape[1]), 0)
    return jnp.where(row == 0, diagonal_of(ham) + level + 2.0, weight)


def quarter_index():
    return lax.axis_index("rhs") * lax.axis_size("energy") + lax.axis_index("energy")


def pack_part_kernel(
    weight_ref, level_hbm, ham_hbm, coupling_hbm, projector_hbm, out_ref, ham_ref, pack_scr,
    level_ref, sems,
):
    part = (out_ref.shape[0] - 8) * 2 // 5
    half = part // 2
    index = quarter_index()
    rows = pl.ds(pl.multiple_of(index * part, 8), part)
    copies = [
        pltpu.make_async_copy(source, target, sems.at[number])
        for number, (source, target) in enumerate(
            (
                (ham_hbm.at[0], ham_ref),
                (level_hbm, level_ref),
                (coupling_hbm.at[0, rows], out_ref.at[half : half + part]),
                (projector_hbm.at[0, rows], out_ref.at[half + part : half + 2 * part]),
            )
        )
    ]
    for copy in copies:
        copy.start()
    copies[0].wait()
    copies[1].wait()
    ham = 0.5 * (ham_ref[...] + ham_ref[...].T)
    pack_scr[...] = pack_symmetric(ham)
    out_ref[:half] = pack_scr[pl.ds(pl.multiple_of(index * half, 8), half), :]
    out_ref[half + 2 * part :] = extra_rows(ham, level_ref[...], weight_ref[0])
    copies[2].wait()
    copies[3].wait()


def pack_part(weight, level, ham, coupling, projector, parts):
    size = ham.shape[1]
    part = size // parts
    smem = pl.BlockSpec(memory_space=pltpu.SMEM)
    vmem = pl.BlockSpec(memory_space=pltpu.VMEM)
    anywhere = pl.BlockSpec(memory_space=pl.ANY)
    height = part // 2 + 2 * part + 8
    return pl.pallas_call(
        pack_part_kernel,
        out_shape=jax.ShapeDtypeStruct((height, size), F32),
        in_specs=[smem] + [anywhere] * 4,
        out_specs=vmem,
        scratch_shapes=[
            pltpu.VMEM((size, size), F32),
            pltpu.VMEM((size // 2, size), F32),
            pltpu.VMEM((1, size), F32),
            pltpu.SemaphoreType.DMA((4,)),
        ],
        compiler_params=pltpu.CompilerParams(vmem_limit_bytes=PACK_BYTES),
        name="pack_part",
    )(weight, level, ham, coupling, projector)


def pack_kernel(weight_ref, level_ref, ham_ref, coupling_ref, projector_ref, whole_ref):
    parts = whole_ref.shape[0]
    size = ham_ref.shape[1]
    part = size // parts
    half = part // 2
    ham = 0.5 * (ham_ref[0] + ham_ref[0].T)
    packed = pack_symmetric(ham)
    extra = extra_rows(ham, level_ref[...], weight_ref[0])
    for n in range(parts):
        rows = slice(n * part, (n + 1) * part)
        whole_ref[n, :half] = packed[n * half : (n + 1) * half]
        whole_ref[n, half : half + part] = coupling_ref[0, rows]
        whole_ref[n, half + part : half + 2 * part] = projector_ref[0, rows]
        whole_ref[n, half + 2 * part :] = extra


def pack(weight, level, ham, coupling, projector, parts):
    size = ham.shape[1]
    part = size // parts
    smem = pl.BlockSpec(memory_space=pltpu.SMEM)
    vmem = pl.BlockSpec(memory_space=pltpu.VMEM)
    return pl.pallas_call(
        pack_kernel,
        out_shape=jax.ShapeDtypeStruct((parts, part // 2 + 2 * part + 8, size), F32),
        in_specs=[smem] + [vmem] * 4,
        out_specs=vmem,
        compiler_params=pltpu.CompilerParams(vmem_limit_bytes=VMEM_BYTES),
        name="pack",
    )(weight, level, ham, coupling, projector)


def potential_kernel(shift_ref, open_ref, basis_ref, out_ref, scalar_ref):
    basis = split(basis_ref[...])
    out_ref[...] = dot3(basis, basis, NT)
    row = lax.broadcasted_iota(jnp.int32, scalar_ref.shape, 0)
    scalar_ref[...] = jnp.where(row == 0, shift_ref[0], open_ref[0].astype(F32))


def potential_of(shift, opened, basis):
    smem = pl.BlockSpec(memory_space=pltpu.SMEM)
    vmem = pl.BlockSpec(memory_space=pltpu.VMEM)
    size = basis.shape[0]
    return pl.pallas_call(
        potential_kernel,
        out_shape=(
            jax.ShapeDtypeStruct((size, size), F32),
            jax.ShapeDtypeStruct((8, size), F32),
        ),
        in_specs=[smem, smem, vmem],
        out_specs=(vmem, vmem),
        compiler_params=pltpu.CompilerParams(vmem_limit_bytes=VMEM_BYTES),
        name="potential",
    )(shift, opened, basis)


def pieces(refs):
    element, quarter = lax.axis_index("elem"), quarter_index()
    for j in range(refs[0].shape[1]):
        yield element, j, refs[0].at[0, j]
        step = 1
        for ref in refs[1:]:
            for k in range(ref.shape[0]):
                yield element ^ (step + k), quarter ^ j, ref.at[k, j]
            step = step + ref.shape[0]


def factor_kernel(groups, scalar_ref, potential_ref, *rest):
    refs, rest = rest[:groups], rest[groups:]
    inverse_ref, link_ref, extra_ref, diag_scr, coupling_ref, pack_scr, *scratch = rest
    matrix_scr, inverse_scr = scratch
    count = extra_ref.shape[0]
    size = potential_ref.shape[0]
    part = size // refs[0].shape[1]
    half = part // 2
    middle = count // 2
    identity = eye_of(size)
    potential = potential_ref[...]
    for element, index, ref in pieces(refs):
        start = pl.multiple_of(index * half, 8)
        pack_scr[element, pl.ds(start, half), :] = ref[:half]
        start = pl.multiple_of(index * part, 8)
        coupling_ref[element, pl.ds(start, part), :] = ref[half : half + part]
        extra_ref[element] = ref[half + 2 * part :]
    for n in range(count):
        diag_scr[n] = (
            unpack_symmetric(pack_scr[n])
            + (extra_ref[n, 0:1] + scalar_ref[0:1]) * identity
            + extra_ref[n, 1:2, :1] * potential
        )

    def eliminate(invert):
        worst = jnp.zeros((1, 1), F32)
        forward = diag_scr[0]
        backward = diag_scr[count - 1]

        def finish(n, matrix, worst):
            inverse, residual = invert(matrix, identity, 2 if n == middle else 1)
            residual16 = None
            if residual is not None:
                worst = jnp.maximum(worst, row_norm(residual))
                residual16 = residual.astype(BF16)
            final = split(correct(inverse, residual16))
            inverse_ref[0, n] = final[0]
            inverse_ref[1, n] = final[1]
            return split(inverse), residual16, worst

        def connect(n, coupling, inverse, residual16):
            parts = split(correct(dot3(coupling, inverse), residual16))
            link_ref[0, n] = parts[0]
            link_ref[1, n] = parts[1]
            return parts

        meeting = diag_scr[middle]
        for step in range(max(middle, count - 1 - middle)):
            ahead, behind = step, count - 1 - step
            if ahead < middle:
                parts, residual16, worst = finish(ahead, forward, worst)
                coupling = split(-(identity + coupling_ref[ahead + 1]))
                link = connect(ahead + 1, coupling, parts, residual16)
                update = dot3(link, coupling, NT)
                if ahead + 1 < middle:
                    forward = diag_scr[ahead + 1] - update
                else:
                    meeting = meeting - update
            if behind > middle:
                parts, residual16, worst = finish(behind, backward, worst)
                raw = -(identity + coupling_ref[behind])
                link = connect(behind, split(raw.T), parts, residual16)
                update = dot3(link, split(raw))
                if behind - 1 > middle:
                    backward = diag_scr[behind - 1] - update
                else:
                    meeting = meeting - update
        _, _, worst = finish(middle, meeting, worst)
        return worst

    worst = jnp.max(eliminate(fast_inverse))

    @pl.when(jnp.logical_not(worst <= RESIDUAL_BOUND))
    def _():
        eliminate(
            functools.partial(slow_inverse, matrix_scr=matrix_scr, inverse_scr=inverse_scr)
        )


def factorize(scalars, potential, payloads):
    count, size = sum(value.shape[0] for value in payloads), potential.shape[0]
    vmem = pl.BlockSpec(memory_space=pltpu.VMEM)
    half = jax.ShapeDtypeStruct((2, count, size, size), BF16)
    return pl.pallas_call(
        functools.partial(factor_kernel, len(payloads)),
        out_shape=(half, half, jax.ShapeDtypeStruct((count, 8, size), F32)),
        in_specs=[vmem] * (2 + len(payloads)),
        out_specs=(vmem, vmem, vmem),
        scratch_shapes=[
            pltpu.VMEM((count, size, size), F32),
            pltpu.VMEM((count, size, size), F32),
            pltpu.VMEM((count, size // 2, size), F32),
            pltpu.VMEM((size, size), F32),
            pltpu.VMEM((size, size), F32),
        ],
        compiler_params=pltpu.CompilerParams(vmem_limit_bytes=VMEM_BYTES),
        name="factorize",
    )(scalars, potential, *payloads)


def load_factors(inverse_ref, link_ref):
    count = inverse_ref.shape[1]
    inverses = [(inverse_ref[0, n], inverse_ref[1, n]) for n in range(count)]
    links = [(link_ref[0, n], link_ref[1, n]) if n != 0 else None for n in range(count)]
    return inverses, links


def solve_blocks(blocks, inverses, links):
    count = len(blocks)
    middle = count // 2
    reduced = list(blocks)
    for n in range(1, middle + 1):
        reduced[n] = reduced[n] - dot3(split(reduced[n - 1]), links[n], NT)
    for n in range(count - 1, middle, -1):
        reduced[n - 1] = reduced[n - 1] - dot3(split(reduced[n]), links[n], NT)
    solved = [dot3(split(reduced[n]), inverses[n]) for n in range(count)]
    for n in range(middle, 0, -1):
        solved[n - 1] = solved[n - 1] - dot3(split(solved[n]), links[n])
    for n in range(middle + 1, count):
        solved[n] = solved[n] - dot3(split(solved[n - 1]), links[n])
    return solved


def solve_kernel(
    groups, scalar_ref, inverse_ref, link_ref, extra_ref, target_ref, *rest
):
    count = inverse_ref.shape[1]
    refs, rest = rest[:groups], rest[groups:]
    *source_refs, wave_ref, adjoint_ref, share_ref, gram_ref, own_scr, k_scr, projector_scr = rest
    channels, width = source_refs[0].shape[1:]
    me, column = lax.axis_index("elem"), lax.axis_index("rhs")
    part = channels // refs[0].shape[1]
    begin = part // 2 + part
    for element, index, ref in pieces(refs):
        start = pl.multiple_of(index * part, 8)
        projector_scr[element, pl.ds(start, part), :] = ref[begin : begin + part]
    order, distance = [0], count // 2
    while distance:
        order = order + [n ^ distance for n in order]
        distance = distance // 2
    for place, n in enumerate(order):
        half = source_refs[0].shape[0]
        own_scr[me ^ n] = source_refs[place // half][place % half]
    inverses, links = load_factors(inverse_ref, link_ref)
    projectors = [split(projector_scr[n]) for n in range(count)]
    wave = solve_blocks([own_scr[n].T for n in range(count)], inverses, links)
    k_total = dot3(split(wave[0]), projectors[0])
    for n in range(1, count):
        k_total = k_total + dot3(split(wave[n]), projectors[n])
    k_rows = lax.broadcasted_iota(jnp.int32, k_total.shape, 1)
    k_columns = lax.broadcasted_iota(jnp.int32, k_total.shape, 0) + column * width
    limit = scalar_ref[1:2, :1]
    opened = (k_rows.astype(F32) < limit) & (k_columns.astype(F32) < limit)
    residual = split(jnp.where(opened, k_total - target_ref[...].T, 0.0))
    drive = [PENALTY * wave[n] + dot3(residual, projectors[n], NT) for n in range(count)]
    adjoint = [value.T for value in solve_blocks(drive, inverses, links)]
    wave = [value.T for value in wave]

    share = share_ref.shape[0]
    k_scr[...] = k_total.T
    share_ref[...] = k_scr[pl.ds(pl.multiple_of(me * share, share), share), :]
    for n in range(count):
        own_scr[n] = wave[n]
    wave_ref[...] = own_scr[me]
    for n in range(count):
        own_scr[n] = adjoint[n]
    adjoint_ref[...] = own_scr[me]
    weighted = [extra_ref[n, 1:2, :1] * wave[n] for n in range(count)]
    weighted = split(jnp.concatenate(weighted, axis=1))
    gram = dot3(split(jnp.concatenate(adjoint, axis=1)), weighted, NT)
    gram = gram + gram.T
    half = channels // 2
    gram_ref[:half] = pack_symmetric(gram)
    gram_ref[half:] = jnp.broadcast_to(diagonal_of(gram), (8, channels))


def solve_all(scalars, inverses, links, extras, target, payloads, sources):
    count, channels, width = inverses.shape[1], *sources[0].shape[1:]
    rows = target.shape[0]
    vmem = pl.BlockSpec(memory_space=pltpu.VMEM)
    return pl.pallas_call(
        functools.partial(solve_kernel, len(payloads)),
        out_shape=(
            jax.ShapeDtypeStruct((channels, width), F32),
            jax.ShapeDtypeStruct((channels, width), F32),
            jax.ShapeDtypeStruct((rows // count, width), F32),
            jax.ShapeDtypeStruct((channels // 2 + 8, channels), F32),
        ),
        in_specs=[vmem] * (5 + len(payloads) + len(sources)),
        out_specs=(vmem,) * 4,
        scratch_shapes=[
            pltpu.VMEM((count, channels, width), F32),
            pltpu.VMEM((rows, width), F32),
            pltpu.VMEM((count, channels, channels), F32),
        ],
        compiler_params=pltpu.CompilerParams(vmem_limit_bytes=VMEM_BYTES),
        name="solve",
    )(scalars, inverses, links, extras, target, *payloads, *sources)


def gradient_kernel(scale, own_ref, other_ref, basis_ref, out_ref):
    size = basis_ref.shape[0]
    total = own_ref[...] + other_ref[...]
    gram = unpack_symmetric(total[: size // 2])
    gram = gram + total[size // 2 : size // 2 + 1] * eye_of(size)
    out_ref[...] = scale * dot3(split(gram), split(basis_ref[...]))


def gradient(scale, own, other, basis):
    vmem = pl.BlockSpec(memory_space=pltpu.VMEM)
    return pl.pallas_call(
        functools.partial(gradient_kernel, scale),
        out_shape=jax.ShapeDtypeStruct(basis.shape, F32),
        in_specs=[vmem, vmem, vmem],
        out_specs=vmem,
        compiler_params=pltpu.CompilerParams(vmem_limit_bytes=VMEM_BYTES),
        name="gradient",
    )(own, other, basis)


def swap(value, axis, step):
    count = lax.axis_size(axis)
    return lax.ppermute(value, axis, [(i, i ^ step) for i in range(count)])


def gradient_total(gram, scale, basis):
    steps = []
    for axis in ("rhs", "energy"):
        step = 1
        while step < lax.axis_size(axis):
            steps.append((axis, step))
            step = step * 2
    other = jnp.zeros_like(gram)
    for index, (axis, step) in enumerate(steps):
        if index:
            gram = gram + other
        other = swap(gram, axis, step)
    return gradient(scale, gram, other, basis)


def per_device(
    ham_noise,
    channel_levels,
    coupling_noise,
    corr_weight,
    corr_basis,
    projector,
    energy_shift,
    sources,
    target,
    open_channels,
):
    elements, energies, halves = (lax.axis_size(axis) for axis in ("elem", "energy", "rhs"))
    parts = energies * halves
    raw = (corr_weight, channel_levels, ham_noise, coupling_noise, projector)
    mine = pack_part(*raw, parts)
    whole = pack(*raw, parts)
    potential, scalars = potential_of(energy_shift, open_channels, corr_basis)

    def reach(found, step):
        low = step & -step
        return swap(found[step ^ low], "elem", low)

    def spread(payload, axis):
        distance = 1
        while distance < lax.axis_size(axis):
            payload = jnp.concatenate([payload, swap(payload, axis, distance)], axis=1)
            distance = distance * 2
        return payload

    steps = range(1, elements)
    far = elements // 2
    near = {0: mine}
    for step in steps:
        near[step] = reach(near, step)
        if step == far:
            near[far], near[1], whole, potential = lax.optimization_barrier(
                (near[far], near[1], whole, potential)
            )
    own, near[far] = lax.optimization_barrier((sources[:, 0], near[far]))
    late, near[elements - 1] = lax.optimization_barrier((own, near[elements - 1]))
    source_sets = {0: own, 1: swap(late, "elem", 1)}
    for step in steps[1:]:
        source_sets[step] = reach(source_sets, step)
    sets = [spread(near[step][None, None], "energy") for step in steps]
    sets[0], source_sets[1], source_sets[far] = lax.optimization_barrier(
        (sets[0], source_sets[1], source_sets[far])
    )
    groups = [sets[:-1], sets[-1:]] if len(sets) > 1 else [sets]
    payloads = [spread(jnp.concatenate(group, axis=0), "rhs") for group in groups]
    payloads = [whole[None], *payloads]
    order, distance = [0], far
    while distance:
        order = order + [n ^ distance for n in order]
        distance = distance // 2
    source_all = [source_sets[n] for n in order]
    inverses, links, extras = factorize(scalars, potential, payloads)
    wave, adjoint, share, gram = solve_all(
        scalars, inverses, links, extras, target[0], payloads, source_all
    )
    basis_grad = gradient_total(gram, -1.0 / (energies * elements), corr_basis)
    return wave[None, None], adjoint[None, None], share[None], basis_grad


def solution(mesh):
    return jax.shard_map(
        per_device,
        mesh=mesh,
        in_specs=(
            P(("groups", "elem"), None, None),
            P(("groups", "elem"), None),
            P(("groups", "elem"), None, None),
            P(("groups", "elem")),
            P("groups", None),
            P(("groups", "elem"), None, None),
            P(("groups", "energy")),
            P(("groups", "energy"), "elem", None, "rhs"),
            P(("groups", "energy"), None, "rhs"),
            P(("groups", "energy")),
        ),
        out_specs=(
            P(("groups", "energy"), "elem", None, "rhs"),
            P(("groups", "energy"), "elem", None, "rhs"),
            P(("groups", "energy"), "elem", "rhs"),
            P("groups", None),
        ),
        check_vma=False,
    )
```

```python
import functools

import jax
import jax.numpy as jnp
from jax import lax
from jax.experimental import pallas as pl
from jax.experimental.pallas import tpu as pltpu
from jax.sharding import PartitionSpec as P

PENALTY = 0.5
START_SCALE = 0.95
SLOW_SCALE = 1.75
RESIDUAL_BOUND = 0.01
F32 = jnp.float32
BF16 = jnp.bfloat16
NN = (((1,), (0,)), ((), ()))
NT = (((1,), (1,)), ((), ()))
VMEM_BYTES = 48 * 1024 * 1024
PACK_BYTES = 60 * 1024 * 1024


def split(value):
    high = value.astype(BF16)
    return high, (value - high.astype(F32)).astype(BF16)


def dot1(lhs, rhs, dims=NN):
    return lax.dot_general(lhs, rhs, dims, preferred_element_type=F32)


def dot3(lhs, rhs, dims=NN):
    return (
        dot1(lhs[0], rhs[0], dims) + dot1(lhs[0], rhs[1], dims) + dot1(lhs[1], rhs[0], dims)
    )


def eye_of(size):
    rows = lax.broadcasted_iota(jnp.int32, (size, size), 0)
    columns = lax.broadcasted_iota(jnp.int32, (size, size), 1)
    return (rows == columns).astype(F32)


def row_norm(matrix):
    return jnp.max(jnp.sum(jnp.abs(matrix), axis=1, keepdims=True), axis=0, keepdims=True)


def fast_inverse(matrix, identity, steps):
    diagonal = matrix * identity
    by_row = START_SCALE / jnp.sum(diagonal, axis=1, keepdims=True)
    by_column = START_SCALE / jnp.sum(diagonal, axis=0, keepdims=True)
    error = identity - by_row * matrix
    inverse = (identity + error) * by_column
    error16 = error.astype(BF16)
    for _ in range(steps):
        error16 = dot1(error16, error16).astype(BF16)
        inverse = inverse + dot1(error16, inverse.astype(BF16))
    return inverse, identity - dot3(split(matrix), split(inverse))


def exact_dot(lhs, rhs):
    return lax.dot_general(
        lhs, rhs, NN, precision=lax.Precision.HIGHEST, preferred_element_type=F32
    )


def slow_inverse(matrix, identity, steps, matrix_scr, inverse_scr):
    matrix_scr[...] = matrix
    inverse_scr[...] = identity * (SLOW_SCALE / row_norm(matrix))

    def going(state):
        count, size = state
        return (size > 1e-3) & (count < 100)

    def step(state):
        count, _ = state
        inverse = inverse_scr[...]
        residual = identity - exact_dot(matrix_scr[...], inverse)
        inverse_scr[...] = inverse + exact_dot(inverse, residual)
        return count + 1, jnp.max(row_norm(residual))

    lax.while_loop(going, step, (jnp.int32(0), jnp.float32(1e9)))
    return inverse_scr[...], None


def correct(product, residual16):
    if residual16 is None:
        return product
    return product + dot1(product.astype(BF16), residual16)


def pack_symmetric(matrix):
    half = matrix.shape[0] // 2
    rows = lax.broadcasted_iota(jnp.int32, (half, half), 0)
    columns = lax.broadcasted_iota(jnp.int32, (half, half), 1)
    first, second = matrix[:half, :half], matrix[half:, half:]
    mixed = jnp.where(rows > columns, first, jnp.where(rows < columns, second, 0.0))
    return jnp.concatenate([matrix[half:, :half], mixed], axis=1)


def unpack_symmetric(packed):
    half = packed.shape[0]
    rows = lax.broadcasted_iota(jnp.int32, (half, half), 0)
    columns = lax.broadcasted_iota(jnp.int32, (half, half), 1)
    corner, mixed = packed[:, :half], packed[:, half:]
    first = jnp.where(rows > columns, mixed, 0.0)
    second = jnp.where(rows < columns, mixed, 0.0)
    return jnp.concatenate(
        [
            jnp.concatenate([first + first.T, corner.T], axis=1),
            jnp.concatenate([corner, second + second.T], axis=1),
        ],
        axis=0,
    )


def diagonal_of(matrix):
    return jnp.sum(matrix * eye_of(matrix.shape[0]), axis=0, keepdims=True)


def extra_rows(ham, level, weight):
    row = lax.broadcasted_iota(jnp.int32, (8, ham.shape[1]), 0)
    return jnp.where(row == 0, diagonal_of(ham) + level + 2.0, weight)


def quarter_index():
    return lax.axis_index("rhs") * lax.axis_size("energy") + lax.axis_index("energy")


def pack_part_kernel(
    weight_ref, level_hbm, ham_hbm, coupling_hbm, projector_hbm, out_ref, ham_ref, pack_scr,
    level_ref, sems,
):
    part = (out_ref.shape[0] - 8) * 2 // 5
    half = part // 2
    index = quarter_index()
    rows = pl.ds(pl.multiple_of(index * part, 8), part)
    copies = [
        pltpu.make_async_copy(source, target, sems.at[number])
        for number, (source, target) in enumerate(
            (
                (ham_hbm.at[0], ham_ref),
                (level_hbm, level_ref),
                (coupling_hbm.at[0, rows], out_ref.at[half : half + part]),
                (projector_hbm.at[0, rows], out_ref.at[half + part : half + 2 * part]),
            )
        )
    ]
    for copy in copies:
        copy.start()
    copies[0].wait()
    copies[1].wait()
    ham = 0.5 * (ham_ref[...] + ham_ref[...].T)
    pack_scr[...] = pack_symmetric(ham)
    out_ref[:half] = pack_scr[pl.ds(pl.multiple_of(index * half, 8), half), :]
    out_ref[half + 2 * part :] = extra_rows(ham, level_ref[...], weight_ref[0])
    copies[2].wait()
    copies[3].wait()


def pack_part(weight, level, ham, coupling, projector, parts):
    size = ham.shape[1]
    part = size // parts
    smem = pl.BlockSpec(memory_space=pltpu.SMEM)
    vmem = pl.BlockSpec(memory_space=pltpu.VMEM)
    anywhere = pl.BlockSpec(memory_space=pl.ANY)
    height = part // 2 + 2 * part + 8
    return pl.pallas_call(
        pack_part_kernel,
        out_shape=jax.ShapeDtypeStruct((height, size), F32),
        in_specs=[smem] + [anywhere] * 4,
        out_specs=vmem,
        scratch_shapes=[
            pltpu.VMEM((size, size), F32),
            pltpu.VMEM((size // 2, size), F32),
            pltpu.VMEM((1, size), F32),
            pltpu.SemaphoreType.DMA((4,)),
        ],
        compiler_params=pltpu.CompilerParams(vmem_limit_bytes=PACK_BYTES),
        name="pack_part",
    )(weight, level, ham, coupling, projector)


def pack_kernel(weight_ref, level_ref, ham_ref, coupling_ref, projector_ref, whole_ref):
    parts = whole_ref.shape[0]
    size = ham_ref.shape[1]
    part = size // parts
    half = part // 2
    ham = 0.5 * (ham_ref[0] + ham_ref[0].T)
    packed = pack_symmetric(ham)
    extra = extra_rows(ham, level_ref[...], weight_ref[0])
    for n in range(parts):
        rows = slice(n * part, (n + 1) * part)
        whole_ref[n, :half] = packed[n * half : (n + 1) * half]
        whole_ref[n, half : half + part] = coupling_ref[0, rows]
        whole_ref[n, half + part : half + 2 * part] = projector_ref[0, rows]
        whole_ref[n, half + 2 * part :] = extra


def pack(weight, level, ham, coupling, projector, parts):
    size = ham.shape[1]
    part = size // parts
    smem = pl.BlockSpec(memory_space=pltpu.SMEM)
    vmem = pl.BlockSpec(memory_space=pltpu.VMEM)
    return pl.pallas_call(
        pack_kernel,
        out_shape=jax.ShapeDtypeStruct((parts, part // 2 + 2 * part + 8, size), F32),
        in_specs=[smem] + [vmem] * 4,
        out_specs=vmem,
        compiler_params=pltpu.CompilerParams(vmem_limit_bytes=VMEM_BYTES),
        name="pack",
    )(weight, level, ham, coupling, projector)


def potential_kernel(shift_ref, open_ref, basis_ref, out_ref, scalar_ref):
    basis = split(basis_ref[...])
    out_ref[...] = dot3(basis, basis, NT)
    row = lax.broadcasted_iota(jnp.int32, scalar_ref.shape, 0)
    scalar_ref[...] = jnp.where(row == 0, shift_ref[0], open_ref[0].astype(F32))


def potential_of(shift, opened, basis):
    smem = pl.BlockSpec(memory_space=pltpu.SMEM)
    vmem = pl.BlockSpec(memory_space=pltpu.VMEM)
    size = basis.shape[0]
    return pl.pallas_call(
        potential_kernel,
        out_shape=(
            jax.ShapeDtypeStruct((size, size), F32),
            jax.ShapeDtypeStruct((8, size), F32),
        ),
        in_specs=[smem, smem, vmem],
        out_specs=(vmem, vmem),
        compiler_params=pltpu.CompilerParams(vmem_limit_bytes=VMEM_BYTES),
        name="potential",
    )(shift, opened, basis)


def pieces(refs):
    element, quarter = lax.axis_index("elem"), quarter_index()
    for j in range(refs[0].shape[1]):
        yield element, j, refs[0].at[0, j]
        step = 1
        for ref in refs[1:]:
            for k in range(ref.shape[0]):
                yield element ^ (step + k), quarter ^ j, ref.at[k, j]
            step = step + ref.shape[0]


def factor_kernel(groups, scalar_ref, potential_ref, *rest):
    refs, rest = rest[:groups], rest[groups:]
    inverse_ref, link_ref, extra_ref, diag_scr, coupling_ref, pack_scr, *scratch = rest
    matrix_scr, inverse_scr = scratch
    count = extra_ref.shape[0]
    size = potential_ref.shape[0]
    part = size // refs[0].shape[1]
    half = part // 2
    middle = count // 2
    identity = eye_of(size)
    potential = potential_ref[...]
    for element, index, ref in pieces(refs):
        start = pl.multiple_of(index * half, 8)
        pack_scr[element, pl.ds(start, half), :] = ref[:half]
        start = pl.multiple_of(index * part, 8)
        coupling_ref[element, pl.ds(start, part), :] = ref[half : half + part]
        extra_ref[element] = ref[half + 2 * part :]
    for n in range(count):
        diag_scr[n] = (
            unpack_symmetric(pack_scr[n])
            + (extra_ref[n, 0:1] + scalar_ref[0:1]) * identity
            + extra_ref[n, 1:2, :1] * potential
        )

    def eliminate(invert):
        worst = jnp.zeros((1, 1), F32)
        forward = diag_scr[0]
        backward = diag_scr[count - 1]

        def finish(n, matrix, worst):
            inverse, residual = invert(matrix, identity, 2 if n == middle else 1)
            residual16 = None
            if residual is not None:
                worst = jnp.maximum(worst, row_norm(residual))
                residual16 = residual.astype(BF16)
            final = split(correct(inverse, residual16))
            inverse_ref[0, n] = final[0]
            inverse_ref[1, n] = final[1]
            return split(inverse), residual16, worst

        def connect(n, coupling, inverse, residual16):
            parts = split(correct(dot3(coupling, inverse), residual16))
            link_ref[0, n] = parts[0]
            link_ref[1, n] = parts[1]
            return parts

        meeting = diag_scr[middle]
        for step in range(max(middle, count - 1 - middle)):
            ahead, behind = step, count - 1 - step
            if ahead < middle:
                parts, residual16, worst = finish(ahead, forward, worst)
                coupling = split(-(identity + coupling_ref[ahead + 1]))
                link = connect(ahead + 1, coupling, parts, residual16)
                update = dot3(link, coupling, NT)
                if ahead + 1 < middle:
                    forward = diag_scr[ahead + 1] - update
                else:
                    meeting = meeting - update
            if behind > middle:
                parts, residual16, worst = finish(behind, backward, worst)
                raw = -(identity + coupling_ref[behind])
                link = connect(behind, split(raw.T), parts, residual16)
                update = dot3(link, split(raw))
                if behind - 1 > middle:
                    backward = diag_scr[behind - 1] - update
                else:
                    meeting = meeting - update
        _, _, worst = finish(middle, meeting, worst)
        return worst

    worst = jnp.max(eliminate(fast_inverse))

    @pl.when(jnp.logical_not(worst <= RESIDUAL_BOUND))
    def _():
        eliminate(
            functools.partial(slow_inverse, matrix_scr=matrix_scr, inverse_scr=inverse_scr)
        )


def factorize(scalars, potential, payloads):
    count, size = sum(value.shape[0] for value in payloads), potential.shape[0]
    vmem = pl.BlockSpec(memory_space=pltpu.VMEM)
    half = jax.ShapeDtypeStruct((2, count, size, size), BF16)
    return pl.pallas_call(
        functools.partial(factor_kernel, len(payloads)),
        out_shape=(half, half, jax.ShapeDtypeStruct((count, 8, size), F32)),
        in_specs=[vmem] * (2 + len(payloads)),
        out_specs=(vmem, vmem, vmem),
        scratch_shapes=[
            pltpu.VMEM((count, size, size), F32),
            pltpu.VMEM((count, size, size), F32),
            pltpu.VMEM((count, size // 2, size), F32),
            pltpu.VMEM((size, size), F32),
            pltpu.VMEM((size, size), F32),
        ],
        compiler_params=pltpu.CompilerParams(vmem_limit_bytes=VMEM_BYTES),
        name="factorize",
    )(scalars, potential, *payloads)


def load_factors(inverse_ref, link_ref):
    count = inverse_ref.shape[1]
    inverses = [(inverse_ref[0, n], inverse_ref[1, n]) for n in range(count)]
    links = [(link_ref[0, n], link_ref[1, n]) if n != 0 else None for n in range(count)]
    return inverses, links


def solve_blocks(blocks, inverses, links):
    count = len(blocks)
    middle = count // 2
    reduced = list(blocks)
    for n in range(1, middle + 1):
        reduced[n] = reduced[n] - dot3(split(reduced[n - 1]), links[n], NT)
    for n in range(count - 1, middle, -1):
        reduced[n - 1] = reduced[n - 1] - dot3(split(reduced[n]), links[n], NT)
    solved = [dot3(split(reduced[n]), inverses[n]) for n in range(count)]
    for n in range(middle, 0, -1):
        solved[n - 1] = solved[n - 1] - dot3(split(solved[n]), links[n])
    for n in range(middle + 1, count):
        solved[n] = solved[n] - dot3(split(solved[n - 1]), links[n])
    return solved


def solve_kernel(
    groups, scalar_ref, inverse_ref, link_ref, extra_ref, target_ref, *rest
):
    count = inverse_ref.shape[1]
    refs, rest = rest[:groups], rest[groups:]
    *source_refs, wave_ref, adjoint_ref, share_ref, gram_ref, own_scr, k_scr, projector_scr = rest
    channels, width = source_refs[0].shape[1:]
    me, column = lax.axis_index("elem"), lax.axis_index("rhs")
    part = channels // refs[0].shape[1]
    begin = part // 2 + part
    for element, index, ref in pieces(refs):
        start = pl.multiple_of(index * part, 8)
        projector_scr[element, pl.ds(start, part), :] = ref[begin : begin + part]
    order, distance = [0], count // 2
    while distance:
        order = order + [n ^ distance for n in order]
        distance = distance // 2
    for place, n in enumerate(order):
        half = source_refs[0].shape[0]
        own_scr[me ^ n] = source_refs[place // half][place % half]
    inverses, links = load_factors(inverse_ref, link_ref)
    projectors = [split(projector_scr[n]) for n in range(count)]
    wave = solve_blocks([own_scr[n].T for n in range(count)], inverses, links)
    k_total = dot3(split(wave[0]), projectors[0])
    for n in range(1, count):
        k_total = k_total + dot3(split(wave[n]), projectors[n])
    k_rows = lax.broadcasted_iota(jnp.int32, k_total.shape, 1)
    k_columns = lax.broadcasted_iota(jnp.int32, k_total.shape, 0) + column * width
    limit = scalar_ref[1:2, :1]
    opened = (k_rows.astype(F32) < limit) & (k_columns.astype(F32) < limit)
    residual = split(jnp.where(opened, k_total - target_ref[...].T, 0.0))
    drive = [PENALTY * wave[n] + dot3(residual, projectors[n], NT) for n in range(count)]
    adjoint = [value.T for value in solve_blocks(drive, inverses, links)]
    wave = [value.T for value in wave]

    share = share_ref.shape[0]
    k_scr[...] = k_total.T
    share_ref[...] = k_scr[pl.ds(pl.multiple_of(me * share, share), share), :]
    for n in range(count):
        own_scr[n] = wave[n]
    wave_ref[...] = own_scr[me]
    for n in range(count):
        own_scr[n] = adjoint[n]
    adjoint_ref[...] = own_scr[me]
    weighted = [extra_ref[n, 1:2, :1] * wave[n] for n in range(count)]
    weighted = split(jnp.concatenate(weighted, axis=1))
    gram = dot3(split(jnp.concatenate(adjoint, axis=1)), weighted, NT)
    gram = gram + gram.T
    half = channels // 2
    gram_ref[:half] = pack_symmetric(gram)
    gram_ref[half:] = jnp.broadcast_to(diagonal_of(gram), (8, channels))


def solve_all(scalars, inverses, links, extras, target, payloads, sources):
    count, channels, width = inverses.shape[1], *sources[0].shape[1:]
    rows = target.shape[0]
    vmem = pl.BlockSpec(memory_space=pltpu.VMEM)
    return pl.pallas_call(
        functools.partial(solve_kernel, len(payloads)),
        out_shape=(
            jax.ShapeDtypeStruct((channels, width), F32),
            jax.ShapeDtypeStruct((channels, width), F32),
            jax.ShapeDtypeStruct((rows // count, width), F32),
            jax.ShapeDtypeStruct((channels // 2 + 8, channels), F32),
        ),
        in_specs=[vmem] * (5 + len(payloads) + len(sources)),
        out_specs=(vmem,) * 4,
        scratch_shapes=[
            pltpu.VMEM((count, channels, width), F32),
            pltpu.VMEM((rows, width), F32),
            pltpu.VMEM((count, channels, channels), F32),
        ],
        compiler_params=pltpu.CompilerParams(vmem_limit_bytes=VMEM_BYTES),
        name="solve",
    )(scalars, inverses, links, extras, target, *payloads, *sources)


def gradient_kernel(scale, own_ref, other_ref, basis_ref, out_ref):
    size = basis_ref.shape[0]
    total = own_ref[...] + other_ref[...]
    gram = unpack_symmetric(total[: size // 2])
    gram = gram + total[size // 2 : size // 2 + 1] * eye_of(size)
    out_ref[...] = scale * dot3(split(gram), split(basis_ref[...]))


def gradient(scale, own, other, basis):
    vmem = pl.BlockSpec(memory_space=pltpu.VMEM)
    return pl.pallas_call(
        functools.partial(gradient_kernel, scale),
        out_shape=jax.ShapeDtypeStruct(basis.shape, F32),
        in_specs=[vmem, vmem, vmem],
        out_specs=vmem,
        compiler_params=pltpu.CompilerParams(vmem_limit_bytes=VMEM_BYTES),
        name="gradient",
    )(own, other, basis)


def swap(value, axis, step):
    count = lax.axis_size(axis)
    return lax.ppermute(value, axis, [(i, i ^ step) for i in range(count)])


def gradient_total(gram, scale, basis):
    steps = []
    for axis in ("rhs", "energy"):
        step = 1
        while step < lax.axis_size(axis):
            steps.append((axis, step))
            step = step * 2
    other = jnp.zeros_like(gram)
    for index, (axis, step) in enumerate(steps):
        if index:
            gram = gram + other
        other = swap(gram, axis, step)
    return gradient(scale, gram, other, basis)


def per_device(
    ham_noise,
    channel_levels,
    coupling_noise,
    corr_weight,
    corr_basis,
    projector,
    energy_shift,
    sources,
    target,
    open_channels,
):
    elements, energies, halves = (lax.axis_size(axis) for axis in ("elem", "energy", "rhs"))
    parts = energies * halves
    raw = (corr_weight, channel_levels, ham_noise, coupling_noise, projector)
    mine = pack_part(*raw, parts)
    whole = pack(*raw, parts)
    potential, scalars = potential_of(energy_shift, open_channels, corr_basis)

    def reach(found, step):
        low = step & -step
        return swap(found[step ^ low], "elem", low)

    def spread(payload, axis):
        distance = 1
        while distance < lax.axis_size(axis):
            payload = jnp.concatenate([payload, swap(payload, axis, distance)], axis=1)
            distance = distance * 2
        return payload

    steps = range(1, elements)
    far = elements // 2
    near = {0: mine}
    for step in steps:
        near[step] = reach(near, step)
        if step == 1:
            near[1], whole, potential = lax.optimization_barrier((near[1], whole, potential))
    own, near[far] = lax.optimization_barrier((sources[:, 0], near[far]))
    source_sets = {0: own}
    for step in steps:
        source_sets[step] = reach(source_sets, step)
    sets = [spread(near[step][None, None], "energy") for step in steps]
    sets[0], source_sets[far] = lax.optimization_barrier((sets[0], source_sets[far]))
    groups = [sets[:-1], sets[-1:]] if len(sets) > 1 else [sets]
    payloads = [spread(jnp.concatenate(group, axis=0), "rhs") for group in groups]
    payloads = [whole[None], *payloads]
    order, distance = [0], far
    while distance:
        order = order + [n ^ distance for n in order]
        distance = distance // 2
    source_all = [source_sets[n] for n in order]
    inverses, links, extras = factorize(scalars, potential, payloads)
    wave, adjoint, share, gram = solve_all(
        scalars, inverses, links, extras, target[0], payloads, source_all
    )
    basis_grad = gradient_total(gram, -1.0 / (energies * elements), corr_basis)
    return wave[None, None], adjoint[None, None], share[None], basis_grad


def solution(mesh):
    return jax.shard_map(
        per_device,
        mesh=mesh,
        in_specs=(
            P(("groups", "elem"), None, None),
            P(("groups", "elem"), None),
            P(("groups", "elem"), None, None),
            P(("groups", "elem")),
            P("groups", None),
            P(("groups", "elem"), None, None),
            P(("groups", "energy")),
            P(("groups", "energy"), "elem", None, "rhs"),
            P(("groups", "energy"), None, "rhs"),
            P(("groups", "energy")),
        ),
        out_specs=(
            P(("groups", "energy"), "elem", None, "rhs"),
            P(("groups", "energy"), "elem", None, "rhs"),
            P(("groups", "energy"), "elem", "rhs"),
            P("groups", None),
        ),
        check_vma=False,
    )
```
